128 devices in a mesh: seq: 16 (over x_hi, y, core), tp: 8 (over z, x_lo).
Axes of the slice: x: 4 (x_hi: 2, x_lo: 2; x = x_hi * 2 + x_lo), y: 4, z: 4, core: 2. Of those that a mesh axis runs over, the one named last changes fastest.
Arguments:
- tokens: bfloat16 [4096, 2048], P('seq'), may hold values from -6 to 6
- gain_attn: float32 [2048], replicated, may hold values from 0.5 to 1.5
- w_query: bfloat16 [2048, 2048], P(None, 'tp'), may hold values from -0.125 to 0.125
- w_key: bfloat16 [2048, 2048], P(None, 'tp'), may hold values from -0.125 to 0.125
- w_value: bfloat16 [2048, 2048], P(None, 'tp'), may hold values from -0.125 to 0.125
- w_out: bfloat16 [2048, 2048], P('tp'), may hold values from -1.5 to 1.5
- gain_ffn: float32 [2048], replicated, may hold values from 0.5 to 1.5
- w_gate: bfloat16 [2048, 5504], P(None, 'tp'), may hold values from -0.125 to 0.125
- w_up: bfloat16 [2048, 5504], P(None, 'tp'), may hold values from -0.125 to 0.125
- w_down: bfloat16 [5504, 2048], P('tp'), may hold values from -0.078125 to 0.078125
- cotangent: bfloat16 [4096, 2048], P('seq'), may hold values from -6 to 6
Outputs:
- block_out: bfloat16 [4096, 2048], P('seq')
- grad_tokens: float32 [4096, 2048], P('seq')
- grad_gain_attn: float32 [2048], P('tp')
- grad_w_query: float32 [2048, 2048], P(None, 'tp')
- grad_w_key: float32 [2048, 2048], P(None, 'tp')
- grad_w_value: float32 [2048, 2048], P(None, 'tp')
- grad_w_out: float32 [2048, 2048], P('tp')
- grad_gain_ffn: float32 [2048], P('tp')
- grad_w_gate: float32 [2048, 5504], P(None, 'tp')
- grad_w_up: float32 [2048, 5504], P(None, 'tp')
- grad_w_down: float32 [5504, 2048], P('tp')
The draws below stay inside these ranges and needn't reach their ends.
All inputs are finite; a program needn't handle non-finite values.
Results may differ from the reference program's by a relative error of at most 0.023.
Values may be sent and summed in bfloat16 or wider, within the bound.
No kernel may reach another device: no remote copies, remote signals or barrier semaphores. Data moves between devices by JAX's collectives and lax.ppermute only.
A program may use at most 192 MiB of HBM per device.

```python
import math
import jax
import jax.numpy as jnp
from jax import lax

D = 2048
H = 16
HD = 128
FF = 5504
W = 1024
TOKENS = 4096


def level_of(own_key, dims, shards, least, top_value):
    gain = 1.0
    for position, blocks in shards:
        steps = jax.random.uniform(jax.random.fold_in(jax.random.fold_in(own_key, 6), position), (blocks,), jnp.float32, least / len(shards), top_value / len(shards))
        gain = gain * jnp.repeat(jnp.exp(steps), dims[position] // blocks).reshape((-1,) + (1,) * (len(dims) - 1 - position))
    return gain


def gaussian(key, dims, width, limit, pieces=(), kind=jnp.bfloat16):
    drawn = jax.random.normal(key, dims, jnp.float32) * width
    if len(pieces) > 0:
        drawn = level_of(key, dims, pieces, -0.22, 0.18) * drawn
    return jnp.clip(drawn, min=-limit, max=limit).astype(kind)


def setup_inputs(seed: int = 0) -> dict:
    arg_keys = jax.random.split(jax.random.key(seed), 12)
    return {
        "tokens": gaussian(arg_keys[0], (TOKENS, D), 1.0, 6.0, ((0, 16),)),
        "gain_attn": jnp.clip(1.0 + 0.1 * jax.random.normal(arg_keys[1], (D,), jnp.float32), 0.5, 1.5),
        "w_query": gaussian(arg_keys[2], (D, D), D ** -0.5, 0.125, ((1, 8),)),
        "w_key": gaussian(arg_keys[3], (D, D), D ** -0.5, 0.125, ((1, 8),)),
        "w_value": gaussian(arg_keys[4], (D, D), D ** -0.5, 0.125, ((1, 8),)),
        "w_out": gaussian(arg_keys[5], (D, D), (max(D // 128, 2)) ** -0.5, 1.5, ((0, 8),)),
        "gain_ffn": jnp.clip(1.0 + 0.1 * jax.random.normal(arg_keys[6], (D,), jnp.float32), 0.5, 1.5),
        "w_gate": gaussian(arg_keys[7], (D, FF), D ** -0.5, 0.125, ((1, 8),)),
        "w_up": gaussian(arg_keys[8], (D, FF), D ** -0.5, 0.125, ((1, 8),)),
        "w_down": gaussian(arg_keys[9], (FF, D), FF ** -0.5, 0.078125, ((0, 8),)),
        "cotangent": gaussian(arg_keys[10], (TOKENS, D), 1.0, 6.0, ((0, 16),)),
    }


@jax.custom_vjp
def low(v):
    return lax.optimization_barrier(v.astype(jnp.bfloat16)).astype(jnp.float32)

@jax.custom_vjp
def low_back(v):
    return v

def low_keep(v):
    return (low(v), None)

def low_pass(kept, grad):
    return (grad,)

def back_keep(v):
    return (v, None)

def back_low(kept, grad):
    return (low(grad),)
low.defvjp(low_keep, low_pass)
low_back.defvjp(back_keep, back_low)
epsilon = 1e-06

def product(left_matrix, right_matrix):
    return jnp.dot(left_matrix, right_matrix, preferred_element_type=jnp.float32, precision=lax.Precision.HIGHEST)

def rms_scale(field_rows, gain_vec):
    return field_rows * lax.rsqrt(lax.optimization_barrier(jnp.mean(field_rows * field_rows, axis=-1, keepdims=True)) + epsilon) * gain_vec

def attend_block(queries, key_rows, value_rows, offset):
    scores = jnp.einsum('ihd,chd->hic', queries, key_rows, precision=lax.Precision.HIGHEST) * HD ** (-0.5)
    scores = low_back(scores)
    query_pos = offset + jnp.arange(queries.shape[0], dtype=jnp.int32)
    key_pos = offset - W + jnp.arange(key_rows.shape[0], dtype=jnp.int32)
    allowed = (key_pos[None, :] >= 0) & (key_pos[None, :] <= query_pos[:, None]) & (key_pos[None, :] > query_pos[:, None] - W)
    masked = jnp.where(allowed[None], scores, -1e+30)
    weights_low = low(jax.nn.softmax(masked, axis=-1))
    return jnp.einsum('hic,chd->ihd', weights_low, value_rows, precision=lax.Precision.HIGHEST)

def forward(tokens, gain_attn, w_query, w_key, w_value, w_out, gain_ffn, w_gate, w_up, w_down):
    seq_len = tokens.shape[0]
    normed_attn = low(rms_scale(tokens, gain_attn))
    queries = low_back(low(product(normed_attn, w_query))).reshape(seq_len, H, HD)
    key_rows = low_back(low(product(normed_attn, w_key))).reshape(seq_len, H, HD)
    value_rows = low_back(low(product(normed_attn, w_value))).reshape(seq_len, H, HD)
    padding = jnp.zeros((W, H, HD), jnp.float32)
    keys_padded = jnp.concatenate([padding, key_rows], axis=0)
    values_padded = jnp.concatenate([padding, value_rows], axis=0)
    block_rows = math.gcd(seq_len, 512)
    starts = jnp.arange(seq_len // block_rows, dtype=jnp.int32) * block_rows
    checked = jax.checkpoint(attend_block)

    def attend_one(offset):
        query_block = lax.dynamic_slice_in_dim(queries, offset, block_rows, 0)
        key_block = lax.dynamic_slice_in_dim(keys_padded, offset, W + block_rows, 0)
        value_block = lax.dynamic_slice_in_dim(values_padded, offset, W + block_rows, 0)
        return checked(query_block, key_block, value_block, offset)
    mixed_heads = lax.map(attend_one, starts).reshape(seq_len, H * HD)
    heads_out = low_back(low(mixed_heads))
    attn_branch = low_back(product(heads_out, w_out))
    hidden = tokens + attn_branch
    normed_ffn = low(rms_scale(hidden, gain_ffn))
    gate_pre = low_back(product(normed_ffn, w_gate))
    up_pre = low_back(product(normed_ffn, w_up))
    activated = low(jax.nn.silu(gate_pre) * up_pre)
    ffn_branch = low_back(product(activated, w_down))
    return hidden + ffn_branch

def reference(tokens, gain_attn, w_query, w_key, w_value, w_out, gain_ffn, w_gate, w_up, w_down, cotangent):
    floats = [argument.astype(jnp.float32) for argument in (tokens, gain_attn, w_query, w_key, w_value, w_out, gain_ffn, w_gate, w_up, w_down)]
    result, pullback = jax.vjp(forward, *floats)
    gradients = pullback(cotangent.astype(jnp.float32))
    return (result.astype(jnp.bfloat16), gradients[0], gradients[1], gradients[2], gradients[3], gradients[4], gradients[5], gradients[6], gradients[7], gradients[8], gradients[9])
```

```python
import jax
import jax.numpy as jnp
from jax import lax
from jax.sharding import PartitionSpec as P

HD = 128
W = 1024
SEQ = 16
TP = 8

epsilon = 1e-06
masked_value = -1e30
low = jnp.bfloat16
wide = jnp.float32


def seq_pairs(step):
    pairs = []
    for x_hi in range(2):
        for y in range(4):
            for core in range(2):
                to_x, to_y, to_core = step(x_hi, y, core)
                pairs.append((x_hi * 8 + y * 2 + core, to_x * 8 + to_y * 2 + to_core))
    return pairs


CORE = seq_pairs(lambda x, y, c: (x, y, 1 - c))
Y_ONE = seq_pairs(lambda x, y, c: (x, y ^ 1, c))
Y_THREE = seq_pairs(lambda x, y, c: (x, y ^ 3, c))
X_HI = seq_pairs(lambda x, y, c: (1 - x, y, c))


def tp_pairs(flip):
    return [(k, k ^ flip) for k in range(TP)]


def shift_pairs(steps):
    return [(k, k + steps) for k in range(SEQ) if 0 <= k + steps < SEQ]


def by_seq(value, pairs):
    return lax.ppermute(value, "seq", pairs)


def by_tp(value, flip):
    return lax.ppermute(value, "tp", tp_pairs(flip))


FLIPS = (5, 7, 3, 4, 6, 2, 1)


def tp_reduce_scatter(partial, tp_index):
    blocks = partial.reshape(TP, partial.shape[0] // TP, partial.shape[1])
    arrived = [
        by_tp(lax.dynamic_index_in_dim(blocks, tp_index ^ flip, 0, False), flip) for flip in FLIPS
    ]
    total = lax.dynamic_index_in_dim(blocks, tp_index, 0, False).astype(wide)
    for piece in arrived:
        total = total + piece.astype(wide)
    return total


def tp_all_gather(rows, tp_index):
    out = jnp.zeros((TP,) + rows.shape, rows.dtype)
    out = lax.dynamic_update_index_in_dim(out, rows, tp_index, 0)
    for flip in FLIPS:
        out = lax.dynamic_update_index_in_dim(out, by_tp(rows, flip), tp_index ^ flip, 0)
    return out.reshape(TP * rows.shape[0], rows.shape[1])


def cut(value, axis, bit):
    size = value.shape[axis] // 2
    first = lax.slice_in_dim(value, 0, size, axis=axis)
    second = lax.slice_in_dim(value, size, 2 * size, axis=axis)
    return jnp.where(bit == 0, first, second)


def join(own, other, axis, bit):
    first = jnp.where(bit == 0, own, other)
    second = jnp.where(bit == 0, other, own)
    return jnp.concatenate([first, second], axis=axis)


def seq_all_reduce(part, axis, bits):
    core, y_gray, y_high, x_hi = bits
    arrived = by_seq(part(1 - core).astype(low), CORE)
    half = part(core) + arrived.astype(wide)
    size = half.shape[axis] // 2
    one = lax.slice_in_dim(half, 0, size, axis=axis)
    two = lax.slice_in_dim(half, size, 2 * size, axis=axis)
    arrived = (
        by_seq(cut(one, axis, 1 - y_gray).astype(low), Y_ONE),
        by_seq(cut(two, axis, 1 - y_high).astype(low), Y_THREE),
    )
    one = cut(one, axis, y_gray) + arrived[0].astype(wide)
    two = cut(two, axis, y_high) + arrived[1].astype(wide)
    arrived = (
        by_seq(cut(one, axis, 1 - y_high).astype(low), Y_THREE),
        by_seq(cut(two, axis, 1 - y_gray).astype(low), Y_ONE),
    )
    one = cut(one, axis, y_high) + arrived[0].astype(wide)
    two = cut(two, axis, y_gray) + arrived[1].astype(wide)
    arrived = by_seq(jnp.where(x_hi == 0, two, one).astype(low), X_HI)
    own = (jnp.where(x_hi == 0, one, two) + arrived.astype(wide)).astype(low)
    arrived = by_seq(own, X_HI)
    one = jnp.where(x_hi == 0, own, arrived)
    two = jnp.where(x_hi == 0, arrived, own)
    arrived = (by_seq(one, Y_THREE), by_seq(two, Y_ONE))
    one = join(one, arrived[0], axis, y_high)
    two = join(two, arrived[1], axis, y_gray)
    arrived = (by_seq(one, Y_ONE), by_seq(two, Y_THREE))
    one = join(one, arrived[0], axis, y_gray)
    two = join(two, arrived[1], axis, y_high)
    half = jnp.concatenate([one, two], axis=axis)
    return join(half, by_seq(half, CORE), axis, core).astype(wide)


def sum_everywhere(value):
    for pairs in (CORE, Y_ONE, Y_THREE, X_HI):
        value = value + by_seq(value, pairs)
    for flip in (2, 6, 1):
        value = value + by_tp(value, flip)
    return value


def rms_factor(field_rows):
    return lax.rsqrt(jnp.mean(field_rows * field_rows, axis=-1, keepdims=True) + epsilon)


def norm_back(grad_normed, unit_rows, factor, gain_vec):
    scaled = grad_normed * gain_vec
    return factor * (scaled - unit_rows * jnp.mean(scaled * unit_rows, axis=-1, keepdims=True))


def matmul(left_matrix, right_matrix):
    return jnp.dot(left_matrix, right_matrix, preferred_element_type=wide)


def outer_sum(left_matrix, right_matrix):
    return lax.dot_general(
        left_matrix, right_matrix, (((0,), (0,)), ((), ())), preferred_element_type=wide
    )


def times_trans(left_matrix, right_matrix):
    return lax.dot_general(
        left_matrix, right_matrix, (((1,), (1,)), ((), ())), preferred_element_type=wide
    )


def neighbours(own, core, way):
    two = by_seq(own, shift_pairs(2 * way))
    four = by_seq(own, shift_pairs(4 * way))
    sends_own = core == (0 if way == 1 else 1)
    across = by_seq(jnp.concatenate([two, jnp.where(sends_own, own, four)], axis=0), CORE)
    return jnp.concatenate([own, two, across[: own.shape[0]], four, across[own.shape[0] :]], axis=0)


def distances(core, way):
    near_first = core == (0 if way == 1 else 1)
    return jnp.stack(
        [
            jnp.int32(0),
            jnp.int32(2),
            jnp.where(near_first, 1, 3).astype(jnp.int32),
            jnp.int32(4),
            jnp.where(near_first, 3, 1).astype(jnp.int32),
        ]
    )


def seen(query_pos, key_pos):
    return (
        (key_pos[None, :] >= 0)
        & (query_pos[:, None] < SEQ * 256)
        & (key_pos[None, :] <= query_pos[:, None])
        & (key_pos[None, :] > query_pos[:, None] - W)
    )


def split_three(value):
    first = value.astype(low)
    rest = value - first.astype(wide)
    second = rest.astype(low)
    third = (rest - second.astype(wide)).astype(low)
    return first, second, third


def on_device(
    tokens, gain_attn, w_query, w_key, w_value, w_out, gain_ffn, w_gate, w_up, w_down, cotangent
):
    rows = tokens.shape[0]
    width = tokens.shape[1]
    heads = w_query.shape[1] // HD
    features = heads * HD
    score_scale = HD ** (-0.5)
    seq_index = lax.axis_index("seq")
    tp_index = lax.axis_index("tp")
    core = seq_index & 1
    y_low = (seq_index >> 1) & 1
    y_high = (seq_index >> 2) & 1
    x_hi = seq_index >> 3
    bits = (core, y_low ^ y_high, y_high, x_hi)
    share = rows // TP

    def own_share(value):
        return lax.dynamic_slice_in_dim(value, tp_index * share, share, 0)

    inputs = tokens.astype(wide)
    factor_attn = rms_factor(inputs)
    unit_attn = inputs * factor_attn
    normed_attn = (unit_attn * gain_attn).astype(low)
    key_rows = matmul(normed_attn, w_key).astype(low)
    value_rows = matmul(normed_attn, w_value).astype(low)
    key_value = neighbours(jnp.concatenate([key_rows, value_rows], axis=1), core, 1)
    query_rows = matmul(normed_attn, w_query).astype(low)

    own_pos = seq_index * rows + jnp.arange(rows, dtype=jnp.int32)
    key_pos = (
        (seq_index - distances(core, 1))[:, None] * rows + jnp.arange(rows, dtype=jnp.int32)[None]
    ).reshape(-1)
    later_pos = (
        (seq_index + distances(core, -1))[:, None] * rows + jnp.arange(rows, dtype=jnp.int32)[None]
    ).reshape(-1)
    allowed = seen(own_pos, key_pos)
    allowed_later = seen(later_pos, own_pos)

    queries = query_rows.reshape(rows, heads, HD)
    key_all = key_value[:, :features].reshape(-1, heads, HD)
    value_all = key_value[:, features:].reshape(-1, heads, HD)

    def scores_of(query_part, key_part, mask):
        scores = (
            jnp.einsum("ihd,chd->hic", query_part, key_part, preferred_element_type=wide)
            * score_scale
        )
        return jnp.where(mask[None], scores, masked_value)

    scores = scores_of(queries, key_all, allowed)
    row_peak = jnp.max(scores, axis=-1, keepdims=True)
    log_total = row_peak + jnp.log(jnp.sum(jnp.exp(scores - row_peak), axis=-1, keepdims=True))
    weights_low = jnp.exp(scores - log_total).astype(low)
    mixed = jnp.einsum("hic,chd->ihd", weights_low, value_all, preferred_element_type=wide)
    heads_out = mixed.reshape(rows, -1).astype(low)

    attn_sum = tp_reduce_scatter(matmul(heads_out, w_out).astype(low), tp_index)
    hidden = own_share(inputs) + attn_sum
    factor_ffn = rms_factor(hidden)
    unit_ffn = hidden * factor_ffn
    normed_ffn = tp_all_gather((unit_ffn * gain_ffn).astype(low), tp_index)

    log_parts = split_three(log_total[:, :, 0])
    log_cols = jnp.concatenate([part.T for part in log_parts], axis=1)
    log_cols = jnp.pad(log_cols, ((0, 0), (0, HD - log_cols.shape[1])))
    query_side = neighbours(
        jnp.concatenate([query_rows, heads_out, log_cols], axis=1), core, -1
    )

    gate_pre = matmul(normed_ffn, w_gate)
    up_pre = matmul(normed_ffn, w_up)
    gate_sigmoid = jax.nn.sigmoid(gate_pre)
    gate_silu = gate_pre * gate_sigmoid
    activated = (gate_silu * up_pre).astype(low)
    grad_act = times_trans(cotangent, w_down)
    grad_gate = (
        grad_act * up_pre * gate_sigmoid * (1.0 + gate_pre * (1.0 - gate_sigmoid))
    ).astype(low)
    grad_up = (grad_act * gate_silu).astype(low)
    grad_normed_ffn = tp_reduce_scatter(
        (times_trans(grad_gate, w_gate) + times_trans(grad_up, w_up)).astype(low), tp_index
    )

    def down_part(bit):
        return outer_sum(activated, cut(cotangent, 1, bit))

    def gate_up_part(bit):
        side = cut(normed_ffn, 1, bit)
        return jnp.concatenate([outer_sum(grad_gate, side), outer_sum(grad_up, side)], axis=0)

    grad_w_down = seq_all_reduce(down_part, 1, bits)
    grad_gate_up = seq_all_reduce(gate_up_part, 1, bits)

    ffn_sum = tp_reduce_scatter(matmul(activated, w_down).astype(low), tp_index)
    block_out = tp_all_gather((hidden + ffn_sum).astype(low), tp_index)

    gain_ffn_part = jnp.sum(grad_normed_ffn * unit_ffn, axis=0)
    grad_hidden = own_share(cotangent).astype(wide) + norm_back(
        grad_normed_ffn, unit_ffn, factor_ffn, gain_ffn
    )
    grad_hidden_low = tp_all_gather(grad_hidden.astype(low), tp_index)
    grad_heads_rows = times_trans(grad_hidden_low, w_out).astype(low)
    grad_heads_all = neighbours(grad_heads_rows, core, -1).reshape(-1, heads, HD)
    grad_heads = grad_heads_rows.reshape(rows, heads, HD)

    inner = jnp.sum(
        grad_heads.astype(wide) * heads_out.reshape(rows, heads, HD).astype(wide), axis=-1
    )
    weights = jnp.exp(scores_of(queries, key_all, allowed) - log_total)
    grad_probs = jnp.einsum("ihd,chd->hic", grad_heads, value_all, preferred_element_type=wide)
    grad_scores = (weights * (grad_probs - inner.T[:, :, None])).astype(low)
    grad_query = (
        jnp.einsum("hic,chd->ihd", grad_scores, key_all, preferred_element_type=wide) * score_scale
    )
    grad_query = grad_query.reshape(rows, -1).astype(low)

    query_all = query_side[:, :features].reshape(-1, heads, HD)
    mixed_all = query_side[:, features : 2 * features].reshape(-1, heads, HD)
    logs = query_side[:, 2 * features : 2 * features + 3 * heads].astype(wide)
    log_all = logs[:, :heads] + logs[:, heads : 2 * heads] + logs[:, 2 * heads :]
    inner_all = jnp.sum(grad_heads_all.astype(wide) * mixed_all.astype(wide), axis=-1)
    own_keys = key_rows.reshape(rows, heads, HD)
    own_values = value_rows.reshape(rows, heads, HD)
    weights_later = jnp.exp(
        scores_of(query_all, own_keys, allowed_later) - log_all.T[:, :, None]
    )
    grad_value = jnp.einsum(
        "hic,ihd->chd", weights_later.astype(low), grad_heads_all, preferred_element_type=wide
    )
    grad_probs_later = jnp.einsum(
        "ihd,chd->hic", grad_heads_all, own_values, preferred_element_type=wide
    )
    grad_scores_later = (weights_later * (grad_probs_later - inner_all.T[:, :, None])).astype(low)
    grad_key = (
        jnp.einsum("hic,ihd->chd", grad_scores_later, query_all, preferred_element_type=wide)
        * score_scale
    )
    grad_key = grad_key.reshape(rows, -1).astype(low)
    grad_value = grad_value.reshape(rows, -1).astype(low)

    grad_qkv = jnp.concatenate([grad_query, grad_key, grad_value], axis=1)

    def attn_part(bit):
        return jnp.concatenate(
            [
                outer_sum(cut(normed_attn, 1, bit), grad_qkv),
                outer_sum(cut(grad_hidden_low, 1, bit), heads_out),
            ],
            axis=1,
        )

    local_back = (
        times_trans(grad_query, w_query)
        + times_trans(grad_key, w_key)
        + times_trans(grad_value, w_value)
    )
    grad_normed_attn = tp_reduce_scatter(local_back.astype(low), tp_index)
    gain_attn_part = jnp.sum(local_back * unit_attn, axis=0)
    grad_attn = seq_all_reduce(attn_part, 0, bits)

    gains = sum_everywhere(jnp.stack([gain_attn_part, gain_ffn_part]))
    gains = lax.dynamic_slice_in_dim(gains, tp_index * (width // TP), width // TP, 1)

    grad_tokens = grad_hidden + norm_back(
        grad_normed_attn, own_share(unit_attn), own_share(factor_attn), gain_attn
    )
    grad_tokens = tp_all_gather(grad_tokens.astype(low), tp_index).astype(wide)
    hidden_units = w_gate.shape[1]
    return (
        block_out,
        grad_tokens,
        gains[0],
        grad_attn[:, :features],
        grad_attn[:, features : 2 * features],
        grad_attn[:, 2 * features : 3 * features],
        grad_attn[:, 3 * features :].T,
        gains[1],
        grad_gate_up[:hidden_units].T,
        grad_gate_up[hidden_units:].T,
        grad_w_down,
    )


def solution(mesh):
    return jax.shard_map(
        on_device,
        mesh=mesh,
        in_specs=(
            P("seq", None),
            P(),
            P(None, "tp"),
            P(None, "tp"),
            P(None, "tp"),
            P("tp", None),
            P(),
            P(None, "tp"),
            P(None, "tp"),
            P("tp", None),
            P("seq", None),
        ),
        out_specs=(
            P("seq", None),
            P("seq", None),
            P("tp"),
            P(None, "tp"),
            P(None, "tp"),
            P(None, "tp"),
            P("tp", None),
            P("tp"),
            P(None, "tp"),
            P(None, "tp"),
            P("tp", None),
        ),
        check_vma=False,
    )
```

```python
import jax
import jax.numpy as jnp
from jax import lax
from jax.experimental import pallas as pl
from jax.experimental.pallas import tpu as pltpu
from jax.sharding import Mesh
from jax.sharding import PartitionSpec as P

HD = 128
W = 1024
SEQ = 16
TP = 8
Z_FLIPS = (2, 1, 3)
FFN_PIECES = (
    ((0, 0, 688), (1, 0, 128)),
    ((1, 128, 688), (2, 0, 256)),
    ((2, 256, 688),),
)
FFN_ROWS = (816, 816, 432)

epsilon = 1e-06
masked_value = -1e30
low = jnp.bfloat16
wide = jnp.float32


def seq_pairs(step):
    pairs = []
    for x_hi in range(2):
        for y in range(4):
            for core in range(2):
                to = step(x_hi, y, core)
                if to is not None:
                    pairs.append((x_hi * 8 + y * 2 + core, to[0] * 8 + to[1] * 2 + to[2]))
    return pairs


EXCHANGE = {
    "core": seq_pairs(lambda x, y, c: (x, y, 1 - c)),
    "y1": seq_pairs(lambda x, y, c: (x, y ^ 1, c)),
    "y3": seq_pairs(lambda x, y, c: (x, y ^ 3, c)),
    "x": seq_pairs(lambda x, y, c: (1 - x, y, c)),
}

SEQ_AXES = ("x_hi", "y", "core")


def by_seq(value, name):
    return lax.ppermute(value, SEQ_AXES, EXCHANGE[name])


def by_tp(value, flip):
    return lax.ppermute(value, "tp", [(k, k ^ flip) for k in range(TP)])


def shifted(value, steps):
    pairs = [(k, k + steps) for k in range(SEQ) if 0 <= k + steps < SEQ]
    return lax.ppermute(value, SEQ_AXES, pairs)


def z_exchange(blocks):
    return [by_tp(block, 2 * flip) for flip, block in zip(Z_FLIPS, blocks)]


def z_spread(block):
    return [by_tp(block, 2 * flip) for flip in Z_FLIPS]


def places():
    x_hi = lax.axis_index("x_hi")
    y = lax.axis_index("y")
    core = lax.axis_index("core")
    tp = lax.axis_index("tp")
    return {
        "seq": x_hi * 8 + y * 2 + core,
        "tp": tp,
        "z": tp >> 1,
        "x_low": tp & 1,
        "core": core,
        "y1": (y & 1) ^ (y >> 1),
        "y3": y >> 1,
        "x": x_hi,
    }


class Order:
    def __init__(self):
        self.last = None

    def __call__(self, body, ins, outs, needs=(), scratch=(), temporary=2 << 20):
        ins = list(ins)
        needs = list(needs)
        if self.last is not None and not any(value is self.last for value in ins):
            needs.append(self.last)
        skip = len(ins) + len(needs)
        out_shape = [jax.ShapeDtypeStruct(shape, kind) for shape, kind in outs]
        count = len(ins)

        def run(*refs):
            body(refs[:count], refs[skip : skip + len(outs)], refs[skip + len(outs) :])

        def size(shape, kind):
            lanes = -(-shape[-1] // 128) * 128
            total = lanes * jnp.dtype(kind).itemsize
            for extent in shape[:-1]:
                total *= max(extent, 1)
            return total

        held = (
            sum(size(value.shape, value.dtype) for value in ins)
            + sum(size(shape, kind) for shape, kind in outs)
            + sum(size(shape, kind) for shape, kind in scratch)
        )
        result = pl.pallas_call(
            run,
            out_shape=out_shape,
            in_specs=[pl.BlockSpec(memory_space=pltpu.VMEM)] * count
            + [pl.BlockSpec(memory_space=pl.ANY)] * len(needs),
            out_specs=[pl.BlockSpec(memory_space=pltpu.VMEM)] * len(outs),
            scratch_shapes=[pltpu.VMEM(shape, kind) for shape, kind in scratch],
            compiler_params=pltpu.CompilerParams(vmem_limit_bytes=held + temporary),
            cost_estimate=pl.CostEstimate(flops=0, bytes_accessed=0, transcendentals=0),
            name=body.__name__,
        )(*ins, *needs)
        self.last = result[0]
        return result


def hold(order, values, needs=()):
    values = list(values)
    needs = list(needs) + [order.last]

    def run(*refs):
        pass

    return pl.pallas_call(
        run,
        out_shape=[jax.ShapeDtypeStruct(value.shape, value.dtype) for value in values],
        in_specs=[pl.BlockSpec(memory_space=pl.ANY)] * (len(values) + len(needs)),
        out_specs=[pl.BlockSpec(memory_space=pl.ANY)] * len(values),
        input_output_aliases={k: k for k in range(len(values))},
        compiler_params=pltpu.CompilerParams(vmem_limit_bytes=1 << 20),
        cost_estimate=pl.CostEstimate(flops=0, bytes_accessed=0, transcendentals=0),
    )(*values, *needs)


def dot(left, right):
    return jnp.dot(left, right, preferred_element_type=wide)


def dot_rows(left, right):
    return lax.dot_general(left, right, (((1,), (1,)), ((), ())), preferred_element_type=wide)


def dot_cols(left, right):
    return lax.dot_general(left, right, (((0,), (0,)), ((), ())), preferred_element_type=wide)


def rms_factor(rows):
    return lax.rsqrt(jnp.mean(rows * rows, axis=-1, keepdims=True) + epsilon)


def norm_back(grad_normed, unit_rows, factor, gain_vec):
    scaled = grad_normed * gain_vec
    return factor * (scaled - unit_rows * jnp.mean(scaled * unit_rows, axis=-1, keepdims=True))


def span(index, size):
    return pl.ds(pl.multiple_of(index * size, size), size)


def write_blocks(partial, z, outs):
    size = outs[0].shape[0]
    for flip, out in zip((0,) + Z_FLIPS, outs):
        out[...] = partial[span(z ^ flip, size), :]


def read_blocks(whole, z, blocks, first=0, width=None):
    size = blocks[0].shape[0]
    for flip, block in zip((0,) + Z_FLIPS, blocks):
        value = block[...] if width is None else block[:, first : first + width]
        whole[span(z ^ flip, size), :] = value.astype(whole.dtype)


def normed_kernel(ins, outs, _):
    tokens, gain, w_key, w_value = ins
    normed, key_value = outs
    inputs = tokens[...].astype(wide)
    rows = (inputs * rms_factor(inputs) * gain[...]).astype(low)
    normed[...] = rows
    features = w_key.shape[1]
    key_value[:, :features] = dot(rows, w_key[...]).astype(low)
    key_value[:, features:] = dot(rows, w_value[...]).astype(low)


def project_kernel(ins, outs, _):
    outs[0][...] = dot(ins[0][...], ins[1][...]).astype(low)


def last_block(at, own_of_partner, four_of_partner, way):
    near = at["core"] == (0 if way == 1 else 1)
    return jnp.where(near, four_of_partner, own_of_partner)


def seen_scores(scores, order, distance, gap, inside):
    if order == 0:
        return jnp.where(gap >= 0, scores, masked_value)
    if order == 3:
        return jnp.where((gap < 0) & inside, scores, masked_value)
    return jnp.where(inside, scores, masked_value)


def distances(at, way):
    near = at["core"] == (0 if way == 1 else 1)
    return [0, 2, jnp.where(near, 1, 3), 4, jnp.where(near, 3, 1)]


def gap_of(rows, flipped=False):
    first = lax.broadcasted_iota(jnp.int32, (rows, rows), 0)
    second = lax.broadcasted_iota(jnp.int32, (rows, rows), 1)
    return second - first if flipped else first - second


def attend_kernel(ins, outs, scratch):
    query, own, two, across, four, partner_own, partner_four, w_out = ins
    side, log_out = outs[:2]
    rows, features = query.shape
    at = places()
    scale = HD ** (-0.5)
    gap = gap_of(rows)
    away = distances(at, 1)
    blocks = [own[...], two[...], across[...], four[...]]
    blocks.append(last_block(at, partner_own[...], partner_four[...], 1))
    logs = []
    mixed = []
    for head in range(features // HD):
        here = slice(head * HD, (head + 1) * HD)
        there = slice(features + head * HD, features + (head + 1) * HD)
        scores = [
            seen_scores(
                dot_rows(query[:, here], block[:, here]) * scale,
                order,
                distance,
                gap,
                at["seq"] >= distance,
            )
            for order, (block, distance) in enumerate(zip(blocks, away))
        ]
        peak = scores[0].max(axis=-1, keepdims=True)
        for part in scores[1:]:
            peak = jnp.maximum(peak, part.max(axis=-1, keepdims=True))
        raised = [jnp.exp(part - peak) for part in scores]
        total = raised[0].sum(axis=-1, keepdims=True)
        for part in raised[1:]:
            total = total + part.sum(axis=-1, keepdims=True)
        inverse = 1.0 / total
        out = dot((raised[0] * inverse).astype(low), blocks[0][:, there])
        for part, block in zip(raised[1:], blocks[1:]):
            out = out + dot((part * inverse).astype(low), block[:, there])
        mixed.append(out.astype(low))
        logs.append(peak + jnp.log(total))
    lane = lax.broadcasted_iota(jnp.int32, (rows, HD), 1)
    both = jnp.where((lane & 32) == 0, logs[0], logs[1])
    first = both.astype(low).astype(wide)
    side[:, :features] = query[...]
    for head, out in enumerate(mixed):
        side[:, features + head * HD : features + (head + 1) * HD] = out
    side[:, 2 * features :] = jnp.where(lane < 64, first, both - first).astype(low)
    log_out[...] = jnp.where(lane < 64, logs[0], logs[1])
    partial = scratch[0]
    partial[...] = dot(side[:, features : 2 * features], w_out[...]).astype(low)
    write_blocks(partial, at["z"], outs[2:])


def sum_z_kernel(ins, outs, _):
    keep, send = outs
    at = places()
    size, width = keep.shape[0], ins[0].shape[1]
    for group in range(len(ins) // 4):
        blocks = ins[4 * group : 4 * group + 4]
        here = slice(group * width, (group + 1) * width)
        for out, index in ((keep, at["x_low"]), (send, 1 - at["x_low"])):
            total = blocks[0][span(index, size), :].astype(wide)
            for block in blocks[1:]:
                total = total + block[span(index, size), :].astype(wide)
            out[:, here] = total.astype(out.dtype)


def norm_rows_kernel(ins, outs, _):
    keep, arrived, tokens, gain = ins
    hidden, normed = outs
    at = places()
    rows = tokens[span(at["tp"], keep.shape[0]), :].astype(wide) + (
        keep[...] + arrived[...].astype(wide)
    )
    hidden[...] = rows
    normed[...] = (rows * rms_factor(rows) * gain[...]).astype(low)


def pair_kernel(ins, outs, _):
    at = places()
    size = ins[0].shape[0]
    outs[0][span(at["x_low"], size), :] = ins[0][...]
    outs[0][span(1 - at["x_low"], size), :] = ins[1][...]


def ffn_kernel(ins, outs, scratch):
    pair, block_two, block_one, block_three, w_gate, w_up, w_down, cotangent = ins
    normed, activated, grad_gate, grad_up = outs[:4]
    at = places()
    read_blocks(normed, at["z"], (pair, block_two, block_one, block_three))
    rows = normed[...]
    gate_pre = dot_rows(rows, w_gate[...])
    up_pre = dot_rows(rows, w_up[...])
    grad_act = dot_rows(cotangent[...], w_down[...])
    sigmoid = jax.nn.sigmoid(gate_pre)
    silu = gate_pre * sigmoid
    activated[...] = (silu * up_pre).astype(low)
    grad_gate[...] = (grad_act * up_pre * sigmoid * (1.0 + gate_pre * (1.0 - sigmoid))).astype(low)
    grad_up[...] = (grad_act * silu).astype(low)
    partial = scratch[0]
    partial[...] = (dot(grad_gate[...], w_gate[...]) + dot(grad_up[...], w_up[...])).astype(low)
    write_blocks(partial, at["z"], outs[4:])


def grad_rows_kernel(ins, outs, _):
    keep, arrived, hidden, cotangent, gain = ins
    grad_hidden, grad_low, gain_part = outs
    at = places()
    grad_normed = keep[...] + arrived[...].astype(wide)
    rows = hidden[...]
    factor = rms_factor(rows)
    unit = rows * factor
    gain_part[...] = jnp.sum(grad_normed * unit, axis=0, keepdims=True)
    grad = cotangent[span(at["tp"], keep.shape[0]), :].astype(wide) + norm_back(
        grad_normed, unit, factor, gain[...]
    )
    grad_hidden[...] = grad
    grad_low[...] = grad.astype(low)


def heads_kernel(ins, outs, _):
    grad_hidden, grad_heads = outs
    read_blocks(grad_hidden, places()["z"], ins[:4])
    grad_heads[...] = dot_rows(grad_hidden[...], ins[4][...]).astype(low)


def grad_query_kernel(ins, outs, _):
    side, logs, grad_heads, own, two, across, four, partner_own, partner_four = ins
    rows, features = grad_heads.shape
    at = places()
    scale = HD ** (-0.5)
    gap = gap_of(rows)
    away = distances(at, 1)
    blocks = [own[...], two[...], across[...], four[...]]
    blocks.append(last_block(at, partner_own[...], partner_four[...], 1))
    for head in range(features // HD):
        here = slice(head * HD, (head + 1) * HD)
        there = slice(features + head * HD, features + (head + 1) * HD)
        query = side[:, here]
        grad = grad_heads[:, here]
        log_total = logs[:, head * 64 : head * 64 + 1]
        inner = jnp.sum(
            grad.astype(wide) * side[:, there].astype(wide), axis=-1, keepdims=True
        )
        total = jnp.zeros((rows, HD), wide)
        for order, (block, distance) in enumerate(zip(blocks, away)):
            scores = seen_scores(
                dot_rows(query, block[:, here]) * scale,
                order,
                distance,
                gap,
                at["seq"] >= distance,
            )
            weights = jnp.exp(scores - log_total)
            grad_scores = weights * (dot_rows(grad, block[:, there]) - inner)
            total = total + dot(grad_scores.astype(low), block[:, here])
        outs[0][:, here] = (total * scale).astype(low)


def grad_key_kernel(ins, outs, scratch):
    key_value = ins[0]
    sides = ins[1:7]
    grads = ins[7:13]
    grad_query, w_query, w_key, w_value, tokens, gain_ffn_part, ffn_partial = ins[13:]
    grad_key, grad_value, keep_one, keep_two, send_one, send_two = outs
    rows, features = grad_query.shape
    at = places()
    scale = HD ** (-0.5)
    gap = gap_of(rows, flipped=True)
    away = distances(at, -1)
    side_blocks = [side[...] for side in sides[:4]]
    side_blocks.append(last_block(at, sides[4][...], sides[5][...], -1))
    grad_blocks = [grad[...] for grad in grads[:4]]
    grad_blocks.append(last_block(at, grads[4][...], grads[5][...], -1))
    log_rows = [side[:, 2 * features :].astype(wide).T for side in side_blocks]
    for head in range(features // HD):
        here = slice(head * HD, (head + 1) * HD)
        there = slice(features + head * HD, features + (head + 1) * HD)
        key = key_value[:, here]
        value = key_value[:, there]
        total_key = jnp.zeros((rows, HD), wide)
        total_value = jnp.zeros((rows, HD), wide)
        for order, (side, grad_all, logs, distance) in enumerate(
            zip(side_blocks, grad_blocks, log_rows, away)
        ):
            query = side[:, here]
            grad = grad_all[:, here]
            log_total = logs[head * 32 : head * 32 + 1] + logs[64 + head * 32 : 65 + head * 32]
            inner = jnp.sum(
                (grad.astype(wide) * side[:, there].astype(wide)).T, axis=0, keepdims=True
            )
            scores = seen_scores(
                dot_rows(key, query) * scale, order, distance, gap, at["seq"] + distance < SEQ
            )
            weights = jnp.exp(scores - log_total)
            total_value = total_value + dot(weights.astype(low), grad)
            grad_scores = weights * (dot_rows(value, grad) - inner)
            total_key = total_key + dot(grad_scores.astype(low), query)
        grad_key[:, here] = (total_key * scale).astype(low)
        grad_value[:, here] = total_value.astype(low)
    back = (
        dot_rows(grad_query[...], w_query[...])
        + dot_rows(grad_key[...], w_key[...])
        + dot_rows(grad_value[...], w_value[...])
    )
    inputs = tokens[...].astype(wide)
    gain_attn_part = jnp.sum(back * (inputs * rms_factor(inputs)), axis=0, keepdims=True)
    partial = scratch[0]
    width = tokens.shape[1]
    partial[:, :width] = back.astype(low)
    share = rows // TP
    cells = width // TP // HD
    for k in range(TP):
        parts = [
            gain[:, (k * cells + cell) * HD : (k * cells + cell + 1) * HD]
            for gain in (gain_attn_part, gain_ffn_part[...])
            for cell in range(cells)
        ]
        parts.append(jnp.zeros((share - len(parts), HD), wide))
        partial[k * share : (k + 1) * share, width:] = jnp.concatenate(parts, axis=0).astype(low)
    size = rows // 4
    z = at["z"]
    cut = width // 2
    for out, first, flips in (
        (keep_one, 0, (0, 3)),
        (send_one, 0, (1, 2)),
        (keep_two, cut, (0, 1)),
        (send_two, cut, (3, 2)),
    ):
        for k, flip in enumerate(flips):
            here = slice(k * size, (k + 1) * size)
            there = span(z ^ flip, size)
            out[here, :cut] = partial[there, first : first + cut]
            out[here, cut:width] = ffn_partial[there, first : first + cut]
            if first > 0:
                out[here, width:] = partial[there, width:]


def sum_middle_kernel(ins, outs, _):
    for keep, arrived, stay, send in ((ins[0], ins[1], outs[0], outs[1]), (ins[2], ins[3], outs[2], outs[3])):
        size = stay.shape[0]
        stay[...] = keep[:size, :].astype(wide) + arrived[:size, :].astype(wide)
        send[...] = (keep[size:, :].astype(wide) + arrived[size:, :].astype(wide)).astype(low)


def sum_last_kernel(ins, outs, _):
    keep, send = outs
    at = places()
    size = keep.shape[0]
    width = ins[0].shape[1]
    cut = width // 2
    for out, index in ((keep, at["x_low"]), (send, 1 - at["x_low"])):
        here = span(index, size)
        first = (ins[0][here, :] + ins[1][here, :].astype(wide)).astype(out.dtype)
        second = (ins[2][here, :] + ins[3][here, :].astype(wide)).astype(out.dtype)
        out[:, :cut] = first[:, :cut]
        out[:, cut:width] = second[:, :cut]
        out[:, width : width + cut] = first[:, cut:]
        out[:, width + cut : 2 * width] = second[:, cut:width]
        out[:, 2 * width :] = second[:, width:]


def last_rows_kernel(ins, outs, _):
    keep, arrived, grad_hidden, hidden, tokens, gain = ins
    rows_out, gains = outs
    width = hidden.shape[1]
    at = places()
    inputs = tokens[span(at["tp"], keep.shape[0]), :].astype(wide)
    factor = rms_factor(inputs)
    grad_normed = keep[:, :width] + arrived[:, :width].astype(wide)
    grad = grad_hidden[...] + norm_back(grad_normed, inputs * factor, factor, gain[...])
    rows_out[:, :width] = grad.astype(low)
    rows_out[:, width:] = (
        hidden[...] + keep[:, width : 2 * width] + arrived[:, width : 2 * width].astype(wide)
    ).astype(low)
    sums = keep[:, 2 * width :] + arrived[:, 2 * width :].astype(wide)
    gains[...] = jnp.zeros_like(gains)
    gains[:, : sums.shape[1]] = sums[: gains.shape[0], :].astype(low)


def last_pair_kernel(ins, outs, _):
    at = places()
    size = ins[0].shape[0]
    width = outs[0].shape[1]
    for value, index in zip(ins, (at["x_low"], 1 - at["x_low"])):
        outs[0][span(index, size), :] = value[:, :width]
        outs[1][span(index, size), :] = value[:, width:]


def stack_kernel(ins, outs, _):
    for k, out in enumerate(outs):
        size = ins[2 * k].shape[0]
        out[:size, :] = ins[2 * k][...]
        out[size:, :] = ins[2 * k + 1][...]


def token_outputs_kernel(ins, outs, _):
    z = places()["z"]
    size = ins[0].shape[0] // 2
    for out, own, arrived, flips in (
        (outs[0], ins[0], ins[1], (0, 1, 3, 2)),
        (outs[1], ins[2], ins[3], (0, 3, 1, 2)),
    ):
        blocks = (own[:size, :], own[size:, :], arrived[:size, :], arrived[size:, :])
        for flip, block in zip(flips, blocks):
            out[span(z ^ flip, size), :] = block.astype(out.dtype)


def part(ref, axis, start, size):
    return ref[:, pl.ds(start, size)] if axis == 1 else ref[pl.ds(start, size), :]


def put(ref, axis, start, size, value):
    if axis == 1:
        ref[:, pl.ds(start, size)] = value
    else:
        ref[pl.ds(start, size), :] = value


def split_op(keep, arrived, bit, axis):
    shape = list(keep.shape)
    shape[axis] //= 2
    size = shape[axis]

    def body(at, ins, outs):
        for out, index in zip(outs, (at[bit], 1 - at[bit])):
            start = pl.multiple_of(index * size, size)
            out[...] = (
                part(ins[0], axis, start, size).astype(wide)
                + part(ins[1], axis, start, size).astype(wide)
            ).astype(low)

    return body, [keep, arrived], [(tuple(shape), low)] * 2


def add_op(keep, arrived):
    def body(at, ins, outs):
        outs[0][...] = (ins[0][...].astype(wide) + ins[1][...].astype(wide)).astype(
            outs[0].dtype
        )

    return body, [keep, arrived], [(keep.shape, keep.dtype)]


def join_op(own, arrived, bit, axis, kind=low):
    shape = list(own.shape)
    size = shape[axis]
    shape[axis] *= 2

    def body(at, ins, outs):
        for value, index in zip(ins, (at[bit], 1 - at[bit])):
            start = pl.multiple_of(index * size, size)
            put(outs[0], axis, start, size, value[...].astype(kind))

    return body, [own, arrived], [(tuple(shape), kind)]


def add_tail_op(keep, arrived, tail):
    rows, width = keep.shape

    def body(at, ins, outs):
        outs[0][:rows, :] = (ins[0][...].astype(wide) + ins[1][...].astype(wide)).astype(low)
        outs[0][rows:, :] = ins[2][...]

    return body, [keep, arrived, tail], [((rows + tail.shape[0], width), low)]


def join_tail_op(own, arrived, bit, tail):
    rows, width = own.shape
    size = rows - tail

    def body(at, ins, outs):
        for value, index in zip(ins, (at[bit], 1 - at[bit])):
            outs[0][span(index, size), :] = value[:size, :]
        outs[0][2 * size :, :] = (
            ins[0][size:, :].astype(wide) + ins[1][size:, :].astype(wide)
        ).astype(low)

    return body, [own, arrived], [((2 * size + tail, width), low)]


def run_ops(order, ops, needs=()):
    ins = [value for _, values, _ in ops for value in values]
    outs = [out for _, _, shapes in ops for out in shapes]

    def body(in_refs, out_refs, _):
        at = places()
        first = last = 0
        for step, values, shapes in ops:
            step(
                at,
                in_refs[first : first + len(values)],
                out_refs[last : last + len(shapes)],
            )
            first += len(values)
            last += len(shapes)

    flat = list(order(body, ins, outs, needs))
    result = []
    for _, _, shapes in ops:
        result.append(flat[: len(shapes)])
        flat = flat[len(shapes) :]
    return result


FFN_ORDERS = (("y1", "y3", "x"), ("y3", "x", "y1"), ("x", "y1", "y3"))


def ffn_terms(ins, k):
    terms = []
    first = 0
    for operand, start, stop in FFN_PIECES[k]:
        last = first + stop - start
        terms.append((first, last, ins[operand][:, start:stop], ins[4 if operand == 2 else 3]))
        first = last
    return terms


def ffn_send_kernel(arrays):
    def ffn_send(ins, outs, _):
        out = outs[0]
        half = out.shape[1]
        other = 1 - places()["core"]
        base = 0
        for k in arrays:
            for first, last, left, right in ffn_terms(ins, k):
                out[base + first : base + last, :] = dot_cols(
                    left, right[:, span(other, half)]
                ).astype(low)
            base += FFN_ROWS[k]

    return ffn_send


def ffn_keep_kernel(arrays):
    def ffn_keep(ins, outs, _):
        at = places()
        arrived = ins[5]
        base = 0
        for k, keep, send in zip(arrays, outs[0::2], outs[1::2]):
            size = keep.shape[1]
            bit = at[FFN_ORDERS[k][0]]
            for out, index in ((keep, bit), (send, 1 - bit)):
                start = pl.multiple_of((2 * at["core"] + index) * size, size)
                for first, last, left, right in ffn_terms(ins, k):
                    own = dot_cols(left, right[:, pl.ds(start, size)])
                    got = arrived[base + first : base + last, span(index, size)]
                    out[first:last, :] = (own + got.astype(wide)).astype(low)
            base += FFN_ROWS[k]

    return ffn_keep


def attn_terms(ins):
    normed, grad_hidden, grad_query, grad_key, grad_value, heads_out = ins
    half = heads_out.shape[1] // 2
    return [
        [(normed, grad_query[...]), (grad_hidden, heads_out[:, :half])],
        [(normed, grad_key[...]), (grad_hidden, heads_out[:, half:])],
        [(normed, grad_value[...])],
    ]


def attn_send_kernel(ins, outs, _):
    out = outs[0]
    half = out.shape[0]
    other = 1 - places()["core"]
    first = 0
    for terms in attn_terms(ins):
        for left, right in terms:
            last = first + right.shape[1]
            out[:, first:last] = dot_cols(left[:, span(other, half)], right).astype(low)
            first = last


ATTN_ORDERS = (("y1", "y3", "x"), ("y3", "x", "y1"), ("x", "y1", "y3"))


def packed_rows(rows, lanes, width):
    across = width // 128
    full, rest = divmod(lanes // 128, across)
    if rest == 1 and rows % across == 0:
        return rows * full + rows // across
    return rows * (full + (rest > 0))


def place_cells(rows, lanes, width):
    across = width // 128
    cells = lanes // 128
    runs = []
    full = cells // across
    for k in range(full * across):
        runs.append((0, k * 128, (k // across) * rows, (k % across) * 128, rows))
    rest = cells - full * across
    if rest and rows % across == 0 and rest == 1:
        size = rows // across
        for k in range(across):
            runs.append((k * size, full * across * 128, full * rows, k * 128, size))
    elif rest:
        for k in range(rest):
            runs.append((0, (full * across + k) * 128, full * rows, k * 128, rows))
    return runs


def pack(message, base, value):
    rows, lanes = value.shape
    for row, lane, to_row, to_lane, size in place_cells(rows, lanes, message.shape[1]):
        message[base + to_row : base + to_row + size, to_lane : to_lane + 128] = value[
            row : row + size, lane : lane + 128
        ]


def add_packed(keep, message, base, lanes):
    rows = keep.shape[0]
    columns = [[] for _ in range(lanes // 128)]
    for row, lane, from_row, from_lane, size in place_cells(rows, lanes, message.shape[1]):
        here = keep[row : row + size, lane : lane + 128].astype(wide)
        there = message[base + from_row : base + from_row + size, from_lane : from_lane + 128]
        columns[lane // 128].append(here + there.astype(wide))
    return [jnp.concatenate(parts, axis=0) if len(parts) > 1 else parts[0] for parts in columns]


ATTN_ORDERS = (("y1", "y3", "x"), ("y3", "x", "y1"), ("x", "y1", "y3"))
WAYS = ("y1", "y3", "x")


def round_one_kernel(ins, outs, _):
    at = places()
    operands, arrived = ins[6:12], ins[12]
    messages = dict(zip(WAYS, outs[:3]))
    tops = {orders[2]: rows for orders, rows in zip(FFN_ORDERS, FFN_ROWS)}
    for k in range(3):
        messages[FFN_ORDERS[k][2]][: FFN_ROWS[k], :] = (
            ins[k][...].astype(wide) + ins[3 + k][...].astype(wide)
        ).astype(low)
    base = 0
    for k, terms in enumerate(attn_terms(operands)):
        keep = outs[3 + k]
        size, lanes = keep.shape
        way = ATTN_ORDERS[k][0]
        for kept, index in ((True, at[way]), (False, 1 - at[way])):
            start = pl.multiple_of((2 * at["core"] + index) * size, size)
            first = 0
            for left, right in terms:
                last = first + right.shape[1]
                value = dot_cols(left[:, pl.ds(start, size)], right)
                value = value + arrived[span(index, size), base + first : base + last].astype(wide)
                value = value.astype(low)
                if kept:
                    keep[:, first:last] = value
                else:
                    for lane in range(first, last, 128):
                        row = tops[way] + lane // 128 * size
                        messages[way][row : row + size, :] = value[
                            :, lane - first : lane - first + 128
                        ]
                first = last
        base += lanes


def round_next_kernel(step):
    def round_next(ins, outs, _):
        at = places()
        sent, arrived = dict(zip(WAYS, ins[:3])), dict(zip(WAYS, ins[3:6]))
        messages = dict(zip(WAYS, outs[:3]))
        came_tops = {orders[3 - step]: rows for orders, rows in zip(FFN_ORDERS, FFN_ROWS)}
        tops = {orders[2 - step]: rows for orders, rows in zip(FFN_ORDERS, FFN_ROWS)}
        for k in range(3):
            back = FFN_ORDERS[k][3 - step]
            message = messages[FFN_ORDERS[k][2 - step]]
            width = sent[back].shape[1]
            rows = FFN_ROWS[k]
            for value, index in ((sent[back], at[back]), (arrived[back], 1 - at[back])):
                start = pl.multiple_of(index * width, width)
                message[:rows, pl.ds(start, width)] = value[:rows, :]
        for k in range(3):
            keep = ins[6 + k]
            came, way = ATTN_ORDERS[k][step - 1], ATTN_ORDERS[k][step]
            columns = add_packed(keep, arrived[came], came_tops[came], keep.shape[1])
            size = keep.shape[0] // 2
            halves = []
            for column in columns:
                halves.append((column[:size, :], column[size:, :]))
            first = at[way] == 0
            stay = [jnp.where(first, one, two).astype(low) for one, two in halves]
            go = [jnp.where(first, two, one).astype(low) for one, two in halves]
            for lane, value in enumerate(stay):
                outs[3 + k][:, lane * 128 : (lane + 1) * 128] = value
            pack(messages[way], tops[way], jnp.concatenate(go, axis=1))

    return round_next


def round_last_kernel(ins, outs, _):
    arrived = dict(zip(WAYS, ins[:3]))
    tops = {orders[0]: rows for orders, rows in zip(FFN_ORDERS, FFN_ROWS)}
    for k in range(3):
        keep = ins[3 + k]
        rows = keep.shape[0]
        way = ATTN_ORDERS[k][2]
        columns = add_packed(keep, arrived[way], tops[way], keep.shape[1])
        for lane, column in enumerate(columns):
            outs[k][:rows, lane * 128 : (lane + 1) * 128] = column.astype(low)
    outs[2][ins[5].shape[0] :, :] = ins[6][...]


def ffn_halves_kernel(ins, outs, _):
    at = places()
    sent, arrived = dict(zip(WAYS, ins[:3])), dict(zip(WAYS, ins[3:]))
    base = 0
    for k, rows in enumerate(FFN_ROWS):
        way = FFN_ORDERS[k][0]
        width = sent[way].shape[1]
        for value, index in ((sent[way], at[way]), (arrived[way], 1 - at[way])):
            start = pl.multiple_of(index * width, width)
            outs[0][base : base + rows, pl.ds(start, width)] = value[:rows, :]
        base += rows


def attn_output_kernel(ins, outs, _):
    core = places()["core"]
    grad_query, grad_key, grad_value, grad_out, gain_attn, gain_ffn = outs
    features = grad_query.shape[1]
    half = ins[0].shape[0]
    for k in (0, 1):
        index = core if k == 0 else 1 - core
        one, two, three = ins[k], ins[2 + k], ins[4 + k]
        here = span(index, half)
        grad_query[here, :] = one[:, :features].astype(wide)
        grad_key[here, :] = two[:, :features].astype(wide)
        grad_value[here, :] = three[:half, :].astype(wide)
        grad_out[: features // 2, here] = one[:, features:].astype(wide).T
        grad_out[features // 2 :, here] = two[:, features:].astype(wide).T
    sums = ins[4][half:, :].astype(wide) + ins[5][half:, :].astype(wide)
    for k, out in enumerate((gain_attn, gain_ffn)):
        out[:, :HD] = sums[2 * k : 2 * k + 1, :HD]
        out[:, HD:] = sums[2 * k + 1 : 2 * k + 2, :HD]


def ffn_output(order, own, arrived, which, units):
    half = own.shape[1]

    def run(own_ref, arrived_ref, need_ref, out_ref):
        first = places()["core"] == 0
        one, two = own_ref[...].astype(wide), arrived_ref[...].astype(wide)
        out_ref[:, :half] = jnp.where(first, one, two)
        out_ref[:, half:] = jnp.where(first, two, one)

    result = pl.pallas_call(
        run,
        out_shape=jax.ShapeDtypeStruct((units, 2 * half), wide),
        grid=(1,),
        in_specs=[pl.BlockSpec((units, half), lambda k: (which, 0))] * 2
        + [pl.BlockSpec(memory_space=pl.ANY)],
        out_specs=pl.BlockSpec((units, 2 * half), lambda k: (0, 0)),
        compiler_params=pltpu.CompilerParams(vmem_limit_bytes=32 << 20),
        cost_estimate=pl.CostEstimate(flops=0, bytes_accessed=0, transcendentals=0),
    )(own, arrived, order.last)
    order.last = result
    return result


def on_device(
    tokens, gain_attn, w_query, w_key, w_value, w_out, gain_ffn, w_gate, w_up, w_down, cotangent
):
    rows, width = tokens.shape
    features = w_query.shape[1]
    units = w_gate.shape[1]
    share = rows // TP
    quarter = rows // 4
    order = Order()
    gain_attn = gain_attn.reshape(1, width)
    gain_ffn = gain_ffn.reshape(1, width)
    w_gate, w_up = w_gate.T, w_up.T
    blocks_out = [((quarter, width), low)] * 4
    whole = ((rows, width), low)
    small = ((rows, features), low)
    keep_and_send = [((share, width), wide), ((share, width), low)]

    normed_attn, own = order(
        normed_kernel,
        [tokens, gain_attn, w_key, w_value],
        [whole, ((rows, 2 * features), low)],
        temporary=6 << 20,
    )
    two, four = shifted(own, 2), shifted(own, 4)
    partner_own = by_seq(own, "core")
    (query,) = order(project_kernel, [normed_attn, w_query], [small])
    across = by_seq(two, "core")
    partner_four = by_seq(four, "core")
    keys = [own, two, across, four, partner_own, partner_four]
    side, logs, *blocks = order(
        attend_kernel,
        [query] + keys + [w_out],
        [((rows, 2 * features + HD), low), ((rows, HD), wide)] + blocks_out,
        scratch=[whole],
        temporary=6 << 20,
    )
    arrived = z_exchange(blocks[1:])
    keep, send = order(sum_z_kernel, [blocks[0]] + arrived, keep_and_send)
    arrived = by_tp(send, 1)

    hidden, normed_rows = order(norm_rows_kernel, [keep, arrived, tokens, gain_ffn], keep_and_send)
    arrived = by_tp(normed_rows, 1)

    (side_out,) = hold(order, [side])
    side_two, side_four = shifted(side_out, -2), shifted(side_out, -4)
    side_partner_own = by_seq(side_out, "core")

    (pair,) = order(pair_kernel, [normed_rows, arrived], [((quarter, width), low)])
    arrived = z_spread(pair)

    normed_ffn, activated, grad_gate, grad_up, *blocks = order(
        ffn_kernel,
        [pair] + arrived + [w_gate, w_up, w_down, cotangent],
        [whole] + [((rows, units), low)] * 3 + blocks_out,
        needs=[side_two, side_four],
        scratch=[whole],
        temporary=12 << 20,
    )
    side_across = by_seq(side_two, "core")
    side_partner_four = by_seq(side_four, "core")
    arrived = z_exchange(blocks[1:])
    ffn_operands = [grad_gate, grad_up, activated, normed_ffn, cotangent]
    half = width // 2
    (sent,) = order(ffn_send_kernel([2]), ffn_operands, [((FFN_ROWS[2], half), low)])
    last_arrived = by_seq(sent, "core")
    (sent,) = order(
        ffn_send_kernel([0, 1]),
        ffn_operands,
        [((FFN_ROWS[0] + FFN_ROWS[1], half), low)],
        needs=[side_across, side_partner_own, side_partner_four],
        temporary=5 << 20,
    )
    first_arrived = by_seq(sent, "core")
    last_keep, last_send = order(
        ffn_keep_kernel([2]),
        ffn_operands + [last_arrived],
        [((FFN_ROWS[2], half // 2), low)] * 2,
    )
    last_arrived = by_seq(last_send, FFN_ORDERS[2][0])
    parts = order(
        ffn_keep_kernel([0, 1]),
        ffn_operands + [first_arrived],
        [((FFN_ROWS[k], half // 2), low) for k in (0, 0, 1, 1)],
        temporary=5 << 20,
    )
    ffn_keeps = [parts[0], parts[2], last_keep]
    ffn_flights = [by_seq(parts[1 + 2 * k], FFN_ORDERS[k][0]) for k in (0, 1)] + [last_arrived]

    def ffn_split(step):
        nonlocal ffn_keeps, ffn_flights
        parts = run_ops(
            order,
            [
                split_op(keep, got, names[step], 1)
                for keep, got, names in zip(ffn_keeps, ffn_flights, FFN_ORDERS)
            ],
        )
        ffn_keeps = [keep for keep, _ in parts]
        ffn_flights = [by_seq(send, names[step]) for (_, send), names in zip(parts, FFN_ORDERS)]

    keep, send = order(sum_z_kernel, [blocks[0]] + arrived, keep_and_send)
    arrived = by_tp(send, 1)
    grad_hidden, grad_low, gain_ffn_part = order(
        grad_rows_kernel,
        [keep, arrived, hidden, cotangent, gain_ffn],
        keep_and_send + [((1, width), wide)],
    )
    arrived = by_tp(grad_low, 1)
    (pair,) = order(pair_kernel, [grad_low, arrived], [((quarter, width), low)])
    arrived = z_spread(pair)
    ffn_split(1)

    grad_hidden_low, grad_heads = order(heads_kernel, [pair] + arrived + [w_out], [whole, small])
    grad_two, grad_four = shifted(grad_heads, -2), shifted(grad_heads, -4)
    grad_partner_own = by_seq(grad_heads, "core")
    (grad_query,) = order(
        grad_query_kernel, [side_out, logs, grad_heads] + keys, [small], temporary=6 << 20
    )
    (ffn_partial,) = order(project_kernel, [activated, w_down], [whole], temporary=6 << 20)
    ffn_split(2)
    grad_two, grad_four = hold(order, [grad_two, grad_four])
    grad_across = by_seq(grad_two, "core")
    grad_partner_four = by_seq(grad_four, "core")
    cut = width
    grad_key, grad_value, keep_one, keep_two, send_one, send_two = order(
        grad_key_kernel,
        [own, side_out, side_two, side_across, side_four, side_partner_own, side_partner_four]
        + [grad_heads, grad_two, grad_across, grad_four, grad_partner_own, grad_partner_four]
        + [grad_query, w_query, w_key, w_value, tokens, gain_ffn_part, ffn_partial],
        [small, small] + [((2 * quarter, cut), low), ((2 * quarter, cut + HD), low)] * 2,
        needs=ffn_flights,
        scratch=[((rows, width + HD), low)],
        temporary=12 << 20,
    )
    one_arrived, two_arrived = by_tp(send_one, 2), by_tp(send_two, 6)

    heads_out = side_out[:, features : 2 * features]
    operands = [normed_attn, grad_hidden_low, grad_query, grad_key, grad_value, heads_out]
    (sent,) = order(
        attn_send_kernel, operands, [((width // 2, 4 * features), low)], temporary=4 << 20
    )
    core_arrived = by_seq(sent, "core")
    widths = (features + features // 2, features + features // 2, features)

    def round_shapes(step):
        lanes = 128 << step
        size = width // 4 >> step
        by_way = {orders[step]: part for orders, part in zip(ATTN_ORDERS, widths)}
        tops = {orders[2 - step]: part for orders, part in zip(FFN_ORDERS, FFN_ROWS)}
        messages = [
            ((tops[way] + packed_rows(size, by_way[way], lanes), lanes), low) for way in WAYS
        ]
        return messages + [((size, lanes_attn), low) for lanes_attn in widths]

    def fly(messages):
        return [by_seq(message, way) for message, way in zip(messages, WAYS)]

    *parts, keep_x, keep_y, keep_z = order(
        round_one_kernel,
        list(ffn_keeps) + ffn_flights + operands + [core_arrived],
        round_shapes(0),
        temporary=4 << 20,
    )
    flights = fly(parts)

    stay_one, go_one, stay_two, go_two = order(
        sum_middle_kernel,
        [keep_one, one_arrived, keep_two, two_arrived],
        [
            ((quarter, cut), wide),
            ((quarter, cut), low),
            ((quarter, cut + HD), wide),
            ((quarter, cut + HD), low),
        ],
    )
    one_arrived, two_arrived = by_tp(go_one, 6), by_tp(go_two, 2)

    *parts, keep_x, keep_y, keep_z = order(
        round_next_kernel(1), parts + flights + [keep_x, keep_y, keep_z], round_shapes(1)
    )
    flights = fly(parts)
    keep, send = order(
        sum_last_kernel,
        [stay_one, one_arrived, stay_two, two_arrived],
        [((share, 2 * width + HD), wide), ((share, 2 * width + HD), low)],
    )
    arrived = by_tp(send, 1)
    last_rows, gains = order(
        last_rows_kernel,
        [keep, arrived, grad_hidden, hidden, tokens, gain_attn],
        [((share, 2 * width), low), ((16, features), low)],
    )
    arrived = by_tp(last_rows, 1)
    *parts, keep_x, keep_y, keep_z = order(
        round_next_kernel(2), parts + flights + [keep_x, keep_y, keep_z], round_shapes(2)
    )
    flights = fly(parts)
    first, second = order(last_pair_kernel, [last_rows, arrived], [((quarter, width), low)] * 2)
    first_arrived, second_arrived = by_tp(first, 2), by_tp(second, 6)
    firsts, seconds = order(
        stack_kernel,
        [first, first_arrived, second, second_arrived],
        [((2 * quarter, width), low)] * 2,
    )
    first_arrived, second_arrived = by_tp(firsts, 6), by_tp(seconds, 2)

    one, two, three = order(
        round_last_kernel,
        flights + [keep_x, keep_y, keep_z, gains],
        [((128, widths[0]), low), ((128, widths[1]), low), ((128 + 16, widths[2]), low)],
    )
    (ffn_half,) = order(ffn_halves_kernel, parts + flights, [((3 * units, width // 2), low)])
    flights = [by_seq(one, "x"), by_seq(two, "y1"), by_seq(three, "y3")]
    ffn_arrived = by_seq(ffn_half, "core")

    def attn_join(step):
        nonlocal one, two, three, flights
        names = [orders[step] for orders in ATTN_ORDERS]
        (one,), (two,), (three,) = run_ops(
            order,
            [
                join_op(one, flights[0], names[0], 0),
                join_op(two, flights[1], names[1], 0),
                join_tail_op(three, flights[2], names[2], gains.shape[0]),
            ],
        )
        names = [orders[step - 1] if step > 0 else "core" for orders in ATTN_ORDERS]
        flights = [by_seq(value, name) for value, name in zip((one, two, three), names)]

    attn_join(2)
    grad_tokens, block_out = order(
        token_outputs_kernel,
        [firsts, first_arrived, seconds, second_arrived],
        [((rows, width), wide), whole],
    )
    attn_join(1)
    grads_ffn = [ffn_output(order, ffn_half, ffn_arrived, k, units) for k in range(3)]
    attn_join(0)
    grad_w_query, grad_w_key, grad_w_value, grad_w_out, grad_gain_attn, grad_gain_ffn = order(
        attn_output_kernel,
        [one, flights[0], two, flights[1], three, flights[2]],
        [((width, features), wide)] * 3 + [((features, width), wide)] + [((1, features), wide)] * 2,
    )
    return (
        block_out,
        grad_tokens,
        grad_gain_attn.reshape(-1),
        grad_w_query,
        grad_w_key,
        grad_w_value,
        grad_w_out,
        grad_gain_ffn.reshape(-1),
        grads_ffn[0].T,
        grads_ffn[1].T,
        grads_ffn[2],
    )


def solution(mesh):
    fine = Mesh(mesh.devices.reshape(2, 4, 2, TP), SEQ_AXES + ("tp",))
    return jax.shard_map(
        on_device,
        mesh=fine,
        in_specs=(
            P(SEQ_AXES, None),
            P(),
            P(None, "tp"),
            P(None, "tp"),
            P(None, "tp"),
            P("tp", None),
            P(),
            P(None, "tp"),
            P(None, "tp"),
            P("tp", None),
            P(SEQ_AXES, None),
        ),
        out_specs=(
            P(SEQ_AXES, None),
            P(SEQ_AXES, None),
            P("tp"),
            P(None, "tp"),
            P(None, "tp"),
            P(None, "tp"),
            P("tp", None),
            P("tp"),
            P(None, "tp"),
            P(None, "tp"),
            P("tp", None),
        ),
        check_vma=False,
    )
```

```python
import jax
import jax.numpy as jnp
from jax import lax
from jax.experimental import pallas as pl
from jax.experimental.pallas import tpu as pltpu
from jax.sharding import Mesh
from jax.sharding import PartitionSpec as P

HD = 128
W = 1024
SEQ = 16
TP = 8
Z_FLIPS = (2, 1, 3)
FFN_PIECES = (
    ((0, 0, 688), (1, 0, 128)),
    ((1, 128, 688), (2, 0, 256)),
    ((2, 256, 688),),
)
FFN_ROWS = (816, 816, 432)

epsilon = 1e-06
masked_value = -1e30
low = jnp.bfloat16
wide = jnp.float32


def seq_pairs(step):
    pairs = []
    for x_hi in range(2):
        for y in range(4):
            for core in range(2):
                to = step(x_hi, y, core)
                if to is not None:
                    pairs.append((x_hi * 8 + y * 2 + core, to[0] * 8 + to[1] * 2 + to[2]))
    return pairs


EXCHANGE = {
    "core": seq_pairs(lambda x, y, c: (x, y, 1 - c)),
    "y1": seq_pairs(lambda x, y, c: (x, y ^ 1, c)),
    "y3": seq_pairs(lambda x, y, c: (x, y ^ 3, c)),
    "x": seq_pairs(lambda x, y, c: (1 - x, y, c)),
}

SEQ_AXES = ("x_hi", "y", "core")


def by_seq(value, name):
    return lax.ppermute(value, SEQ_AXES, EXCHANGE[name])


def by_tp(value, flip):
    return lax.ppermute(value, "tp", [(k, k ^ flip) for k in range(TP)])


def shifted(value, steps):
    pairs = [(k, k + steps) for k in range(SEQ) if 0 <= k + steps < SEQ]
    return lax.ppermute(value, SEQ_AXES, pairs)


def z_exchange(blocks):
    return [by_tp(block, 2 * flip) for flip, block in zip(Z_FLIPS, blocks)]


def z_spread(block):
    return [by_tp(block, 2 * flip) for flip in Z_FLIPS]


def places():
    x_hi = lax.axis_index("x_hi")
    y = lax.axis_index("y")
    core = lax.axis_index("core")
    tp = lax.axis_index("tp")
    return {
        "seq": x_hi * 8 + y * 2 + core,
        "tp": tp,
        "z": tp >> 1,
        "x_low": tp & 1,
        "core": core,
        "y1": (y & 1) ^ (y >> 1),
        "y3": y >> 1,
        "x": x_hi,
    }


class Order:
    def __init__(self):
        self.last = None

    def __call__(self, body, ins, outs, needs=(), scratch=(), temporary=2 << 20, cost=0.3):
        ins = list(ins)
        needs = list(needs)
        if self.last is not None and not any(value is self.last for value in ins):
            needs.append(self.last)
        skip = len(ins) + len(needs)
        out_shape = [jax.ShapeDtypeStruct(shape, kind) for shape, kind in outs]
        count = len(ins)

        def run(*refs):
            body(refs[:count], refs[skip : skip + len(outs)], refs[skip + len(outs) :])

        def size(shape, kind):
            lanes = -(-shape[-1] // 128) * 128
            total = lanes * jnp.dtype(kind).itemsize
            for extent in shape[:-1]:
                total *= max(extent, 1)
            return total

        held = (
            sum(size(value.shape, value.dtype) for value in ins)
            + sum(size(shape, kind) for shape, kind in outs)
            + sum(size(shape, kind) for shape, kind in scratch)
        )
        result = pl.pallas_call(
            run,
            out_shape=out_shape,
            in_specs=[pl.BlockSpec(memory_space=pltpu.VMEM)] * count
            + [pl.BlockSpec(memory_space=pl.ANY)] * len(needs),
            out_specs=[pl.BlockSpec(memory_space=pltpu.VMEM)] * len(outs),
            scratch_shapes=[pltpu.VMEM(shape, kind) for shape, kind in scratch],
            compiler_params=pltpu.CompilerParams(vmem_limit_bytes=held + temporary),
            cost_estimate=pl.CostEstimate(
                flops=int(cost * 1e9), bytes_accessed=0, transcendentals=0
            ),
            name=body.__name__,
        )(*ins, *needs)
        self.last = min(result, key=lambda value: value.size * value.dtype.itemsize)
        return result


def hold(order, values, needs=()):
    values = list(values)
    needs = list(needs) + [order.last]

    def run(*refs):
        pass

    return pl.pallas_call(
        run,
        out_shape=[jax.ShapeDtypeStruct(value.shape, value.dtype) for value in values],
        in_specs=[pl.BlockSpec(memory_space=pl.ANY)] * (len(values) + len(needs)),
        out_specs=[pl.BlockSpec(memory_space=pl.ANY)] * len(values),
        input_output_aliases={k: k for k in range(len(values))},
        compiler_params=pltpu.CompilerParams(vmem_limit_bytes=1 << 20),
        cost_estimate=pl.CostEstimate(flops=0, bytes_accessed=0, transcendentals=0),
    )(*values, *needs)


def dot(left, right):
    return jnp.dot(left, right, preferred_element_type=wide)


def dot_rows(left, right):
    return lax.dot_general(left, right, (((1,), (1,)), ((), ())), preferred_element_type=wide)


def dot_cols(left, right):
    return lax.dot_general(left, right, (((0,), (0,)), ((), ())), preferred_element_type=wide)


def rms_factor(rows):
    return lax.rsqrt(jnp.mean(rows * rows, axis=-1, keepdims=True) + epsilon)


def norm_back(grad_normed, unit_rows, factor, gain_vec):
    scaled = grad_normed * gain_vec
    return factor * (scaled - unit_rows * jnp.mean(scaled * unit_rows, axis=-1, keepdims=True))


def span(index, size):
    return pl.ds(pl.multiple_of(index * size, size), size)


def write_blocks(partial, z, outs):
    size = outs[0].shape[0]
    for flip, out in zip((0,) + Z_FLIPS, outs):
        out[...] = partial[span(z ^ flip, size), :]


def read_blocks(whole, z, blocks, first=0, width=None):
    size = blocks[0].shape[0]
    for flip, block in zip((0,) + Z_FLIPS, blocks):
        value = block[...] if width is None else block[:, first : first + width]
        whole[span(z ^ flip, size), :] = value.astype(whole.dtype)


def normed_kernel(ins, outs, _):
    tokens, gain, w_key, w_value = ins
    normed, key_value = outs
    inputs = tokens[...].astype(wide)
    rows = (inputs * rms_factor(inputs) * gain[...]).astype(low)
    normed[...] = rows
    features = w_key.shape[1]
    key_value[:, :features] = dot(rows, w_key[...]).astype(low)
    key_value[:, features:] = dot(rows, w_value[...]).astype(low)


def project_kernel(ins, outs, _):
    outs[0][...] = dot(ins[0][...], ins[1][...]).astype(low)


def last_block(at, own_of_partner, four_of_partner, way):
    near = at["core"] == (0 if way == 1 else 1)
    return jnp.where(near, four_of_partner, own_of_partner)


def seen_scores(scores, order, distance, gap, inside):
    if order == 0:
        return jnp.where(gap >= 0, scores, masked_value)
    if order == 3:
        return jnp.where((gap < 0) & inside, scores, masked_value)
    return jnp.where(inside, scores, masked_value)


def distances(at, way):
    near = at["core"] == (0 if way == 1 else 1)
    return [0, 2, jnp.where(near, 1, 3), 4, jnp.where(near, 3, 1)]


def gap_of(rows, flipped=False):
    first = lax.broadcasted_iota(jnp.int32, (rows, rows), 0)
    second = lax.broadcasted_iota(jnp.int32, (rows, rows), 1)
    return second - first if flipped else first - second


def attend_kernel(ins, outs, scratch):
    query, own, two, across, four, partner_own, partner_four, w_out = ins
    side, log_out = outs[:2]
    rows, features = query.shape
    at = places()
    scale = HD ** (-0.5)
    gap = gap_of(rows)
    away = distances(at, 1)
    blocks = [own[...], two[...], across[...], four[...]]
    blocks.append(last_block(at, partner_own[...], partner_four[...], 1))
    logs = []
    mixed = []
    for head in range(features // HD):
        here = slice(head * HD, (head + 1) * HD)
        there = slice(features + head * HD, features + (head + 1) * HD)
        scores = [
            seen_scores(
                dot_rows(query[:, here], block[:, here]) * scale,
                order,
                distance,
                gap,
                at["seq"] >= distance,
            )
            for order, (block, distance) in enumerate(zip(blocks, away))
        ]
        peak = scores[0].max(axis=-1, keepdims=True)
        for part in scores[1:]:
            peak = jnp.maximum(peak, part.max(axis=-1, keepdims=True))
        raised = [jnp.exp(part - peak) for part in scores]
        total = raised[0].sum(axis=-1, keepdims=True)
        for part in raised[1:]:
            total = total + part.sum(axis=-1, keepdims=True)
        inverse = 1.0 / total
        out = dot((raised[0] * inverse).astype(low), blocks[0][:, there])
        for part, block in zip(raised[1:], blocks[1:]):
            out = out + dot((part * inverse).astype(low), block[:, there])
        mixed.append(out.astype(low))
        logs.append(peak + jnp.log(total))
    lane = lax.broadcasted_iota(jnp.int32, (rows, HD), 1)
    both = jnp.where((lane & 32) == 0, logs[0], logs[1])
    first = both.astype(low).astype(wide)
    side[:, :features] = query[...]
    for head, out in enumerate(mixed):
        side[:, features + head * HD : features + (head + 1) * HD] = out
    side[:, 2 * features :] = jnp.where(lane < 64, first, both - first).astype(low)
    log_out[...] = jnp.where(lane < 64, logs[0], logs[1])
    partial = scratch[0]
    partial[...] = dot(side[:, features : 2 * features], w_out[...]).astype(low)
    write_blocks(partial, at["z"], outs[2:])


def sum_z_kernel(ins, outs, _):
    keep, send = outs
    at = places()
    size, width = keep.shape[0], ins[0].shape[1]
    for group in range(len(ins) // 4):
        blocks = ins[4 * group : 4 * group + 4]
        here = slice(group * width, (group + 1) * width)
        for out, index in ((keep, at["x_low"]), (send, 1 - at["x_low"])):
            total = blocks[0][span(index, size), :].astype(wide)
            for block in blocks[1:]:
                total = total + block[span(index, size), :].astype(wide)
            out[:, here] = total.astype(out.dtype)


def norm_rows_kernel(ins, outs, _):
    keep, arrived, tokens, gain = ins
    hidden, normed = outs
    at = places()
    rows = tokens[span(at["tp"], keep.shape[0]), :].astype(wide) + (
        keep[...] + arrived[...].astype(wide)
    )
    hidden[...] = rows
    normed[...] = (rows * rms_factor(rows) * gain[...]).astype(low)


def pair_kernel(ins, outs, _):
    at = places()
    size = ins[0].shape[0]
    outs[0][span(at["x_low"], size), :] = ins[0][...]
    outs[0][span(1 - at["x_low"], size), :] = ins[1][...]


def ffn_kernel(ins, outs, scratch):
    pair, block_two, block_one, block_three, w_gate, w_up, w_down, cotangent = ins
    normed, activated, grad_gate, grad_up = outs[:4]
    at = places()
    read_blocks(normed, at["z"], (pair, block_two, block_one, block_three))
    rows = normed[...]
    gate_pre = dot_rows(rows, w_gate[...])
    up_pre = dot_rows(rows, w_up[...])
    grad_act = dot_rows(cotangent[...], w_down[...])
    sigmoid = jax.nn.sigmoid(gate_pre)
    silu = gate_pre * sigmoid
    activated[...] = (silu * up_pre).astype(low)
    grad_gate[...] = (grad_act * up_pre * sigmoid * (1.0 + gate_pre * (1.0 - sigmoid))).astype(low)
    grad_up[...] = (grad_act * silu).astype(low)
    partial = scratch[0]
    partial[...] = (dot(grad_gate[...], w_gate[...]) + dot(grad_up[...], w_up[...])).astype(low)
    write_blocks(partial, at["z"], outs[4:])


def grad_rows_kernel(ins, outs, _):
    keep, arrived, hidden, cotangent, gain = ins
    grad_hidden, grad_low, gain_part = outs
    at = places()
    grad_normed = keep[...] + arrived[...].astype(wide)
    rows = hidden[...]
    factor = rms_factor(rows)
    unit = rows * factor
    gain_part[...] = jnp.sum(grad_normed * unit, axis=0, keepdims=True)
    grad = cotangent[span(at["tp"], keep.shape[0]), :].astype(wide) + norm_back(
        grad_normed, unit, factor, gain[...]
    )
    grad_hidden[...] = grad
    grad_low[...] = grad.astype(low)


def heads_kernel(ins, outs, _):
    grad_hidden, grad_heads = outs
    read_blocks(grad_hidden, places()["z"], ins[:4])
    grad_heads[...] = dot_rows(grad_hidden[...], ins[4][...]).astype(low)


def grad_query_kernel(ins, outs, _):
    side, logs, grad_heads, own, two, across, four, partner_own, partner_four = ins
    rows, features = grad_heads.shape
    at = places()
    scale = HD ** (-0.5)
    gap = gap_of(rows)
    away = distances(at, 1)
    blocks = [own[...], two[...], across[...], four[...]]
    blocks.append(last_block(at, partner_own[...], partner_four[...], 1))
    for head in range(features // HD):
        here = slice(head * HD, (head + 1) * HD)
        there = slice(features + head * HD, features + (head + 1) * HD)
        query = side[:, here]
        grad = grad_heads[:, here]
        log_total = logs[:, head * 64 : head * 64 + 1]
        inner = jnp.sum(
            grad.astype(wide) * side[:, there].astype(wide), axis=-1, keepdims=True
        )
        total = jnp.zeros((rows, HD), wide)
        for order, (block, distance) in enumerate(zip(blocks, away)):
            scores = seen_scores(
                dot_rows(query, block[:, here]) * scale,
                order,
                distance,
                gap,
                at["seq"] >= distance,
            )
            weights = jnp.exp(scores - log_total)
            grad_scores = weights * (dot_rows(grad, block[:, there]) - inner)
            total = total + dot(grad_scores.astype(low), block[:, here])
        outs[0][:, here] = (total * scale).astype(low)


def grad_key_kernel(ins, outs, scratch):
    key_value = ins[0]
    sides = ins[1:7]
    grads = ins[7:13]
    grad_query, w_query, w_key, w_value, tokens, gain_ffn_part, ffn_partial = ins[13:]
    grad_key, grad_value, keep_one, keep_two, send_one, send_two = outs
    rows, features = grad_query.shape
    at = places()
    scale = HD ** (-0.5)
    gap = gap_of(rows, flipped=True)
    away = distances(at, -1)
    side_blocks = [side[...] for side in sides[:4]]
    side_blocks.append(last_block(at, sides[4][...], sides[5][...], -1))
    grad_blocks = [grad[...] for grad in grads[:4]]
    grad_blocks.append(last_block(at, grads[4][...], grads[5][...], -1))
    log_rows = [side[:, 2 * features :].astype(wide).T for side in side_blocks]
    for head in range(features // HD):
        here = slice(head * HD, (head + 1) * HD)
        there = slice(features + head * HD, features + (head + 1) * HD)
        key = key_value[:, here]
        value = key_value[:, there]
        total_key = jnp.zeros((rows, HD), wide)
        total_value = jnp.zeros((rows, HD), wide)
        for order, (side, grad_all, logs, distance) in enumerate(
            zip(side_blocks, grad_blocks, log_rows, away)
        ):
            query = side[:, here]
            grad = grad_all[:, here]
            log_total = logs[head * 32 : head * 32 + 1] + logs[64 + head * 32 : 65 + head * 32]
            inner = jnp.sum(
                (grad.astype(wide) * side[:, there].astype(wide)).T, axis=0, keepdims=True
            )
            scores = seen_scores(
                dot_rows(key, query) * scale, order, distance, gap, at["seq"] + distance < SEQ
            )
            weights = jnp.exp(scores - log_total)
            total_value = total_value + dot(weights.astype(low), grad)
            grad_scores = weights * (dot_rows(value, grad) - inner)
            total_key = total_key + dot(grad_scores.astype(low), query)
        grad_key[:, here] = (total_key * scale).astype(low)
        grad_value[:, here] = total_value.astype(low)
    back = (
        dot_rows(grad_query[...], w_query[...])
        + dot_rows(grad_key[...], w_key[...])
        + dot_rows(grad_value[...], w_value[...])
    )
    inputs = tokens[...].astype(wide)
    gain_attn_part = jnp.sum(back * (inputs * rms_factor(inputs)), axis=0, keepdims=True)
    partial = scratch[0]
    width = tokens.shape[1]
    partial[:, :width] = back.astype(low)
    share = rows // TP
    cells = width // TP // HD
    for k in range(TP):
        parts = [
            gain[:, (k * cells + cell) * HD : (k * cells + cell + 1) * HD]
            for gain in (gain_attn_part, gain_ffn_part[...])
            for cell in range(cells)
        ]
        parts.append(jnp.zeros((share - len(parts), HD), wide))
        partial[k * share : (k + 1) * share, width:] = jnp.concatenate(parts, axis=0).astype(low)
    size = rows // 4
    z = at["z"]
    cut = width // 2
    for out, first, flips in (
        (keep_one, 0, (0, 3)),
        (send_one, 0, (1, 2)),
        (keep_two, cut, (0, 1)),
        (send_two, cut, (3, 2)),
    ):
        for k, flip in enumerate(flips):
            here = slice(k * size, (k + 1) * size)
            there = span(z ^ flip, size)
            out[here, :cut] = partial[there, first : first + cut]
            out[here, cut:width] = ffn_partial[there, first : first + cut]
            if first > 0:
                out[here, width:] = partial[there, width:]


def sum_middle_kernel(ins, outs, _):
    for keep, arrived, stay, send in ((ins[0], ins[1], outs[0], outs[1]), (ins[2], ins[3], outs[2], outs[3])):
        size = stay.shape[0]
        stay[...] = keep[:size, :].astype(wide) + arrived[:size, :].astype(wide)
        send[...] = (keep[size:, :].astype(wide) + arrived[size:, :].astype(wide)).astype(low)


def sum_last_kernel(ins, outs, _):
    keep, send = outs
    at = places()
    size = keep.shape[0]
    width = ins[0].shape[1]
    cut = width // 2
    for out, index in ((keep, at["x_low"]), (send, 1 - at["x_low"])):
        here = span(index, size)
        first = (ins[0][here, :] + ins[1][here, :].astype(wide)).astype(out.dtype)
        second = (ins[2][here, :] + ins[3][here, :].astype(wide)).astype(out.dtype)
        out[:, :cut] = first[:, :cut]
        out[:, cut:width] = second[:, :cut]
        out[:, width : width + cut] = first[:, cut:]
        out[:, width + cut : 2 * width] = second[:, cut:width]
        out[:, 2 * width :] = second[:, width:]


def last_rows_kernel(ins, outs, _):
    keep, arrived, grad_hidden, hidden, tokens, gain = ins
    rows_out, gains = outs
    width = hidden.shape[1]
    at = places()
    inputs = tokens[span(at["tp"], keep.shape[0]), :].astype(wide)
    factor = rms_factor(inputs)
    grad_normed = keep[:, :width] + arrived[:, :width].astype(wide)
    grad = grad_hidden[...] + norm_back(grad_normed, inputs * factor, factor, gain[...])
    rows_out[:, :width] = grad.astype(low)
    rows_out[:, width:] = (
        hidden[...] + keep[:, width : 2 * width] + arrived[:, width : 2 * width].astype(wide)
    ).astype(low)
    sums = keep[:, 2 * width :] + arrived[:, 2 * width :].astype(wide)
    gains[...] = jnp.zeros_like(gains)
    gains[:, : sums.shape[1]] = sums[: gains.shape[0], :].astype(low)


def last_pair_kernel(ins, outs, _):
    at = places()
    size = ins[0].shape[0]
    width = outs[0].shape[1]
    for value, index in zip(ins, (at["x_low"], 1 - at["x_low"])):
        outs[0][span(index, size), :] = value[:, :width]
        outs[1][span(index, size), :] = value[:, width:]


def stack_kernel(ins, outs, _):
    for k, out in enumerate(outs):
        size = ins[2 * k].shape[0]
        out[:size, :] = ins[2 * k][...]
        out[size:, :] = ins[2 * k + 1][...]


def token_outputs_kernel(ins, outs, _):
    outs[2][...] = jnp.zeros_like(outs[2])
    z = places()["z"]
    size = ins[0].shape[0] // 2
    for out, own, arrived, flips in (
        (outs[0], ins[0], ins[1], (0, 1, 3, 2)),
        (outs[1], ins[2], ins[3], (0, 3, 1, 2)),
    ):
        blocks = (own[:size, :], own[size:, :], arrived[:size, :], arrived[size:, :])
        for flip, block in zip(flips, blocks):
            out[span(z ^ flip, size), :] = block.astype(out.dtype)


def part(ref, axis, start, size):
    return ref[:, pl.ds(start, size)] if axis == 1 else ref[pl.ds(start, size), :]


def put(ref, axis, start, size, value):
    if axis == 1:
        ref[:, pl.ds(start, size)] = value
    else:
        ref[pl.ds(start, size), :] = value


def split_op(keep, arrived, bit, axis):
    shape = list(keep.shape)
    shape[axis] //= 2
    size = shape[axis]

    def body(at, ins, outs):
        for out, index in zip(outs, (at[bit], 1 - at[bit])):
            start = pl.multiple_of(index * size, size)
            out[...] = (
                part(ins[0], axis, start, size).astype(wide)
                + part(ins[1], axis, start, size).astype(wide)
            ).astype(low)

    return body, [keep, arrived], [(tuple(shape), low)] * 2


def add_op(keep, arrived):
    def body(at, ins, outs):
        outs[0][...] = (ins[0][...].astype(wide) + ins[1][...].astype(wide)).astype(
            outs[0].dtype
        )

    return body, [keep, arrived], [(keep.shape, keep.dtype)]


def join_op(own, arrived, bit, axis, kind=low):
    shape = list(own.shape)
    size = shape[axis]
    shape[axis] *= 2

    def body(at, ins, outs):
        for value, index in zip(ins, (at[bit], 1 - at[bit])):
            start = pl.multiple_of(index * size, size)
            put(outs[0], axis, start, size, value[...].astype(kind))

    return body, [own, arrived], [(tuple(shape), kind)]


def add_tail_op(keep, arrived, tail):
    rows, width = keep.shape

    def body(at, ins, outs):
        outs[0][:rows, :] = (ins[0][...].astype(wide) + ins[1][...].astype(wide)).astype(low)
        outs[0][rows:, :] = ins[2][...]

    return body, [keep, arrived, tail], [((rows + tail.shape[0], width), low)]


def join_tail_op(own, arrived, bit, tail):
    rows, width = own.shape
    size = rows - tail

    def body(at, ins, outs):
        for value, index in zip(ins, (at[bit], 1 - at[bit])):
            outs[0][span(index, size), :] = value[:size, :]
        outs[0][2 * size :, :] = (
            ins[0][size:, :].astype(wide) + ins[1][size:, :].astype(wide)
        ).astype(low)

    return body, [own, arrived], [((2 * size + tail, width), low)]


def run_ops(order, ops, needs=()):
    ins = [value for _, values, _ in ops for value in values]
    outs = [out for _, _, shapes in ops for out in shapes]

    def body(in_refs, out_refs, _):
        at = places()
        first = last = 0
        for step, values, shapes in ops:
            step(
                at,
                in_refs[first : first + len(values)],
                out_refs[last : last + len(shapes)],
            )
            first += len(values)
            last += len(shapes)

    flat = list(order(body, ins, outs, needs))
    result = []
    for _, _, shapes in ops:
        result.append(flat[: len(shapes)])
        flat = flat[len(shapes) :]
    return result


FFN_ORDERS = (("y1", "y3", "x"), ("y3", "x", "y1"), ("x", "y1", "y3"))


def ffn_terms(ins, k):
    terms = []
    first = 0
    for operand, start, stop in FFN_PIECES[k]:
        last = first + stop - start
        terms.append((first, last, ins[operand][:, start:stop], ins[4 if operand == 2 else 3]))
        first = last
    return terms


def ffn_send_kernel(arrays):
    def ffn_send(ins, outs, _):
        out = outs[0]
        half = out.shape[1]
        other = 1 - places()["core"]
        base = 0
        for k in arrays:
            for first, last, left, right in ffn_terms(ins, k):
                out[base + first : base + last, :] = dot_cols(
                    left, right[:, span(other, half)]
                ).astype(low)
            base += FFN_ROWS[k]

    return ffn_send


def ffn_keep_kernel(arrays):
    def ffn_keep(ins, outs, _):
        at = places()
        arrived = ins[5]
        base = 0
        for k, keep, send in zip(arrays, outs[0::2], outs[1::2]):
            size = keep.shape[1]
            bit = at[FFN_ORDERS[k][0]]
            for out, index in ((keep, bit), (send, 1 - bit)):
                start = pl.multiple_of((2 * at["core"] + index) * size, size)
                for first, last, left, right in ffn_terms(ins, k):
                    own = dot_cols(left, right[:, pl.ds(start, size)])
                    got = arrived[base + first : base + last, span(index, size)]
                    out[first:last, :] = (own + got.astype(wide)).astype(low)
            base += FFN_ROWS[k]

    return ffn_keep


def attn_terms(ins):
    normed, grad_hidden, grad_query, grad_key, grad_value, heads_out = ins
    half = heads_out.shape[1] // 2
    return [
        [(normed, grad_query[...]), (grad_hidden, heads_out[:, :half])],
        [(normed, grad_key[...]), (grad_hidden, heads_out[:, half:])],
        [(normed, grad_value[...])],
    ]


def attn_send_kernel(ins, outs, _):
    out = outs[0]
    half = out.shape[0]
    other = 1 - places()["core"]
    first = 0
    for terms in attn_terms(ins):
        for left, right in terms:
            last = first + right.shape[1]
            out[:, first:last] = dot_cols(left[:, span(other, half)], right).astype(low)
            first = last


ATTN_ORDERS = (("y1", "y3", "x"), ("y3", "x", "y1"), ("x", "y1", "y3"))


def packed_rows(rows, lanes, width):
    across = width // 128
    full, rest = divmod(lanes // 128, across)
    if rest == 1 and rows % across == 0:
        return rows * full + rows // across
    return rows * (full + (rest > 0))


def place_cells(rows, lanes, width):
    across = width // 128
    cells = lanes // 128
    runs = []
    full = cells // across
    for k in range(full * across):
        runs.append((0, k * 128, (k // across) * rows, (k % across) * 128, rows))
    rest = cells - full * across
    if rest and rows % across == 0 and rest == 1:
        size = rows // across
        for k in range(across):
            runs.append((k * size, full * across * 128, full * rows, k * 128, size))
    elif rest:
        for k in range(rest):
            runs.append((0, (full * across + k) * 128, full * rows, k * 128, rows))
    return runs


def pack(message, base, value):
    rows, lanes = value.shape
    for row, lane, to_row, to_lane, size in place_cells(rows, lanes, message.shape[1]):
        message[base + to_row : base + to_row + size, to_lane : to_lane + 128] = value[
            row : row + size, lane : lane + 128
        ]


def add_packed(keep, message, base, lanes):
    rows = keep.shape[0]
    columns = [[] for _ in range(lanes // 128)]
    for row, lane, from_row, from_lane, size in place_cells(rows, lanes, message.shape[1]):
        here = keep[row : row + size, lane : lane + 128].astype(wide)
        there = message[base + from_row : base + from_row + size, from_lane : from_lane + 128]
        columns[lane // 128].append(here + there.astype(wide))
    return [jnp.concatenate(parts, axis=0) if len(parts) > 1 else parts[0] for parts in columns]


ATTN_ORDERS = (("y1", "y3", "x"), ("y3", "x", "y1"), ("x", "y1", "y3"))
WAYS = ("y1", "y3", "x")


def tops(step):
    return {orders[step]: rows for orders, rows in zip(FFN_ORDERS, FFN_ROWS)}


def round_one_kernel(ins, outs, _):
    at = places()
    operands, arrived = ins[6:12], ins[12]
    messages = dict(zip(WAYS, outs[:3]))
    for k in range(3):
        way = FFN_ORDERS[k][2]
        size = outs[6 + k].shape[1]
        for out, index in ((outs[6 + k], at[way]), (messages[way], 1 - at[way])):
            start = pl.multiple_of(index * size, size)
            out[: FFN_ROWS[k], :] = (
                ins[k][:, pl.ds(start, size)].astype(wide)
                + ins[3 + k][:, pl.ds(start, size)].astype(wide)
            ).astype(low)
    base = 0
    for k, terms in enumerate(attn_terms(operands)):
        keep = outs[3 + k]
        size, lanes = keep.shape
        way = ATTN_ORDERS[k][0]
        for kept, index in ((True, at[way]), (False, 1 - at[way])):
            start = pl.multiple_of((2 * at["core"] + index) * size, size)
            first = 0
            for left, right in terms:
                last = first + right.shape[1]
                value = dot_cols(left[:, pl.ds(start, size)], right)
                value = value + arrived[span(index, size), base + first : base + last].astype(wide)
                value = value.astype(low)
                if kept:
                    keep[:, first:last] = value
                else:
                    for lane in range(first, last, 128):
                        row = tops(2)[way] + lane // 128 * size
                        messages[way][row : row + size, :] = value[
                            :, lane - first : lane - first + 128
                        ]
                first = last
        base += lanes


def attn_step(at, keeps, arrived, top, step, outs, messages, message_top):
    for k, (keep, out) in enumerate(zip(keeps, outs)):
        came, way = ATTN_ORDERS[k][step - 1], ATTN_ORDERS[k][step]
        columns = add_packed(keep, arrived[came], top[came], keep.shape[1])
        size = keep.shape[0] // 2
        first = at[way] == 0
        go = []
        for lane, column in enumerate(columns):
            one, two = column[:size, :], column[size:, :]
            out[:, lane * 128 : (lane + 1) * 128] = jnp.where(first, one, two).astype(low)
            go.append(jnp.where(first, two, one).astype(low))
        pack(messages[way], message_top[way], jnp.concatenate(go, axis=1))


def ffn_joined(at, sent, arrived, step, messages):
    for k, rows in enumerate(FFN_ROWS):
        back = FFN_ORDERS[k][step]
        message = messages[FFN_ORDERS[k][step - 1]]
        width = sent[back].shape[1]
        for value, index in ((sent[back], at[back]), (arrived[back], 1 - at[back])):
            start = pl.multiple_of(index * width, width)
            message[:rows, pl.ds(start, width)] = value[:rows, :]


def round_two_kernel(ins, outs, _):
    at = places()
    arrived, messages = dict(zip(WAYS, ins[:3])), dict(zip(WAYS, outs[:3]))
    for k, rows in enumerate(FFN_ROWS):
        way = FFN_ORDERS[k][2]
        messages[way][:rows, :] = (
            ins[3 + k][...].astype(wide) + arrived[way][:rows, :].astype(wide)
        ).astype(low)
    attn_step(at, ins[6:9], arrived, tops(2), 1, outs[3:], messages, tops(2))


def round_three_kernel(ins, outs, _):
    at = places()
    sent, arrived = dict(zip(WAYS, ins[:3])), dict(zip(WAYS, ins[3:6]))
    messages = dict(zip(WAYS, outs[:3]))
    ffn_joined(at, sent, arrived, 2, messages)
    attn_step(at, ins[6:9], arrived, tops(2), 2, outs[3:], messages, tops(1))


def round_four_kernel(ins, outs, _):
    at = places()
    sent, arrived = dict(zip(WAYS, ins[:3])), dict(zip(WAYS, ins[3:6]))
    messages = dict(zip(WAYS, outs))
    ffn_joined(at, sent, arrived, 1, messages)
    for k in range(3):
        way = ATTN_ORDERS[k][2]
        keep = ins[6 + k]
        rows, lanes = keep.shape
        first = tops(0)[way]
        for lane, column in enumerate(add_packed(keep, arrived[way], tops(1)[way], lanes)):
            messages[way][first : first + rows, lane * 128 : (lane + 1) * 128] = column.astype(low)
        if k == 2:
            gains = ins[9]
            messages[way][first + rows : first + rows + gains.shape[0], :lanes] = gains[...]


def round_five_kernel(ins, outs, _):
    at = places()
    sent, arrived = dict(zip(WAYS, ins[:3])), dict(zip(WAYS, ins[3:]))
    for k, out in enumerate(outs):
        way = ATTN_ORDERS[k][2]
        first = tops(0)[way]
        lanes = out.shape[1]
        rows = 128
        for value, index in ((sent[way], at[way]), (arrived[way], 1 - at[way])):
            out[span(index, rows), :] = value[first : first + rows, :lanes]
        if k == 2:
            tail = slice(first + rows, first + rows + out.shape[0] - 2 * rows)
            out[2 * rows :, :] = (
                sent[way][tail, :lanes].astype(wide) + arrived[way][tail, :lanes].astype(wide)
            ).astype(low)


def ffn_halves_kernel(ins, outs, _):
    at = places()
    sent, arrived = dict(zip(WAYS, ins[:3])), dict(zip(WAYS, ins[3:]))
    base = 0
    for k, rows in enumerate(FFN_ROWS):
        way = FFN_ORDERS[k][0]
        width = sent[way].shape[1]
        for value, index in ((sent[way], at[way]), (arrived[way], 1 - at[way])):
            start = pl.multiple_of(index * width, width)
            outs[0][base : base + rows, pl.ds(start, width)] = value[:rows, :]
        base += rows


def attn_output_kernel(ins, outs, _):
    core = places()["core"]
    grad_query, grad_key, grad_value, grad_out, gain_attn, gain_ffn = outs
    features = grad_query.shape[1]
    half = ins[0].shape[0]
    for k in (0, 1):
        index = core if k == 0 else 1 - core
        one, two, three = ins[k], ins[2 + k], ins[4 + k]
        here = span(index, half)
        grad_query[here, :] = one[:, :features].astype(wide)
        grad_key[here, :] = two[:, :features].astype(wide)
        grad_value[here, :] = three[:half, :].astype(wide)
        grad_out[: features // 2, here] = one[:, features:].astype(wide).T
        grad_out[features // 2 :, here] = two[:, features:].astype(wide).T
    sums = ins[4][half:, :].astype(wide) + ins[5][half:, :].astype(wide)
    for k, out in enumerate((gain_attn, gain_ffn)):
        out[:, :HD] = sums[2 * k : 2 * k + 1, :HD]
        out[:, HD:] = sums[2 * k + 1 : 2 * k + 2, :HD]


def ffn_output_kernel(first):
    def ffn_output(ins, outs, _):
        outs[1][...] = jnp.zeros_like(outs[1])
        rows = outs[0].shape[0]
        half = ins[0].shape[1]
        mine = places()["core"] == 0
        one = ins[0][first : first + rows, :].astype(wide)
        two = ins[1][first : first + rows, :].astype(wide)
        outs[0][:, :half] = jnp.where(mine, one, two)
        outs[0][:, half:] = jnp.where(mine, two, one)

    return ffn_output


def on_device(
    tokens, gain_attn, w_query, w_key, w_value, w_out, gain_ffn, w_gate, w_up, w_down, cotangent
):
    rows, width = tokens.shape
    features = w_query.shape[1]
    units = w_gate.shape[1]
    share = rows // TP
    quarter = rows // 4
    order = Order()
    gain_attn = gain_attn.reshape(1, width)
    gain_ffn = gain_ffn.reshape(1, width)
    w_gate, w_up = w_gate.T, w_up.T
    blocks_out = [((quarter, width), low)] * 4
    whole = ((rows, width), low)
    small = ((rows, features), low)
    keep_and_send = [((share, width), wide), ((share, width), low)]

    normed_attn, own = order(
        normed_kernel,
        [tokens, gain_attn, w_key, w_value],
        [whole, ((rows, 2 * features), low)],
        temporary=6 << 20, cost=1.0)
    two, four = shifted(own, 2), shifted(own, 4)
    partner_own = by_seq(own, "core")
    (query,) = order(project_kernel, [normed_attn, w_query], [small])
    across = by_seq(two, "core")
    partner_four = by_seq(four, "core")
    keys = [own, two, across, four, partner_own, partner_four]
    side, logs, *blocks = order(
        attend_kernel,
        [query] + keys + [w_out],
        [((rows, 2 * features + HD), low), ((rows, HD), wide)] + blocks_out,
        scratch=[whole],
        temporary=6 << 20, cost=2.5)
    arrived = z_exchange(blocks[1:])
    keep, send = order(sum_z_kernel, [blocks[0]] + arrived, keep_and_send)
    arrived = by_tp(send, 1)

    hidden, normed_rows = order(norm_rows_kernel, [keep, arrived, tokens, gain_ffn], keep_and_send)
    arrived = by_tp(normed_rows, 1)

    (side_out,) = hold(order, [side])
    side_two, side_four = shifted(side_out, -2), shifted(side_out, -4)
    side_partner_own = by_seq(side_out, "core")

    (pair,) = order(pair_kernel, [normed_rows, arrived], [((quarter, width), low)])
    arrived = z_spread(pair)

    normed_ffn, activated, grad_gate, grad_up, *blocks = order(
        ffn_kernel,
        [pair] + arrived + [w_gate, w_up, w_down, cotangent],
        [whole] + [((rows, units), low)] * 3 + blocks_out,
        needs=[side_two, side_four],
        scratch=[whole],
        temporary=12 << 20, cost=5.0)
    side_across = by_seq(side_two, "core")
    side_partner_four = by_seq(side_four, "core")
    arrived = z_exchange(blocks[1:])
    ffn_operands = [grad_gate, grad_up, activated, normed_ffn, cotangent]
    half = width // 2
    (sent,) = order(
        ffn_send_kernel([0, 1, 2]),
        ffn_operands,
        [((3 * units, half), low)],
        needs=[side_across, side_partner_own, side_partner_four],
        temporary=6 << 20, cost=2.5)
    core_arrived = by_seq(sent, "core")
    parts = order(
        ffn_keep_kernel([0, 1, 2]),
        ffn_operands + [core_arrived],
        [((rows_k, half // 2), low) for rows_k in FFN_ROWS for _ in range(2)],
        temporary=6 << 20, cost=2.5)
    ffn_keeps = list(parts[0::2])
    ffn_flights = [by_seq(part, names[0]) for part, names in zip(parts[1:4:2], FFN_ORDERS)]

    def ffn_split(steps, needs=()):
        parts = run_ops(
            order,
            [
                split_op(ffn_keeps[k], ffn_flights[k], FFN_ORDERS[k][step], 1)
                for k, step in steps
            ],
            needs,
        )
        for (k, step), (keep, send) in zip(steps, parts):
            ffn_keeps[k] = keep
            ffn_flights[k] = by_seq(send, FFN_ORDERS[k][step])

    keep, send = order(sum_z_kernel, [blocks[0]] + arrived, keep_and_send, cost=3.0)
    arrived = by_tp(send, 1)
    grad_hidden, grad_low, gain_ffn_part = order(
        grad_rows_kernel,
        [keep, arrived, hidden, cotangent, gain_ffn],
        keep_and_send + [((1, width), wide)], cost=1.5)
    arrived = by_tp(grad_low, 1)
    (pair,) = order(pair_kernel, [grad_low, arrived], [((quarter, width), low)], cost=1.5)
    arrived = z_spread(pair)
    ffn_flights += [by_seq(value, FFN_ORDERS[2][0]) for value in hold(order, [parts[5]])]
    ffn_split([(0, 1), (1, 1)])

    grad_hidden_low, grad_heads = order(heads_kernel, [pair] + arrived + [w_out], [whole, small], cost=2.0)
    grad_two, grad_four = shifted(grad_heads, -2), shifted(grad_heads, -4)
    (grad_query,) = order(
        grad_query_kernel, [side_out, logs, grad_heads] + keys, [small], temporary=6 << 20, cost=2.0)
    (ffn_partial,) = order(project_kernel, [activated, w_down], [whole], temporary=6 << 20, cost=1.0)
    grad_two, grad_four, grad_late = hold(order, [grad_two, grad_four, grad_heads])
    grad_partner_own = by_seq(grad_late, "core")
    grad_across = by_seq(grad_two, "core")
    grad_partner_four = by_seq(grad_four, "core")
    cut = width
    grad_key, grad_value, keep_one, keep_two, send_one, send_two = order(
        grad_key_kernel,
        [own, side_out, side_two, side_across, side_four, side_partner_own, side_partner_four]
        + [grad_late, grad_two, grad_across, grad_four, grad_partner_own, grad_partner_four]
        + [grad_query, w_query, w_key, w_value, tokens, gain_ffn_part, ffn_partial],
        [small, small] + [((2 * quarter, cut), low), ((2 * quarter, cut + HD), low)] * 2,
        needs=ffn_flights,
        scratch=[((rows, width + HD), low)],
        temporary=12 << 20, cost=3.0)
    one_arrived, two_arrived = by_tp(send_one, 2), by_tp(send_two, 6)
    ffn_split([(2, 1)])

    heads_out = side_out[:, features : 2 * features]
    operands = [normed_attn, grad_hidden_low, grad_query, grad_key, grad_value, heads_out]
    (sent,) = order(
        attn_send_kernel, operands, [((width // 2, 4 * features), low)], temporary=4 << 20, cost=2.5)
    core_arrived = by_seq(sent, "core")
    widths = (features + features // 2, features + features // 2, features)

    def messages_of(width_out, size, ffn_step, attn_step_out):
        by_way = {orders[attn_step_out]: part for orders, part in zip(ATTN_ORDERS, widths)}
        top = tops(ffn_step)
        return [
            ((top[way] + packed_rows(size, by_way[way], width_out), width_out), low)
            for way in WAYS
        ]

    def kept(size):
        return [((size, part), low) for part in widths]

    def fly(messages):
        return [by_seq(message, way) for message, way in zip(messages, WAYS)]

    *parts, keep_x, keep_y, keep_z, ffn_x, ffn_y, ffn_z = order(
        round_one_kernel,
        ffn_keeps + ffn_flights + operands + [core_arrived],
        messages_of(128, 512, 2, 0) + kept(512) + [((rows_k, 128), low) for rows_k in FFN_ROWS],
        temporary=4 << 20, cost=4.0,
    )
    flights = fly(parts)

    stay_one, go_one, stay_two, go_two = order(
        sum_middle_kernel,
        [keep_one, one_arrived, keep_two, two_arrived],
        [
            ((quarter, cut), wide),
            ((quarter, cut), low),
            ((quarter, cut + HD), wide),
            ((quarter, cut + HD), low),
        ], cost=3.0)
    one_arrived, two_arrived = by_tp(go_one, 6), by_tp(go_two, 2)

    *parts, keep_x, keep_y, keep_z = order(
        round_two_kernel,
        flights + [ffn_x, ffn_y, ffn_z, keep_x, keep_y, keep_z],
        messages_of(128, 256, 2, 1) + kept(256),
    )
    flights = fly(parts)
    keep, send = order(
        sum_last_kernel,
        [stay_one, one_arrived, stay_two, two_arrived],
        [((share, 2 * width + HD), wide), ((share, 2 * width + HD), low)],
    )
    arrived = by_tp(send, 1)
    *parts, keep_x, keep_y, keep_z = order(
        round_three_kernel,
        parts + flights + [keep_x, keep_y, keep_z],
        messages_of(256, 128, 1, 2) + kept(128),
    )
    flights = fly(parts)
    last_rows, gains = order(
        last_rows_kernel,
        [keep, arrived, grad_hidden, hidden, tokens, gain_attn],
        [((share, 2 * width), low), ((16, features), low)],
    )
    arrived = by_tp(last_rows, 1)
    below = {ATTN_ORDERS[0][2]: 128, ATTN_ORDERS[1][2]: 128, ATTN_ORDERS[2][2]: 128 + 16}
    parts = order(
        round_four_kernel,
        parts + flights + [keep_x, keep_y, keep_z, gains],
        [((tops(0)[way] + below[way], 512), low) for way in WAYS],
    )
    flights = fly(parts)
    first, second = order(last_pair_kernel, [last_rows, arrived], [((quarter, width), low)] * 2)
    first_arrived, second_arrived = by_tp(first, 2), by_tp(second, 6)
    firsts, seconds = order(
        stack_kernel,
        [first, first_arrived, second, second_arrived],
        [((2 * quarter, width), low)] * 2,
    )

    one, two, three = order(
        round_five_kernel,
        list(parts) + flights,
        [((256, widths[0]), low), ((256, widths[1]), low), ((256 + 16, widths[2]), low)],
    )
    ffn_last = list(parts) + flights
    flights = [by_seq(value, orders[1]) for value, orders in zip((one, two, three), ATTN_ORDERS)]
    (ffn_half,) = order(ffn_halves_kernel, ffn_last, [((3 * units, width // 2), low)])
    ffn_arrived = by_seq(ffn_half, "core")

    def attn_join(step, needs=()):
        nonlocal one, two, three, flights
        names = [orders[step] for orders in ATTN_ORDERS]
        (one,), (two,), (three,) = run_ops(
            order,
            [
                join_op(one, flights[0], names[0], 0),
                join_op(two, flights[1], names[1], 0),
                join_tail_op(three, flights[2], names[2], gains.shape[0]),
            ],
            needs,
        )
        names = [orders[step - 1] if step > 0 else "core" for orders in ATTN_ORDERS]
        flights = [by_seq(value, name) for value, name in zip((one, two, three), names)]

    attn_join(1)
    firsts_out, seconds_out = hold(order, [firsts, seconds])
    first_arrived, second_arrived = by_tp(firsts_out, 6), by_tp(seconds_out, 2)
    token = ((8, 128), wide)
    grads_ffn = [
        order(
            ffn_output_kernel(k * units), [ffn_half, ffn_arrived], [((units, width), wide), token], cost=0.3)[0]
        for k in range(3)
    ]
    attn_join(0, [first_arrived, second_arrived])
    grad_tokens, block_out, _ = order(
        token_outputs_kernel,
        [firsts_out, first_arrived, seconds_out, second_arrived],
        [((rows, width), wide), whole, token], cost=2.0,
    )
    grad_w_query, grad_w_key, grad_w_value, grad_w_out, grad_gain_attn, grad_gain_ffn = order(
        attn_output_kernel,
        [one, flights[0], two, flights[1], three, flights[2]],
        [((width, features), wide)] * 3 + [((features, width), wide)] + [((1, features), wide)] * 2, cost=4.0)
    return (
        block_out,
        grad_tokens,
        grad_gain_attn.reshape(-1),
        grad_w_query,
        grad_w_key,
        grad_w_value,
        grad_w_out,
        grad_gain_ffn.reshape(-1),
        grads_ffn[0].T,
        grads_ffn[1].T,
        grads_ffn[2],
    )


def solution(mesh):
    fine = Mesh(mesh.devices.reshape(2, 4, 2, TP), SEQ_AXES + ("tp",))
    return jax.shard_map(
        on_device,
        mesh=fine,
        in_specs=(
            P(SEQ_AXES, None),
            P(),
            P(None, "tp"),
            P(None, "tp"),
            P(None, "tp"),
            P("tp", None),
            P(),
            P(None, "tp"),
            P(None, "tp"),
            P("tp", None),
            P(SEQ_AXES, None),
        ),
        out_specs=(
            P(SEQ_AXES, None),
            P(SEQ_AXES, None),
            P("tp"),
            P(None, "tp"),
            P(None, "tp"),
            P(None, "tp"),
            P("tp", None),
            P("tp"),
            P(None, "tp"),
            P(None, "tp"),
            P("tp", None),
        ),
        check_vma=False,
    )
```

```python
import jax
import jax.numpy as jnp
from jax import lax
from jax.experimental import pallas as pl
from jax.experimental.pallas import tpu as pltpu
from jax.sharding import Mesh
from jax.sharding import PartitionSpec as P

HD = 128
W = 1024
SEQ = 16
TP = 8
Z_FLIPS = (2, 1, 3)
FFN_PIECES = (
    ((0, 0, 688), (1, 0, 128)),
    ((1, 128, 688), (2, 0, 256)),
    ((2, 256, 688),),
)
FFN_ROWS = (816, 816, 432)

epsilon = 1e-06
masked_value = -1e30
low = jnp.bfloat16
wide = jnp.float32


def seq_pairs(step):
    pairs = []
    for x_hi in range(2):
        for y in range(4):
            for core in range(2):
                to = step(x_hi, y, core)
                if to is not None:
                    pairs.append((x_hi * 8 + y * 2 + core, to[0] * 8 + to[1] * 2 + to[2]))
    return pairs


EXCHANGE = {
    "core": seq_pairs(lambda x, y, c: (x, y, 1 - c)),
    "y1": seq_pairs(lambda x, y, c: (x, y ^ 1, c)),
    "y3": seq_pairs(lambda x, y, c: (x, y ^ 3, c)),
    "x": seq_pairs(lambda x, y, c: (1 - x, y, c)),
}

SEQ_AXES = ("x_hi", "y", "core")


def by_seq(value, name):
    return lax.ppermute(value, SEQ_AXES, EXCHANGE[name])


def by_tp(value, flip):
    return lax.ppermute(value, "tp", [(k, k ^ flip) for k in range(TP)])


def shifted(value, steps):
    pairs = [(k, k + steps) for k in range(SEQ) if 0 <= k + steps < SEQ]
    return lax.ppermute(value, SEQ_AXES, pairs)


def z_exchange(blocks):
    return [by_tp(block, 2 * flip) for flip, block in zip(Z_FLIPS, blocks)]


def z_spread(block):
    return [by_tp(block, 2 * flip) for flip in Z_FLIPS]


def gather_tp(rows):
    mine = [by_tp(rows, 2 * flip) for flip in Z_FLIPS]
    other = by_tp(rows, 1)
    theirs = [by_tp(other, 2 * flip) for flip in Z_FLIPS]
    return [rows, other] + mine + theirs


def places():
    x_hi = lax.axis_index("x_hi")
    y = lax.axis_index("y")
    core = lax.axis_index("core")
    tp = lax.axis_index("tp")
    return {
        "seq": x_hi * 8 + y * 2 + core,
        "tp": tp,
        "z": tp >> 1,
        "x_low": tp & 1,
        "core": core,
        "y1": (y & 1) ^ (y >> 1),
        "y3": y >> 1,
        "x": x_hi,
    }


class Order:
    def __init__(self):
        self.last = None

    def __call__(self, body, ins, outs, needs=(), scratch=(), temporary=2 << 20, cost=0.3):
        ins = list(ins)
        needs = list(needs)
        if self.last is not None:
            needs.append(self.last)
        skip = len(ins) + len(needs)
        outs = list(outs) + [((8, 128), wide)]
        out_shape = [jax.ShapeDtypeStruct(shape, kind) for shape, kind in outs]
        count = len(ins)

        def run(*refs):
            given = refs[skip : skip + len(outs)]
            given[-1][...] = jnp.zeros_like(given[-1])
            body(refs[:count], given[:-1], refs[skip + len(outs) :])

        def size(shape, kind):
            lanes = -(-shape[-1] // 128) * 128
            total = lanes * jnp.dtype(kind).itemsize
            for extent in shape[:-1]:
                total *= max(extent, 1)
            return total

        held = (
            sum(size(value.shape, value.dtype) for value in ins)
            + sum(size(shape, kind) for shape, kind in outs)
            + sum(size(shape, kind) for shape, kind in scratch)
        )
        result = pl.pallas_call(
            run,
            out_shape=out_shape,
            in_specs=[pl.BlockSpec(memory_space=pltpu.VMEM)] * count
            + [pl.BlockSpec(memory_space=pl.ANY)] * len(needs),
            out_specs=[pl.BlockSpec(memory_space=pltpu.VMEM)] * len(outs),
            scratch_shapes=[pltpu.VMEM(shape, kind) for shape, kind in scratch],
            compiler_params=pltpu.CompilerParams(vmem_limit_bytes=held + temporary),
            cost_estimate=pl.CostEstimate(
                flops=int(cost * 1e9), bytes_accessed=0, transcendentals=0
            ),
            name=body.__name__,
        )(*ins, *needs)
        self.last = result[-1]
        return result[:-1]


def hold(order, values, strict=False):
    values = list(values)
    needs = [order.last]
    if strict:
        values, needs = values + needs, []

    def run(*refs):
        pass

    result = pl.pallas_call(
        run,
        out_shape=[jax.ShapeDtypeStruct(value.shape, value.dtype) for value in values],
        in_specs=[pl.BlockSpec(memory_space=pl.ANY)] * (len(values) + len(needs)),
        out_specs=[pl.BlockSpec(memory_space=pl.ANY)] * len(values),
        input_output_aliases={k: k for k in range(len(values))},
        compiler_params=pltpu.CompilerParams(vmem_limit_bytes=1 << 20),
        cost_estimate=pl.CostEstimate(flops=0, bytes_accessed=0, transcendentals=0),
    )(*values, *needs)
    if strict:
        order.last = result[-1]
        result = result[:-1]
    return result


def dot(left, right):
    return jnp.dot(left, right, preferred_element_type=wide)


def dot_rows(left, right):
    return lax.dot_general(left, right, (((1,), (1,)), ((), ())), preferred_element_type=wide)


def dot_cols(left, right):
    return lax.dot_general(left, right, (((0,), (0,)), ((), ())), preferred_element_type=wide)


def rms_factor(rows):
    return lax.rsqrt(jnp.mean(rows * rows, axis=-1, keepdims=True) + epsilon)


def norm_back(grad_normed, unit_rows, factor, gain_vec):
    scaled = grad_normed * gain_vec
    return factor * (scaled - unit_rows * jnp.mean(scaled * unit_rows, axis=-1, keepdims=True))


def span(index, size):
    return pl.ds(pl.multiple_of(index * size, size), size)


def eight_blocks(at, size):
    here = [span(2 * at["z"] + x, size) for x in (at["x_low"], 1 - at["x_low"])]
    mine = [span(2 * (at["z"] ^ flip) + at["x_low"], size) for flip in Z_FLIPS]
    theirs = [span(2 * (at["z"] ^ flip) + 1 - at["x_low"], size) for flip in Z_FLIPS]
    return here + mine + theirs


def write_eight(partial, at, outs):
    for place, out in zip(eight_blocks(at, outs[0].shape[0]), outs):
        out[...] = partial[place, :]


def read_eight(whole, at, blocks):
    for place, block in zip(eight_blocks(at, blocks[0].shape[0]), blocks):
        whole[place, :] = block[...]


def read_pairs(whole, z, blocks):
    size = blocks[0].shape[0]
    for flip, block in zip((0,) + Z_FLIPS, blocks):
        whole[span(z ^ flip, size), :] = block[...]


def normed_kernel(ins, outs, _):
    tokens, gain, w_key, w_value = ins
    normed, key_value = outs
    inputs = tokens[...].astype(wide)
    rows = (inputs * rms_factor(inputs) * gain[...]).astype(low)
    normed[...] = rows
    features = w_key.shape[1]
    key_value[:, :features] = dot(rows, w_key[...]).astype(low)
    key_value[:, features:] = dot(rows, w_value[...]).astype(low)


def project_kernel(ins, outs, _):
    outs[0][...] = dot(ins[0][...], ins[1][...]).astype(low)


def last_block(at, own_of_partner, four_of_partner, way):
    near = at["core"] == (0 if way == 1 else 1)
    return jnp.where(near, four_of_partner, own_of_partner)


def seen_scores(scores, order, distance, gap, inside):
    if order == 0:
        return jnp.where(gap >= 0, scores, masked_value)
    if order == 3:
        return jnp.where((gap < 0) & inside, scores, masked_value)
    return jnp.where(inside, scores, masked_value)


def distances(at, way):
    near = at["core"] == (0 if way == 1 else 1)
    return [0, 2, jnp.where(near, 1, 3), 4, jnp.where(near, 3, 1)]


def gap_of(rows, flipped=False):
    first = lax.broadcasted_iota(jnp.int32, (rows, rows), 0)
    second = lax.broadcasted_iota(jnp.int32, (rows, rows), 1)
    return second - first if flipped else first - second


def attend_kernel(ins, outs, scratch):
    query, own, two, across, four, partner_own, partner_four, w_out = ins
    heads_out, log_out = outs[:2]
    rows, features = query.shape
    at = places()
    scale = HD ** (-0.5)
    gap = gap_of(rows)
    away = distances(at, 1)
    blocks = [own[...], two[...], across[...], four[...]]
    blocks.append(last_block(at, partner_own[...], partner_four[...], 1))
    logs = []
    mixed = []
    for head in range(features // HD):
        here = slice(head * HD, (head + 1) * HD)
        there = slice(features + head * HD, features + (head + 1) * HD)
        scores = [
            seen_scores(
                dot_rows(query[:, here], block[:, here]) * scale,
                order,
                distance,
                gap,
                at["seq"] >= distance,
            )
            for order, (block, distance) in enumerate(zip(blocks, away))
        ]
        peak = scores[0].max(axis=-1, keepdims=True)
        for part in scores[1:]:
            peak = jnp.maximum(peak, part.max(axis=-1, keepdims=True))
        raised = [jnp.exp(part - peak) for part in scores]
        total = raised[0].sum(axis=-1, keepdims=True)
        for part in raised[1:]:
            total = total + part.sum(axis=-1, keepdims=True)
        inverse = 1.0 / total
        out = dot((raised[0] * inverse).astype(low), blocks[0][:, there])
        for part, block in zip(raised[1:], blocks[1:]):
            out = out + dot((part * inverse).astype(low), block[:, there])
        mixed.append(out.astype(low))
        logs.append(peak + jnp.log(total))
    for head, out in enumerate(mixed):
        heads_out[:, head * HD : (head + 1) * HD] = out
    lane = lax.broadcasted_iota(jnp.int32, (rows, HD), 1)
    log_out[...] = jnp.where(lane < 64, logs[0], logs[1])
    partial = scratch[0]
    partial[...] = dot(heads_out[...], w_out[...]).astype(low)
    write_eight(partial, at, outs[2:])


def sum_kernel(ins, outs, _):
    total = ins[0][...].astype(wide)
    for block in ins[1:]:
        total = total + block[...].astype(wide)
    outs[0][...] = total.astype(outs[0].dtype)


def sum_refs(refs):
    total = refs[0][...].astype(wide)
    for ref in refs[1:]:
        total = total + ref[...].astype(wide)
    return total


def norm_rows_kernel(ins, outs, _):
    tokens, gain = ins[5:]
    hidden, normed = outs
    at = places()
    rows = tokens[span(at["tp"], hidden.shape[0]), :].astype(wide) + sum_refs(ins[:5])
    hidden[...] = rows
    normed[...] = (rows * rms_factor(rows) * gain[...]).astype(low)


def pair_kernel(ins, outs, _):
    at = places()
    size = ins[0].shape[0]
    outs[0][span(at["x_low"], size), :] = ins[0][...]
    outs[0][span(1 - at["x_low"], size), :] = ins[1][...]


def ffn_kernel(ins, outs, scratch):
    w_gate, w_up, w_down, cotangent = ins[8:]
    normed, activated, grad_gate, grad_up = outs[:4]
    at = places()
    read_eight(normed, at, ins[:8])
    rows = normed[...]
    gate_pre = dot_rows(rows, w_gate[...])
    up_pre = dot_rows(rows, w_up[...])
    grad_act = dot_rows(cotangent[...], w_down[...])
    sigmoid = jax.nn.sigmoid(gate_pre)
    silu = gate_pre * sigmoid
    activated[...] = (silu * up_pre).astype(low)
    grad_gate[...] = (grad_act * up_pre * sigmoid * (1.0 + gate_pre * (1.0 - sigmoid))).astype(low)
    grad_up[...] = (grad_act * silu).astype(low)
    partial = scratch[0]
    partial[...] = (dot(grad_gate[...], w_gate[...]) + dot(grad_up[...], w_up[...])).astype(low)
    write_eight(partial, at, outs[4:])


def grad_rows_kernel(ins, outs, _):
    hidden, cotangent, gain = ins[5:]
    grad_hidden, grad_low, gain_part = outs
    at = places()
    grad_normed = sum_refs(ins[:5])
    rows = hidden[...]
    factor = rms_factor(rows)
    unit = rows * factor
    gain_part[...] = jnp.sum(grad_normed * unit, axis=0, keepdims=True)
    grad = cotangent[span(at["tp"], rows.shape[0]), :].astype(wide) + norm_back(
        grad_normed, unit, factor, gain[...]
    )
    grad_hidden[...] = grad
    grad_low[...] = grad.astype(low)


def heads_kernel(ins, outs, _):
    w_out, logs, heads_out = ins[4:]
    grad_hidden, grad_heads = outs
    read_pairs(grad_hidden, places()["z"], ins[:4])
    grad = dot_rows(grad_hidden[...], w_out[...]).astype(low)
    rows, features = grad.shape
    grad_heads[:, :features] = grad
    product = grad.astype(wide) * heads_out[...].astype(wide)
    values = [logs[:, :1], logs[:, 64:65]]
    for head in range(2):
        values.append(jnp.sum(product[:, head * HD : (head + 1) * HD], axis=-1, keepdims=True))
    group = lax.broadcasted_iota(jnp.int32, (rows, HD), 1) >> 4
    both = jnp.zeros((rows, HD), wide)
    for k, value in enumerate(values):
        both = jnp.where((group & 3) == k, value, both)
    first = both.astype(low).astype(wide)
    grad_heads[:, features:] = jnp.where(group < 4, first, both - first).astype(low)


def grad_query_kernel(ins, outs, _):
    query_all, heads_out, logs, grad_heads, own, two, across, four, partner_own, partner_four = ins
    rows, features = query_all.shape
    at = places()
    scale = HD ** (-0.5)
    gap = gap_of(rows)
    away = distances(at, 1)
    blocks = [own[...], two[...], across[...], four[...]]
    blocks.append(last_block(at, partner_own[...], partner_four[...], 1))
    for head in range(features // HD):
        here = slice(head * HD, (head + 1) * HD)
        there = slice(features + head * HD, features + (head + 1) * HD)
        query = query_all[:, here]
        grad = grad_heads[:, here]
        log_total = logs[:, head * 64 : head * 64 + 1]
        inner = jnp.sum(
            grad.astype(wide) * heads_out[:, here].astype(wide), axis=-1, keepdims=True
        )
        total = jnp.zeros((rows, HD), wide)
        for order, (block, distance) in enumerate(zip(blocks, away)):
            scores = seen_scores(
                dot_rows(query, block[:, here]) * scale,
                order,
                distance,
                gap,
                at["seq"] >= distance,
            )
            weights = jnp.exp(scores - log_total)
            grad_scores = weights * (dot_rows(grad, block[:, there]) - inner)
            total = total + dot(grad_scores.astype(low), block[:, here])
        outs[0][:, here] = (total * scale).astype(low)


def grad_key_kernel(ins, outs, scratch):
    key_value = ins[0]
    sides = ins[1:7]
    grads = ins[7:13]
    grad_query, w_query, w_key, w_value, tokens, gain_ffn_part, ffn_partial = ins[13:]
    grad_key, grad_value, keep_one, keep_two, send_one, send_two = outs
    rows, features = grad_query.shape
    at = places()
    scale = HD ** (-0.5)
    gap = gap_of(rows, flipped=True)
    away = distances(at, -1)
    side_blocks = [side[...] for side in sides[:4]]
    side_blocks.append(last_block(at, sides[4][...], sides[5][...], -1))
    grad_blocks = [grad[...] for grad in grads[:4]]
    grad_blocks.append(last_block(at, grads[4][...], grads[5][...], -1))
    sums = [grad[:, features:].astype(wide).T for grad in grad_blocks]
    for head in range(features // HD):
        here = slice(head * HD, (head + 1) * HD)
        there = slice(features + head * HD, features + (head + 1) * HD)
        key = key_value[:, here]
        value = key_value[:, there]
        total_key = jnp.zeros((rows, HD), wide)
        total_value = jnp.zeros((rows, HD), wide)
        for order, (side, grad_all, logs, distance) in enumerate(
            zip(side_blocks, grad_blocks, sums, away)
        ):
            query = side[:, here]
            grad = grad_all[:, here]
            log_total, inner = [
                logs[16 * k : 16 * k + 1] + logs[64 + 16 * k : 65 + 16 * k] for k in (head, 2 + head)
            ]
            scores = seen_scores(
                dot_rows(key, query) * scale, order, distance, gap, at["seq"] + distance < SEQ
            )
            weights = jnp.exp(scores - log_total)
            total_value = total_value + dot(weights.astype(low), grad)
            grad_scores = weights * (dot_rows(value, grad) - inner)
            total_key = total_key + dot(grad_scores.astype(low), query)
        grad_key[:, here] = (total_key * scale).astype(low)
        grad_value[:, here] = total_value.astype(low)
    back = (
        dot_rows(grad_query[...], w_query[...])
        + dot_rows(grad_key[...], w_key[...])
        + dot_rows(grad_value[...], w_value[...])
    )
    inputs = tokens[...].astype(wide)
    gain_attn_part = jnp.sum(back * (inputs * rms_factor(inputs)), axis=0, keepdims=True)
    partial = scratch[0]
    width = tokens.shape[1]
    partial[:, :width] = back.astype(low)
    share = rows // TP
    cells = width // TP // HD
    for k in range(TP):
        parts = [
            gain[:, (k * cells + cell) * HD : (k * cells + cell + 1) * HD]
            for gain in (gain_attn_part, gain_ffn_part[...])
            for cell in range(cells)
        ]
        parts.append(jnp.zeros((share - len(parts), HD), wide))
        partial[k * share : (k + 1) * share, width:] = jnp.concatenate(parts, axis=0).astype(low)
    size = rows // 4
    z = at["z"]
    cut = width // 2
    for out, first, flips in (
        (keep_one, 0, (0, 3)),
        (send_one, 0, (1, 2)),
        (keep_two, cut, (0, 1)),
        (send_two, cut, (3, 2)),
    ):
        for k, flip in enumerate(flips):
            here = slice(k * size, (k + 1) * size)
            there = span(z ^ flip, size)
            out[here, :cut] = partial[there, first : first + cut]
            out[here, cut:width] = ffn_partial[there, first : first + cut]
            if first > 0:
                out[here, width:] = partial[there, width:]


def sum_middle_kernel(ins, outs, _):
    for keep, arrived, stay, send in ((ins[0], ins[1], outs[0], outs[1]), (ins[2], ins[3], outs[2], outs[3])):
        size = stay.shape[0]
        stay[...] = keep[:size, :].astype(wide) + arrived[:size, :].astype(wide)
        send[...] = (keep[size:, :].astype(wide) + arrived[size:, :].astype(wide)).astype(low)


def sum_last_kernel(ins, outs, _):
    keep, send = outs
    at = places()
    size = keep.shape[0]
    width = ins[0].shape[1]
    cut = width // 2
    for out, index in ((keep, at["x_low"]), (send, 1 - at["x_low"])):
        here = span(index, size)
        first = (ins[0][here, :] + ins[1][here, :].astype(wide)).astype(out.dtype)
        second = (ins[2][here, :] + ins[3][here, :].astype(wide)).astype(out.dtype)
        out[:, :cut] = first[:, :cut]
        out[:, cut:width] = second[:, :cut]
        out[:, width : width + cut] = first[:, cut:]
        out[:, width + cut : 2 * width] = second[:, cut:width]
        out[:, 2 * width :] = second[:, width:]


def last_rows_kernel(ins, outs, _):
    keep, arrived, grad_hidden, hidden, tokens, gain = ins
    rows_out, gains = outs
    width = hidden.shape[1]
    at = places()
    inputs = tokens[span(at["tp"], keep.shape[0]), :].astype(wide)
    factor = rms_factor(inputs)
    grad_normed = keep[:, :width] + arrived[:, :width].astype(wide)
    grad = grad_hidden[...] + norm_back(grad_normed, inputs * factor, factor, gain[...])
    rows_out[:, :width] = grad.astype(low)
    rows_out[:, width:] = (
        hidden[...] + keep[:, width : 2 * width] + arrived[:, width : 2 * width].astype(wide)
    ).astype(low)
    sums = keep[:, 2 * width :] + arrived[:, 2 * width :].astype(wide)
    gains[...] = jnp.zeros_like(gains)
    gains[:, : sums.shape[1]] = sums[: gains.shape[0], :].astype(low)


def last_pair_kernel(ins, outs, _):
    at = places()
    size = ins[0].shape[0]
    width = outs[0].shape[1]
    for value, index in zip(ins, (at["x_low"], 1 - at["x_low"])):
        outs[0][span(index, size), :] = value[:, :width]
        outs[1][span(index, size), :] = value[:, width:]


def stack_kernel(ins, outs, _):
    for k, out in enumerate(outs):
        size = ins[2 * k].shape[0]
        out[:size, :] = ins[2 * k][...]
        out[size:, :] = ins[2 * k + 1][...]


def token_outputs_kernel(ins, outs, _):
    z = places()["z"]
    size = ins[0].shape[0] // 2
    for out, own, arrived, flips in (
        (outs[0], ins[0], ins[1], (0, 1, 3, 2)),
        (outs[1], ins[2], ins[3], (0, 3, 1, 2)),
    ):
        blocks = (own[:size, :], own[size:, :], arrived[:size, :], arrived[size:, :])
        for flip, block in zip(flips, blocks):
            out[span(z ^ flip, size), :] = block.astype(out.dtype)


def part(ref, axis, start, size):
    return ref[:, pl.ds(start, size)] if axis == 1 else ref[pl.ds(start, size), :]


def put(ref, axis, start, size, value):
    if axis == 1:
        ref[:, pl.ds(start, size)] = value
    else:
        ref[pl.ds(start, size), :] = value


def split_op(keep, arrived, bit, axis):
    shape = list(keep.shape)
    shape[axis] //= 2
    size = shape[axis]

    def body(at, ins, outs):
        for out, index in zip(outs, (at[bit], 1 - at[bit])):
            start = pl.multiple_of(index * size, size)
            out[...] = (
                part(ins[0], axis, start, size).astype(wide)
                + part(ins[1], axis, start, size).astype(wide)
            ).astype(low)

    return body, [keep, arrived], [(tuple(shape), low)] * 2


def add_op(keep, arrived):
    def body(at, ins, outs):
        outs[0][...] = (ins[0][...].astype(wide) + ins[1][...].astype(wide)).astype(
            outs[0].dtype
        )

    return body, [keep, arrived], [(keep.shape, keep.dtype)]


def join_op(own, arrived, bit, axis, kind=low):
    shape = list(own.shape)
    size = shape[axis]
    shape[axis] *= 2

    def body(at, ins, outs):
        for value, index in zip(ins, (at[bit], 1 - at[bit])):
            start = pl.multiple_of(index * size, size)
            put(outs[0], axis, start, size, value[...].astype(kind))

    return body, [own, arrived], [(tuple(shape), kind)]


def add_tail_op(keep, arrived, tail):
    rows, width = keep.shape

    def body(at, ins, outs):
        outs[0][:rows, :] = (ins[0][...].astype(wide) + ins[1][...].astype(wide)).astype(low)
        outs[0][rows:, :] = ins[2][...]

    return body, [keep, arrived, tail], [((rows + tail.shape[0], width), low)]


def join_tail_op(own, arrived, bit, tail):
    rows, width = own.shape
    size = rows - tail

    def body(at, ins, outs):
        for value, index in zip(ins, (at[bit], 1 - at[bit])):
            outs[0][span(index, size), :] = value[:size, :]
        outs[0][2 * size :, :] = (
            ins[0][size:, :].astype(wide) + ins[1][size:, :].astype(wide)
        ).astype(low)

    return body, [own, arrived], [((2 * size + tail, width), low)]


def run_ops(order, ops, needs=()):
    ins = [value for _, values, _ in ops for value in values]
    outs = [out for _, _, shapes in ops for out in shapes]

    def body(in_refs, out_refs, _):
        at = places()
        first = last = 0
        for step, values, shapes in ops:
            step(
                at,
                in_refs[first : first + len(values)],
                out_refs[last : last + len(shapes)],
            )
            first += len(values)
            last += len(shapes)

    flat = list(order(body, ins, outs, needs))
    result = []
    for _, _, shapes in ops:
        result.append(flat[: len(shapes)])
        flat = flat[len(shapes) :]
    return result


FFN_ORDERS = (("y1", "y3", "x"), ("y3", "x", "y1"), ("x", "y1", "y3"))


def ffn_terms(ins, k):
    terms = []
    first = 0
    for operand, start, stop in FFN_PIECES[k]:
        last = first + stop - start
        terms.append((first, last, ins[operand][:, start:stop], ins[4 if operand == 2 else 3]))
        first = last
    return terms


def ffn_send_kernel(arrays):
    def ffn_send(ins, outs, _):
        out = outs[0]
        half = out.shape[1]
        other = 1 - places()["core"]
        base = 0
        for k in arrays:
            for first, last, left, right in ffn_terms(ins, k):
                out[base + first : base + last, :] = dot_cols(
                    left, right[:, span(other, half)]
                ).astype(low)
            base += FFN_ROWS[k]

    return ffn_send


def ffn_keep_kernel(arrays):
    def ffn_keep(ins, outs, _):
        at = places()
        arrived = ins[5]
        base = 0
        for k, keep, send in zip(arrays, outs[0::2], outs[1::2]):
            size = keep.shape[1]
            bit = at[FFN_ORDERS[k][0]]
            for out, index in ((keep, bit), (send, 1 - bit)):
                start = pl.multiple_of((2 * at["core"] + index) * size, size)
                for first, last, left, right in ffn_terms(ins, k):
                    own = dot_cols(left, right[:, pl.ds(start, size)])
                    got = arrived[base + first : base + last, span(index, size)]
                    out[first:last, :] = (own + got.astype(wide)).astype(low)
            base += FFN_ROWS[k]

    return ffn_keep


def attn_terms(ins):
    normed, grad_hidden, grad_query, grad_key, grad_value, heads_out = ins
    half = heads_out.shape[1] // 2
    return [
        [(normed, grad_query[...]), (grad_hidden, heads_out[:, :half])],
        [(normed, grad_key[...]), (grad_hidden, heads_out[:, half:])],
        [(normed, grad_value[...])],
    ]


def attn_send_kernel(ins, outs, _):
    out = outs[0]
    half = out.shape[0]
    other = 1 - places()["core"]
    first = 0
    for terms in attn_terms(ins):
        for left, right in terms:
            last = first + right.shape[1]
            out[:, first:last] = dot_cols(left[:, span(other, half)], right).astype(low)
            first = last


ATTN_ORDERS = (("y1", "y3", "x"), ("y3", "x", "y1"), ("x", "y1", "y3"))


def packed_rows(rows, lanes, width):
    across = width // 128
    full, rest = divmod(lanes // 128, across)
    if rest == 1 and rows % across == 0:
        return rows * full + rows // across
    return rows * (full + (rest > 0))


def place_cells(rows, lanes, width):
    across = width // 128
    cells = lanes // 128
    runs = []
    full = cells // across
    for k in range(full * across):
        runs.append((0, k * 128, (k // across) * rows, (k % across) * 128, rows))
    rest = cells - full * across
    if rest and rows % across == 0 and rest == 1:
        size = rows // across
        for k in range(across):
            runs.append((k * size, full * across * 128, full * rows, k * 128, size))
    elif rest:
        for k in range(rest):
            runs.append((0, (full * across + k) * 128, full * rows, k * 128, rows))
    return runs


def pack(message, base, value):
    rows, lanes = value.shape
    for row, lane, to_row, to_lane, size in place_cells(rows, lanes, message.shape[1]):
        message[base + to_row : base + to_row + size, to_lane : to_lane + 128] = value[
            row : row + size, lane : lane + 128
        ]


def add_packed(keep, message, base, lanes):
    rows = keep.shape[0]
    columns = [[] for _ in range(lanes // 128)]
    for row, lane, from_row, from_lane, size in place_cells(rows, lanes, message.shape[1]):
        here = keep[row : row + size, lane : lane + 128].astype(wide)
        there = message[base + from_row : base + from_row + size, from_lane : from_lane + 128]
        columns[lane // 128].append(here + there.astype(wide))
    return [jnp.concatenate(parts, axis=0) if len(parts) > 1 else parts[0] for parts in columns]


ATTN_ORDERS = (("y1", "y3", "x"), ("y3", "x", "y1"), ("x", "y1", "y3"))
WAYS = ("y1", "y3", "x")


def tops(step):
    return {orders[step]: rows for orders, rows in zip(FFN_ORDERS, FFN_ROWS)}


def round_one_kernel(ins, outs, _):
    at = places()
    operands, arrived = ins[6:12], ins[12]
    messages = dict(zip(WAYS, outs[:3]))
    for k in range(3):
        way = FFN_ORDERS[k][2]
        size = outs[6 + k].shape[1]
        for out, index in ((outs[6 + k], at[way]), (messages[way], 1 - at[way])):
            start = pl.multiple_of(index * size, size)
            out[: FFN_ROWS[k], :] = (
                ins[k][:, pl.ds(start, size)].astype(wide)
                + ins[3 + k][:, pl.ds(start, size)].astype(wide)
            ).astype(low)
    base = 0
    for k, terms in enumerate(attn_terms(operands)):
        keep = outs[3 + k]
        size, lanes = keep.shape
        way = ATTN_ORDERS[k][0]
        for kept, index in ((True, at[way]), (False, 1 - at[way])):
            start = pl.multiple_of((2 * at["core"] + index) * size, size)
            first = 0
            for left, right in terms:
                last = first + right.shape[1]
                value = dot_cols(left[:, pl.ds(start, size)], right)
                value = value + arrived[span(index, size), base + first : base + last].astype(wide)
                value = value.astype(low)
                if kept:
                    keep[:, first:last] = value
                else:
                    for lane in range(first, last, 128):
                        row = tops(2)[way] + lane // 128 * size
                        messages[way][row : row + size, :] = value[
                            :, lane - first : lane - first + 128
                        ]
                first = last
        base += lanes


def attn_step(at, keeps, arrived, top, step, outs, messages, message_top):
    for k, (keep, out) in enumerate(zip(keeps, outs)):
        came, way = ATTN_ORDERS[k][step - 1], ATTN_ORDERS[k][step]
        columns = add_packed(keep, arrived[came], top[came], keep.shape[1])
        size = keep.shape[0] // 2
        first = at[way] == 0
        go = []
        for lane, column in enumerate(columns):
            one, two = column[:size, :], column[size:, :]
            out[:, lane * 128 : (lane + 1) * 128] = jnp.where(first, one, two).astype(low)
            go.append(jnp.where(first, two, one).astype(low))
        pack(messages[way], message_top[way], jnp.concatenate(go, axis=1))


def ffn_joined(at, sent, arrived, step, messages):
    for k, rows in enumerate(FFN_ROWS):
        back = FFN_ORDERS[k][step]
        message = messages[FFN_ORDERS[k][step - 1]]
        width = sent[back].shape[1]
        for value, index in ((sent[back], at[back]), (arrived[back], 1 - at[back])):
            start = pl.multiple_of(index * width, width)
            message[:rows, pl.ds(start, width)] = value[:rows, :]


def round_two_kernel(ins, outs, _):
    at = places()
    arrived, messages = dict(zip(WAYS, ins[:3])), dict(zip(WAYS, outs[:3]))
    for k, rows in enumerate(FFN_ROWS):
        way = FFN_ORDERS[k][2]
        messages[way][:rows, :] = (
            ins[3 + k][...].astype(wide) + arrived[way][:rows, :].astype(wide)
        ).astype(low)
    attn_step(at, ins[6:9], arrived, tops(2), 1, outs[3:], messages, tops(2))


def round_three_kernel(ins, outs, _):
    at = places()
    sent, arrived = dict(zip(WAYS, ins[:3])), dict(zip(WAYS, ins[3:6]))
    messages = dict(zip(WAYS, outs[:3]))
    ffn_joined(at, sent, arrived, 2, messages)
    attn_step(at, ins[6:9], arrived, tops(2), 2, outs[3:], messages, tops(1))


def round_four_kernel(ins, outs, _):
    at = places()
    sent, arrived = dict(zip(WAYS, ins[:3])), dict(zip(WAYS, ins[3:6]))
    messages = dict(zip(WAYS, outs))
    ffn_joined(at, sent, arrived, 1, messages)
    for k in range(3):
        way = ATTN_ORDERS[k][2]
        keep = ins[6 + k]
        rows, lanes = keep.shape
        first = tops(0)[way]
        for lane, column in enumerate(add_packed(keep, arrived[way], tops(1)[way], lanes)):
            messages[way][first : first + rows, lane * 128 : (lane + 1) * 128] = column.astype(low)
        if k == 2:
            gains = ins[9]
            messages[way][first + rows : first + rows + gains.shape[0], :lanes] = gains[...]


def round_five_kernel(ins, outs, _):
    at = places()
    sent, arrived = dict(zip(WAYS, ins[:3])), dict(zip(WAYS, ins[3:]))
    for k, out in enumerate(outs):
        way = ATTN_ORDERS[k][2]
        first = tops(0)[way]
        lanes = out.shape[1]
        rows = 128
        for value, index in ((sent[way], at[way]), (arrived[way], 1 - at[way])):
            out[span(index, rows), :] = value[first : first + rows, :lanes]
        if k == 2:
            tail = slice(first + rows, first + rows + out.shape[0] - 2 * rows)
            out[2 * rows :, :] = (
                sent[way][tail, :lanes].astype(wide) + arrived[way][tail, :lanes].astype(wide)
            ).astype(low)


def ffn_halves_kernel(ins, outs, _):
    at = places()
    sent, arrived = dict(zip(WAYS, ins[:3])), dict(zip(WAYS, ins[3:]))
    base = 0
    for k, rows in enumerate(FFN_ROWS):
        way = FFN_ORDERS[k][0]
        width = sent[way].shape[1]
        for value, index in ((sent[way], at[way]), (arrived[way], 1 - at[way])):
            start = pl.multiple_of(index * width, width)
            outs[0][base : base + rows, pl.ds(start, width)] = value[:rows, :]
        base += rows


def write_out(order, body, ins, outs, buffers, small=(), into=None, cost=0.3):
    ins, old = list(ins), list(into or [])
    needs = [order.last]
    count, many = len(ins), len(outs)
    skip = count + len(old) + len(needs)
    small = list(small) + [((8, 128), wide)]

    def run(*refs):
        targets = refs[skip : skip + many]
        others = refs[skip + many : skip + many + len(small)]
        scratch = refs[skip + many + len(small) :]
        held, arrived = scratch[: len(buffers)], scratch[len(buffers)]
        others[-1][...] = jnp.zeros_like(others[-1])
        copies = []
        for k, (value, target) in enumerate(body(places(), refs[:count], targets, others[:-1])):
            held[k][...] = value
            copies.append(pltpu.make_async_copy(held[k], target, arrived.at[k]))
            copies[-1].start()
        for copy in copies:
            copy.wait()

    size = sum(shape[0] * shape[1] * 4 for shape in buffers) + sum(
        value.size * value.dtype.itemsize for value in ins
    )
    result = pl.pallas_call(
        run,
        out_shape=[jax.ShapeDtypeStruct(shape, wide) for shape in outs]
        + [jax.ShapeDtypeStruct(shape, kind) for shape, kind in small],
        in_specs=[pl.BlockSpec(memory_space=pltpu.VMEM)] * count
        + [pl.BlockSpec(memory_space=pltpu.HBM)] * len(old)
        + [pl.BlockSpec(memory_space=pl.ANY)] * len(needs),
        out_specs=[pl.BlockSpec(memory_space=pltpu.HBM)] * many
        + [pl.BlockSpec(memory_space=pltpu.VMEM)] * len(small),
        scratch_shapes=[pltpu.VMEM(shape, wide) for shape in buffers]
        + [pltpu.SemaphoreType.DMA((len(buffers),))],
        input_output_aliases={count + k: k for k in range(len(old))},
        compiler_params=pltpu.CompilerParams(vmem_limit_bytes=size + (6 << 20)),
        cost_estimate=pl.CostEstimate(
            flops=int(cost * 1e9), bytes_accessed=0, transcendentals=0
        ),
        name=body.__name__,
    )(*ins, *old, *needs)
    order.last = result[-1]
    return list(result[:-1])


def write_ffn(own):
    def write_ffn_half(at, ins, targets, _):
        half = ins[0].shape[1]
        index = at["core"] if own else 1 - at["core"]
        rows = targets[0].shape[0]
        for k, target in enumerate(targets):
            yield ins[0][k * rows : (k + 1) * rows, :].astype(wide), target.at[:, span(index, half)]

    return write_ffn_half


def write_attn(own):
    def write_attn_half(at, ins, targets, small):
        one, two, three = ins[:3]
        features = three.shape[1]
        half = one.shape[0]
        here = span(at["core"] if own else 1 - at["core"], half)
        yield one[:, :features].astype(wide), targets[0].at[here, :]
        yield two[:, :features].astype(wide), targets[1].at[here, :]
        yield three[:half, :].astype(wide), targets[2].at[here, :]
        halves = (one[:, features:], two[:, features:])
        out = jnp.concatenate([value.astype(wide).T for value in halves], axis=0)
        yield out, targets[3].at[:, here]
        if not own:
            sums = ins[3][half:, :].astype(wide) + three[half:, :].astype(wide)
            for k, gain in enumerate(small):
                gain[:, :HD] = sums[2 * k : 2 * k + 1, :HD]
                gain[:, HD:] = sums[2 * k + 1 : 2 * k + 2, :HD]

    return write_attn_half


def on_device(
    tokens, gain_attn, w_query, w_key, w_value, w_out, gain_ffn, w_gate, w_up, w_down, cotangent
):
    rows, width = tokens.shape
    features = w_query.shape[1]
    units = w_gate.shape[1]
    share = rows // TP
    quarter = rows // 4
    order = Order()
    gain_attn = gain_attn.reshape(1, width)
    gain_ffn = gain_ffn.reshape(1, width)
    w_gate, w_up = w_gate.T, w_up.T
    blocks_out = [((share, width), low)] * 8
    whole = ((rows, width), low)
    small = ((rows, features), low)
    keep_and_send = [((share, width), wide), ((share, width), low)]

    normed_attn, own = order(
        normed_kernel,
        [tokens, gain_attn, w_key, w_value],
        [whole, ((rows, 2 * features), low)],
        temporary=6 << 20, cost=1.0)
    two, four = shifted(own, 2), shifted(own, 4)
    partner_own = by_seq(own, "core")
    (query,) = order(project_kernel, [normed_attn, w_query], [small])
    query_two, query_four = shifted(query, -2), shifted(query, -4)
    query_partner_own = by_seq(query, "core")
    across = by_seq(two, "core")
    partner_four = by_seq(four, "core")
    keys = [own, two, across, four, partner_own, partner_four]
    heads_out, logs, *blocks = order(
        attend_kernel,
        [query] + keys + [w_out],
        [small, ((rows, HD), wide)] + blocks_out,
        scratch=[whole],
        temporary=6 << 20, cost=2.5,
    )
    theirs = z_exchange(blocks[5:])
    mine = z_exchange(blocks[2:5])
    (send,) = order(
        sum_kernel, [blocks[1]] + theirs, [((share, width), low)], needs=[query_two, query_four]
    )
    arrived = by_tp(send, 1)
    query_two, query_four = hold(order, [query_two, query_four])
    query_across = by_seq(query_two, "core")
    query_partner_four = by_seq(query_four, "core")
    hidden, normed_rows = order(
        norm_rows_kernel,
        [blocks[0]] + mine + [arrived, tokens, gain_ffn],
        keep_and_send,
        needs=[query_across, query_partner_own, query_partner_four],
    )
    gathered = gather_tp(normed_rows)

    normed_ffn, activated, grad_gate, grad_up, *blocks = order(
        ffn_kernel,
        gathered + [w_gate, w_up, w_down, cotangent],
        [whole] + [((rows, units), low)] * 3 + blocks_out,
        scratch=[whole],
        temporary=12 << 20, cost=5.0)
    theirs = z_exchange(blocks[5:])
    ffn_operands = [grad_gate, grad_up, activated, normed_ffn, cotangent]
    half = width // 2
    (sent,) = order(
        ffn_send_kernel([0, 1, 2]),
        ffn_operands,
        [((3 * units, half), low)],
        temporary=6 << 20, cost=2.5)
    core_arrived = by_seq(sent, "core")
    mine = z_exchange(hold(order, blocks[2:5]))
    parts = order(
        ffn_keep_kernel([0, 1, 2]),
        ffn_operands + [core_arrived],
        [((rows_k, half // 2), low) for rows_k in FFN_ROWS for _ in range(2)],
        temporary=6 << 20, cost=2.5)
    ffn_keeps = list(parts[0::2])
    last_part = parts[5]
    ffn_flights = [by_seq(part, names[0]) for part, names in zip(parts[1:4:2], FFN_ORDERS)]

    def ffn_split(steps, needs=()):
        parts = run_ops(
            order,
            [
                split_op(ffn_keeps[k], ffn_flights[k], FFN_ORDERS[k][step], 1)
                for k, step in steps
            ],
            needs,
        )
        for (k, step), (keep, send) in zip(steps, parts):
            ffn_keeps[k] = keep
            ffn_flights[k] = by_seq(send, FFN_ORDERS[k][step])

    (send,) = order(sum_kernel, [blocks[1]] + theirs, [((share, width), low)], cost=3.0)
    arrived = by_tp(send, 1)
    grad_hidden, grad_low, gain_ffn_part = order(
        grad_rows_kernel,
        [blocks[0]] + mine + [arrived, hidden, cotangent, gain_ffn],
        keep_and_send + [((1, width), wide)], cost=1.5)
    (pair,) = order(
        pair_kernel, [grad_low, by_tp(grad_low, 1)], [((quarter, width), low)], cost=1.5
    )
    gathered = [pair] + z_spread(pair)
    ffn_flights += [by_seq(value, FFN_ORDERS[2][0]) for value in hold(order, [last_part])]
    ffn_split([(0, 1), (1, 1)])
    grad_hidden_low, grad_heads = order(
        heads_kernel,
        gathered + [w_out, logs, heads_out],
        [whole, ((rows, features + HD), low)], cost=2.0)
    grad_two, grad_four = shifted(grad_heads, -2), shifted(grad_heads, -4)
    (grad_query,) = order(
        grad_query_kernel,
        [query, heads_out, logs, grad_heads] + keys,
        [small],
        temporary=6 << 20, cost=2.0)
    (ffn_partial,) = order(project_kernel, [activated, w_down], [whole], temporary=6 << 20, cost=1.0)
    grad_two, grad_four, grad_late = hold(order, [grad_two, grad_four, grad_heads])
    grad_partner_own = by_seq(grad_late, "core")
    grad_across = by_seq(grad_two, "core")
    grad_partner_four = by_seq(grad_four, "core")
    cut = width
    grad_key, grad_value, keep_one, keep_two, send_one, send_two = order(
        grad_key_kernel,
        [own, query, query_two, query_across, query_four, query_partner_own, query_partner_four]
        + [grad_late, grad_two, grad_across, grad_four, grad_partner_own, grad_partner_four]
        + [grad_query, w_query, w_key, w_value, tokens, gain_ffn_part, ffn_partial],
        [small, small] + [((2 * quarter, cut), low), ((2 * quarter, cut + HD), low)] * 2,
        needs=ffn_flights[2:],
        scratch=[((rows, width + HD), low)],
        temporary=12 << 20, cost=0.3)
    one_arrived, two_arrived = by_tp(send_one, 2), by_tp(send_two, 6)
    ffn_split([(2, 1)], ffn_flights[:2])

    operands = [normed_attn, grad_hidden_low, grad_query, grad_key, grad_value, heads_out]
    (sent,) = order(
        attn_send_kernel, operands, [((width // 2, 4 * features), low)], temporary=4 << 20, cost=2.5)
    core_arrived = by_seq(sent, "core")
    widths = (features + features // 2, features + features // 2, features)

    def messages_of(width_out, size, ffn_step, attn_step_out):
        by_way = {orders[attn_step_out]: part for orders, part in zip(ATTN_ORDERS, widths)}
        top = tops(ffn_step)
        return [
            ((top[way] + packed_rows(size, by_way[way], width_out), width_out), low)
            for way in WAYS
        ]

    def kept(size):
        return [((size, part), low) for part in widths]

    def fly(messages):
        return [by_seq(message, way) for message, way in zip(messages, WAYS)]

    *parts, keep_x, keep_y, keep_z, ffn_x, ffn_y, ffn_z = order(
        round_one_kernel,
        ffn_keeps + ffn_flights + operands + [core_arrived],
        messages_of(128, 512, 2, 0) + kept(512) + [((rows_k, 128), low) for rows_k in FFN_ROWS],
        temporary=4 << 20, cost=4.0,
    )
    flights = fly(parts)

    stay_one, go_one, stay_two, go_two = order(
        sum_middle_kernel,
        [keep_one, one_arrived, keep_two, two_arrived],
        [
            ((quarter, cut), wide),
            ((quarter, cut), low),
            ((quarter, cut + HD), wide),
            ((quarter, cut + HD), low),
        ], cost=3.0)
    one_arrived, two_arrived = by_tp(go_one, 6), by_tp(go_two, 2)

    keep, send = order(
        sum_last_kernel,
        [stay_one, one_arrived, stay_two, two_arrived],
        [((share, 2 * width + HD), wide), ((share, 2 * width + HD), low)],
    )
    arrived = by_tp(send, 1)
    *parts, keep_x, keep_y, keep_z = order(
        round_two_kernel,
        flights + [ffn_x, ffn_y, ffn_z, keep_x, keep_y, keep_z],
        messages_of(128, 256, 2, 1) + kept(256),
    )
    flights = fly(parts)
    *parts, keep_x, keep_y, keep_z = order(
        round_three_kernel,
        parts + flights + [keep_x, keep_y, keep_z],
        messages_of(256, 128, 1, 2) + kept(128),
    )
    flights = fly(parts)
    last_rows, gains = order(
        last_rows_kernel,
        [keep, arrived, grad_hidden, hidden, tokens, gain_attn],
        [((share, 2 * width), low), ((16, features), low)],
    )
    arrived = by_tp(last_rows, 1)
    first, second = order(last_pair_kernel, [last_rows, arrived], [((quarter, width), low)] * 2)
    first_arrived, second_arrived = by_tp(first, 2), by_tp(second, 6)
    below = {ATTN_ORDERS[0][2]: 128, ATTN_ORDERS[1][2]: 128, ATTN_ORDERS[2][2]: 128 + 16}
    parts = order(
        round_four_kernel,
        parts + flights + [keep_x, keep_y, keep_z, gains],
        [((tops(0)[way] + below[way], 512), low) for way in WAYS],
    )
    flights = fly(parts)
    firsts, seconds = order(
        stack_kernel,
        [first, first_arrived, second, second_arrived],
        [((2 * quarter, width), low)] * 2,
    )
    first_arrived, second_arrived = by_tp(firsts, 6), by_tp(seconds, 2)
    one, two, three = order(
        round_five_kernel,
        list(parts) + flights,
        [((256, widths[0]), low), ((256, widths[1]), low), ((256 + 16, widths[2]), low)],
    )
    ffn_last = list(parts) + flights
    flights = [by_seq(value, orders[1]) for value, orders in zip((one, two, three), ATTN_ORDERS)]
    (ffn_half,) = order(ffn_halves_kernel, ffn_last, [((3 * units, width // 2), low)])

    def attn_join(step, needs=()):
        nonlocal one, two, three, flights
        names = [orders[step] for orders in ATTN_ORDERS]
        (one,), (two,), (three,) = run_ops(
            order,
            [
                join_op(one, flights[0], names[0], 0),
                join_op(two, flights[1], names[1], 0),
                join_tail_op(three, flights[2], names[2], gains.shape[0]),
            ],
            needs,
        )
        names = [orders[step - 1] if step > 0 else "core" for orders in ATTN_ORDERS]
        flights = [by_seq(value, name) for value, name in zip((one, two, three), names)]

    ffn_shapes = [(units, width)] * 3
    ffn_buffers = [(units, width // 2)] * 3
    grads_ffn = write_out(order, write_ffn(True), [ffn_half], ffn_shapes, ffn_buffers)
    attn_join(1, [first_arrived, second_arrived])
    (ffn_half,) = hold(order, [ffn_half], True)
    ffn_arrived = by_seq(ffn_half, "core")
    grads_ffn = write_out(
        order, write_ffn(False), [ffn_arrived], ffn_shapes, ffn_buffers, into=grads_ffn, cost=8.0
    )
    attn_join(0)
    attn_shapes = [(width, features)] * 3 + [(features, width)]
    attn_buffers = [(width // 2, features)] * 3 + [(features, width // 2)]
    grads_attn = write_out(
        order, write_attn(True), [one, two, three], attn_shapes, attn_buffers
    )
    grad_tokens, block_out = order(
        token_outputs_kernel,
        [firsts, first_arrived, seconds, second_arrived],
        [((rows, width), wide), whole],
    )
    grad_w_query, grad_w_key, grad_w_value, grad_w_out, grad_gain_attn, grad_gain_ffn = write_out(
        order,
        write_attn(False),
        flights + [three],
        attn_shapes,
        attn_buffers,
        small=[((1, features), wide)] * 2,
        into=grads_attn,
    )
    return (
        block_out,
        grad_tokens,
        grad_gain_attn.reshape(-1),
        grad_w_query,
        grad_w_key,
        grad_w_value,
        grad_w_out,
        grad_gain_ffn.reshape(-1),
        grads_ffn[0].T,
        grads_ffn[1].T,
        grads_ffn[2],
    )


def solution(mesh):
    fine = Mesh(mesh.devices.reshape(2, 4, 2, TP), SEQ_AXES + ("tp",))
    return jax.shard_map(
        on_device,
        mesh=fine,
        in_specs=(
            P(SEQ_AXES, None),
            P(),
            P(None, "tp"),
            P(None, "tp"),
            P(None, "tp"),
            P("tp", None),
            P(),
            P(None, "tp"),
            P(None, "tp"),
            P("tp", None),
            P(SEQ_AXES, None),
        ),
        out_specs=(
            P(SEQ_AXES, None),
            P(SEQ_AXES, None),
            P("tp"),
            P(None, "tp"),
            P(None, "tp"),
            P(None, "tp"),
            P("tp", None),
            P("tp"),
            P(None, "tp"),
            P(None, "tp"),
            P("tp", None),
        ),
        check_vma=False,
    )
```

```python
import jax
import jax.numpy as jnp
from jax import lax
from jax.experimental import pallas as pl
from jax.experimental.pallas import tpu as pltpu
from jax.sharding import Mesh
from jax.sharding import PartitionSpec as P

HD = 128
W = 1024
SEQ = 16
TP = 8
Z_FLIPS = (2, 1, 3)
FFN_PIECES = (
    ((0, 0, 688), (1, 0, 128)),
    ((1, 128, 688), (2, 0, 256)),
    ((2, 256, 688),),
)
FFN_ROWS = (816, 816, 432)

epsilon = 1e-06
masked_value = -1e30
low = jnp.bfloat16
wide = jnp.float32


def seq_pairs(step):
    pairs = []
    for x_hi in range(2):
        for y in range(4):
            for core in range(2):
                to = step(x_hi, y, core)
                if to is not None:
                    pairs.append((x_hi * 8 + y * 2 + core, to[0] * 8 + to[1] * 2 + to[2]))
    return pairs


EXCHANGE = {
    "core": seq_pairs(lambda x, y, c: (x, y, 1 - c)),
    "y1": seq_pairs(lambda x, y, c: (x, y ^ 1, c)),
    "y3": seq_pairs(lambda x, y, c: (x, y ^ 3, c)),
    "x": seq_pairs(lambda x, y, c: (1 - x, y, c)),
}

SEQ_AXES = ("x_hi", "y", "core")


def by_seq(value, name):
    return lax.ppermute(value, SEQ_AXES, EXCHANGE[name])


def by_tp(value, flip):
    return lax.ppermute(value, "tp", [(k, k ^ flip) for k in range(TP)])


def shifted(value, steps):
    pairs = [(k, k + steps) for k in range(SEQ) if 0 <= k + steps < SEQ]
    return lax.ppermute(value, SEQ_AXES, pairs)


def z_exchange(blocks):
    return [by_tp(block, 2 * flip) for flip, block in zip(Z_FLIPS, blocks)]


def z_spread(block):
    return [by_tp(block, 2 * flip) for flip in Z_FLIPS]


def gather_tp(rows):
    mine = [by_tp(rows, 2 * flip) for flip in Z_FLIPS]
    other = by_tp(rows, 1)
    theirs = [by_tp(other, 2 * flip) for flip in Z_FLIPS]
    return [rows, other] + mine + theirs


def places():
    x_hi = lax.axis_index("x_hi")
    y = lax.axis_index("y")
    core = lax.axis_index("core")
    tp = lax.axis_index("tp")
    return {
        "seq": x_hi * 8 + y * 2 + core,
        "tp": tp,
        "z": tp >> 1,
        "x_low": tp & 1,
        "core": core,
        "y1": (y & 1) ^ (y >> 1),
        "y3": y >> 1,
        "x": x_hi,
    }


class Order:
    def __init__(self):
        self.last = None

    def __call__(self, body, ins, outs, needs=(), scratch=(), temporary=2 << 20, cost=0.3):
        ins = list(ins)
        needs = list(needs)
        if self.last is not None:
            needs.append(self.last)
        skip = len(ins) + len(needs)
        outs = list(outs) + [((8, 128), wide)]
        out_shape = [jax.ShapeDtypeStruct(shape, kind) for shape, kind in outs]
        count = len(ins)

        def run(*refs):
            given = refs[skip : skip + len(outs)]
            given[-1][...] = jnp.zeros_like(given[-1])
            body(refs[:count], given[:-1], refs[skip + len(outs) :])

        def size(shape, kind):
            lanes = -(-shape[-1] // 128) * 128
            total = lanes * jnp.dtype(kind).itemsize
            for extent in shape[:-1]:
                total *= max(extent, 1)
            return total

        held = (
            sum(size(value.shape, value.dtype) for value in ins)
            + sum(size(shape, kind) for shape, kind in outs)
            + sum(size(shape, kind) for shape, kind in scratch)
        )
        result = pl.pallas_call(
            run,
            out_shape=out_shape,
            in_specs=[pl.BlockSpec(memory_space=pltpu.VMEM)] * count
            + [pl.BlockSpec(memory_space=pl.ANY)] * len(needs),
            out_specs=[pl.BlockSpec(memory_space=pltpu.VMEM)] * len(outs),
            scratch_shapes=[pltpu.VMEM(shape, kind) for shape, kind in scratch],
            compiler_params=pltpu.CompilerParams(vmem_limit_bytes=held + temporary),
            cost_estimate=pl.CostEstimate(
                flops=int(cost * 1e9), bytes_accessed=0, transcendentals=0
            ),
            name=body.__name__,
        )(*ins, *needs)
        self.last = result[-1]
        return result[:-1]


def hold(order, values, strict=False):
    values = list(values)
    needs = [order.last]
    if strict:
        values, needs = values + needs, []

    def run(*refs):
        pass

    result = pl.pallas_call(
        run,
        out_shape=[jax.ShapeDtypeStruct(value.shape, value.dtype) for value in values],
        in_specs=[pl.BlockSpec(memory_space=pl.ANY)] * (len(values) + len(needs)),
        out_specs=[pl.BlockSpec(memory_space=pl.ANY)] * len(values),
        input_output_aliases={k: k for k in range(len(values))},
        compiler_params=pltpu.CompilerParams(vmem_limit_bytes=1 << 20),
        cost_estimate=pl.CostEstimate(flops=0, bytes_accessed=0, transcendentals=0),
    )(*values, *needs)
    if strict:
        order.last = result[-1]
        result = result[:-1]
    return result


def dot(left, right):
    return jnp.dot(left, right, preferred_element_type=wide)


def dot_rows(left, right):
    return lax.dot_general(left, right, (((1,), (1,)), ((), ())), preferred_element_type=wide)


def dot_cols(left, right):
    return lax.dot_general(left, right, (((0,), (0,)), ((), ())), preferred_element_type=wide)


def rms_factor(rows):
    return lax.rsqrt(jnp.mean(rows * rows, axis=-1, keepdims=True) + epsilon)


def norm_back(grad_normed, unit_rows, factor, gain_vec):
    scaled = grad_normed * gain_vec
    return factor * (scaled - unit_rows * jnp.mean(scaled * unit_rows, axis=-1, keepdims=True))


def span(index, size):
    return pl.ds(pl.multiple_of(index * size, size), size)


def eight_blocks(at, size):
    here = [span(2 * at["z"] + x, size) for x in (at["x_low"], 1 - at["x_low"])]
    mine = [span(2 * (at["z"] ^ flip) + at["x_low"], size) for flip in Z_FLIPS]
    theirs = [span(2 * (at["z"] ^ flip) + 1 - at["x_low"], size) for flip in Z_FLIPS]
    return here + mine + theirs


def write_eight(partial, at, outs):
    for place, out in zip(eight_blocks(at, outs[0].shape[0]), outs):
        out[...] = partial[place, :]


def read_eight(whole, at, blocks):
    for place, block in zip(eight_blocks(at, blocks[0].shape[0]), blocks):
        whole[place, :] = block[...]


def read_pairs(whole, z, blocks):
    size = blocks[0].shape[0]
    for flip, block in zip((0,) + Z_FLIPS, blocks):
        whole[span(z ^ flip, size), :] = block[...]


def normed_kernel(ins, outs, _):
    tokens, gain, w_key, w_value = ins
    normed, key_value = outs
    inputs = tokens[...].astype(wide)
    rows = (inputs * rms_factor(inputs) * gain[...]).astype(low)
    normed[...] = rows
    features = w_key.shape[1]
    key_value[:, :features] = dot(rows, w_key[...]).astype(low)
    key_value[:, features:] = dot(rows, w_value[...]).astype(low)


def project_kernel(ins, outs, _):
    outs[0][...] = dot(ins[0][...], ins[1][...]).astype(low)


def last_block(at, own_of_partner, four_of_partner, way):
    near = at["core"] == (0 if way == 1 else 1)
    return jnp.where(near, four_of_partner, own_of_partner)


def seen_scores(scores, order, distance, gap, inside):
    if order == 0:
        return jnp.where(gap >= 0, scores, masked_value)
    if order == 3:
        return jnp.where((gap < 0) & inside, scores, masked_value)
    return jnp.where(inside, scores, masked_value)


def distances(at, way):
    near = at["core"] == (0 if way == 1 else 1)
    return [0, 2, jnp.where(near, 1, 3), 4, jnp.where(near, 3, 1)]


def gap_of(rows, flipped=False):
    first = lax.broadcasted_iota(jnp.int32, (rows, rows), 0)
    second = lax.broadcasted_iota(jnp.int32, (rows, rows), 1)
    return second - first if flipped else first - second


def attend_kernel(ins, outs, scratch):
    query, own, two, across, four, partner_own, partner_four, w_out = ins
    heads_out, log_out = outs[:2]
    rows, features = query.shape
    at = places()
    scale = HD ** (-0.5)
    gap = gap_of(rows)
    away = distances(at, 1)
    blocks = [own[...], two[...], across[...], four[...]]
    blocks.append(last_block(at, partner_own[...], partner_four[...], 1))
    logs = []
    mixed = []
    for head in range(features // HD):
        here = slice(head * HD, (head + 1) * HD)
        there = slice(features + head * HD, features + (head + 1) * HD)
        scores = [
            seen_scores(
                dot_rows(query[:, here], block[:, here]) * scale,
                order,
                distance,
                gap,
                at["seq"] >= distance,
            )
            for order, (block, distance) in enumerate(zip(blocks, away))
        ]
        peak = scores[0].max(axis=-1, keepdims=True)
        for part in scores[1:]:
            peak = jnp.maximum(peak, part.max(axis=-1, keepdims=True))
        raised = [jnp.exp(part - peak) for part in scores]
        total = raised[0].sum(axis=-1, keepdims=True)
        for part in raised[1:]:
            total = total + part.sum(axis=-1, keepdims=True)
        inverse = 1.0 / total
        out = dot((raised[0] * inverse).astype(low), blocks[0][:, there])
        for part, block in zip(raised[1:], blocks[1:]):
            out = out + dot((part * inverse).astype(low), block[:, there])
        mixed.append(out.astype(low))
        logs.append(peak + jnp.log(total))
    for head, out in enumerate(mixed):
        heads_out[:, head * HD : (head + 1) * HD] = out
    lane = lax.broadcasted_iota(jnp.int32, (rows, HD), 1)
    log_out[...] = jnp.where(lane < 64, logs[0], logs[1])
    partial = scratch[0]
    partial[...] = dot(heads_out[...], w_out[...]).astype(low)
    write_eight(partial, at, outs[2:])


def sum_kernel(ins, outs, _):
    total = ins[0][...].astype(wide)
    for block in ins[1:]:
        total = total + block[...].astype(wide)
    outs[0][...] = total.astype(outs[0].dtype)


def sum_refs(refs):
    total = refs[0][...].astype(wide)
    for ref in refs[1:]:
        total = total + ref[...].astype(wide)
    return total


def norm_rows_kernel(ins, outs, _):
    tokens, gain = ins[5:]
    hidden, normed = outs
    at = places()
    rows = tokens[span(at["tp"], hidden.shape[0]), :].astype(wide) + sum_refs(ins[:5])
    hidden[...] = rows
    normed[...] = (rows * rms_factor(rows) * gain[...]).astype(low)


def pair_kernel(ins, outs, _):
    at = places()
    size = ins[0].shape[0]
    outs[0][span(at["x_low"], size), :] = ins[0][...]
    outs[0][span(1 - at["x_low"], size), :] = ins[1][...]


def ffn_kernel(ins, outs, scratch):
    w_gate, w_up, w_down, cotangent = ins[8:]
    normed, activated, grad_gate, grad_up = outs[:4]
    at = places()
    read_eight(normed, at, ins[:8])
    rows = normed[...]
    gate_pre = dot_rows(rows, w_gate[...])
    up_pre = dot_rows(rows, w_up[...])
    grad_act = dot_rows(cotangent[...], w_down[...])
    sigmoid = jax.nn.sigmoid(gate_pre)
    silu = gate_pre * sigmoid
    activated[...] = (silu * up_pre).astype(low)
    grad_gate[...] = (grad_act * up_pre * sigmoid * (1.0 + gate_pre * (1.0 - sigmoid))).astype(low)
    grad_up[...] = (grad_act * silu).astype(low)
    partial = scratch[0]
    partial[...] = (dot(grad_gate[...], w_gate[...]) + dot(grad_up[...], w_up[...])).astype(low)
    write_eight(partial, at, outs[4:])


def grad_rows_kernel(ins, outs, _):
    hidden, cotangent, gain = ins[5:]
    grad_hidden, grad_low, gain_part = outs
    at = places()
    grad_normed = sum_refs(ins[:5])
    rows = hidden[...]
    factor = rms_factor(rows)
    unit = rows * factor
    gain_part[...] = jnp.sum(grad_normed * unit, axis=0, keepdims=True)
    grad = cotangent[span(at["tp"], rows.shape[0]), :].astype(wide) + norm_back(
        grad_normed, unit, factor, gain[...]
    )
    grad_hidden[...] = grad
    grad_low[...] = grad.astype(low)


def heads_kernel(ins, outs, _):
    w_out, logs, heads_out = ins[4:]
    grad_hidden, grad_heads = outs
    read_pairs(grad_hidden, places()["z"], ins[:4])
    grad = dot_rows(grad_hidden[...], w_out[...]).astype(low)
    rows, features = grad.shape
    grad_heads[:, :features] = grad
    product = grad.astype(wide) * heads_out[...].astype(wide)
    values = [logs[:, :1], logs[:, 64:65]]
    for head in range(2):
        values.append(jnp.sum(product[:, head * HD : (head + 1) * HD], axis=-1, keepdims=True))
    group = lax.broadcasted_iota(jnp.int32, (rows, HD), 1) >> 3
    both = jnp.zeros((rows, HD), wide)
    for k, value in enumerate(values):
        both = jnp.where((group & 3) == k, value, both)
    first = both.astype(low).astype(wide)
    second = (both - first).astype(low).astype(wide)
    rest = jnp.where(group < 8, second, both - first - second)
    grad_heads[:, features:] = jnp.where(group < 4, first, rest).astype(low)


def grad_query_kernel(ins, outs, _):
    query_all, heads_out, logs, grad_heads, own, two, across, four, partner_own, partner_four = ins
    rows, features = query_all.shape
    at = places()
    scale = HD ** (-0.5)
    gap = gap_of(rows)
    away = distances(at, 1)
    blocks = [own[...], two[...], across[...], four[...]]
    blocks.append(last_block(at, partner_own[...], partner_four[...], 1))
    for head in range(features // HD):
        here = slice(head * HD, (head + 1) * HD)
        there = slice(features + head * HD, features + (head + 1) * HD)
        query = query_all[:, here]
        grad = grad_heads[:, here]
        log_total = logs[:, head * 64 : head * 64 + 1]
        inner = jnp.sum(
            grad.astype(wide) * heads_out[:, here].astype(wide), axis=-1, keepdims=True
        )
        total = jnp.zeros((rows, HD), wide)
        for order, (block, distance) in enumerate(zip(blocks, away)):
            scores = seen_scores(
                dot_rows(query, block[:, here]) * scale,
                order,
                distance,
                gap,
                at["seq"] >= distance,
            )
            weights = jnp.exp(scores - log_total)
            grad_scores = weights * (dot_rows(grad, block[:, there]) - inner)
            total = total + dot(grad_scores.astype(low), block[:, here])
        outs[0][:, here] = (total * scale).astype(low)


def grad_key_kernel(ins, outs, scratch):
    key_value = ins[0]
    sides = ins[1:7]
    grads = ins[7:13]
    grad_key, grad_value = outs
    rows, features = grad_key.shape
    at = places()
    scale = HD ** (-0.5)
    gap = gap_of(rows, flipped=True)
    away = distances(at, -1)
    side_blocks = [side[...] for side in sides[:4]]
    side_blocks.append(last_block(at, sides[4][...], sides[5][...], -1))
    grad_blocks = [grad[...] for grad in grads[:4]]
    grad_blocks.append(last_block(at, grads[4][...], grads[5][...], -1))
    sums = [grad[:, features:].astype(wide).T for grad in grad_blocks]
    for head in range(features // HD):
        here = slice(head * HD, (head + 1) * HD)
        there = slice(features + head * HD, features + (head + 1) * HD)
        key = key_value[:, here]
        value = key_value[:, there]
        total_key = jnp.zeros((rows, HD), wide)
        total_value = jnp.zeros((rows, HD), wide)
        for order, (side, grad_all, logs, distance) in enumerate(
            zip(side_blocks, grad_blocks, sums, away)
        ):
            query = side[:, here]
            grad = grad_all[:, here]
            log_total, inner = [
                logs[8 * k : 8 * k + 1]
                + logs[32 + 8 * k : 33 + 8 * k]
                + logs[64 + 8 * k : 65 + 8 * k]
                for k in (head, 2 + head)
            ]
            scores = seen_scores(
                dot_rows(key, query) * scale, order, distance, gap, at["seq"] + distance < SEQ
            )
            weights = jnp.exp(scores - log_total)
            total_value = total_value + dot(weights.astype(low), grad)
            grad_scores = weights * (dot_rows(value, grad) - inner)
            total_key = total_key + dot(grad_scores.astype(low), query)
        grad_key[:, here] = (total_key * scale).astype(low)
        grad_value[:, here] = total_value.astype(low)


def back_kernel(ins, outs, scratch):
    grad_query, grad_key, grad_value, w_query, w_key, w_value, tokens, gain_ffn_part, ffn_partial = ins
    keep_one, keep_two, send_one, send_two = outs
    at = places()
    rows = tokens.shape[0]
    back = (
        dot_rows(grad_query[...], w_query[...])
        + dot_rows(grad_key[...], w_key[...])
        + dot_rows(grad_value[...], w_value[...])
    )
    inputs = tokens[...].astype(wide)
    gain_attn_part = jnp.sum(back * (inputs * rms_factor(inputs)), axis=0, keepdims=True)
    partial = scratch[0]
    width = tokens.shape[1]
    partial[:, :width] = back.astype(low)
    share = rows // TP
    cells = width // TP // HD
    for k in range(TP):
        parts = [
            gain[:, (k * cells + cell) * HD : (k * cells + cell + 1) * HD]
            for gain in (gain_attn_part, gain_ffn_part[...])
            for cell in range(cells)
        ]
        parts.append(jnp.zeros((share - len(parts), HD), wide))
        partial[k * share : (k + 1) * share, width:] = jnp.concatenate(parts, axis=0).astype(low)
    size = rows // 4
    z = at["z"]
    cut = width // 2
    for out, first, flips in (
        (keep_one, 0, (0, 3)),
        (send_one, 0, (1, 2)),
        (keep_two, cut, (0, 1)),
        (send_two, cut, (3, 2)),
    ):
        for k, flip in enumerate(flips):
            here = slice(k * size, (k + 1) * size)
            there = span(z ^ flip, size)
            out[here, :cut] = partial[there, first : first + cut]
            out[here, cut:width] = ffn_partial[there, first : first + cut]
            if first > 0:
                out[here, width:] = partial[there, width:]


def sum_middle_kernel(ins, outs, _):
    for keep, arrived, stay, send in ((ins[0], ins[1], outs[0], outs[1]), (ins[2], ins[3], outs[2], outs[3])):
        size = stay.shape[0]
        stay[...] = keep[:size, :].astype(wide) + arrived[:size, :].astype(wide)
        send[...] = (keep[size:, :].astype(wide) + arrived[size:, :].astype(wide)).astype(low)


def sum_last_kernel(ins, outs, _):
    keep, send = outs
    at = places()
    size = keep.shape[0]
    width = ins[0].shape[1]
    cut = width // 2
    for out, index in ((keep, at["x_low"]), (send, 1 - at["x_low"])):
        here = span(index, size)
        first = (ins[0][here, :] + ins[1][here, :].astype(wide)).astype(out.dtype)
        second = (ins[2][here, :] + ins[3][here, :].astype(wide)).astype(out.dtype)
        out[:, :cut] = first[:, :cut]
        out[:, cut:width] = second[:, :cut]
        out[:, width : width + cut] = first[:, cut:]
        out[:, width + cut : 2 * width] = second[:, cut:width]
        out[:, 2 * width :] = second[:, width:]


def last_rows_kernel(ins, outs, _):
    keep, arrived, grad_hidden, hidden, tokens, gain = ins
    rows_out, gains = outs
    width = hidden.shape[1]
    at = places()
    inputs = tokens[span(at["tp"], keep.shape[0]), :].astype(wide)
    factor = rms_factor(inputs)
    grad_normed = keep[:, :width] + arrived[:, :width].astype(wide)
    grad = grad_hidden[...] + norm_back(grad_normed, inputs * factor, factor, gain[...])
    rows_out[:, :width] = grad.astype(low)
    rows_out[:, width:] = (
        hidden[...] + keep[:, width : 2 * width] + arrived[:, width : 2 * width].astype(wide)
    ).astype(low)
    sums = keep[:, 2 * width :] + arrived[:, 2 * width :].astype(wide)
    gains[...] = jnp.zeros_like(gains)
    gains[:, : sums.shape[1]] = sums[: gains.shape[0], :].astype(low)


def last_pair_kernel(ins, outs, _):
    at = places()
    size = ins[0].shape[0]
    width = outs[0].shape[1]
    for value, index in zip(ins, (at["x_low"], 1 - at["x_low"])):
        outs[0][span(index, size), :] = value[:, :width]
        outs[1][span(index, size), :] = value[:, width:]


def stack_kernel(ins, outs, _):
    for k, out in enumerate(outs):
        size = ins[2 * k].shape[0]
        out[:size, :] = ins[2 * k][...]
        out[size:, :] = ins[2 * k + 1][...]


def token_outputs_kernel(ins, outs, _):
    z = places()["z"]
    size = ins[0].shape[0] // 2
    for out, own, arrived, flips in (
        (outs[0], ins[0], ins[1], (0, 1, 3, 2)),
        (outs[1], ins[2], ins[3], (0, 3, 1, 2)),
    ):
        blocks = (own[:size, :], own[size:, :], arrived[:size, :], arrived[size:, :])
        for flip, block in zip(flips, blocks):
            out[span(z ^ flip, size), :] = block.astype(out.dtype)


def part(ref, axis, start, size):
    return ref[:, pl.ds(start, size)] if axis == 1 else ref[pl.ds(start, size), :]


def put(ref, axis, start, size, value):
    if axis == 1:
        ref[:, pl.ds(start, size)] = value
    else:
        ref[pl.ds(start, size), :] = value


def split_op(keep, arrived, bit, axis):
    shape = list(keep.shape)
    shape[axis] //= 2
    size = shape[axis]

    def body(at, ins, outs):
        for out, index in zip(outs, (at[bit], 1 - at[bit])):
            start = pl.multiple_of(index * size, size)
            out[...] = (
                part(ins[0], axis, start, size).astype(wide)
                + part(ins[1], axis, start, size).astype(wide)
            ).astype(low)

    return body, [keep, arrived], [(tuple(shape), low)] * 2


def add_op(keep, arrived):
    def body(at, ins, outs):
        outs[0][...] = (ins[0][...].astype(wide) + ins[1][...].astype(wide)).astype(
            outs[0].dtype
        )

    return body, [keep, arrived], [(keep.shape, keep.dtype)]


def join_op(own, arrived, bit, axis, kind=low):
    shape = list(own.shape)
    size = shape[axis]
    shape[axis] *= 2

    def body(at, ins, outs):
        for value, index in zip(ins, (at[bit], 1 - at[bit])):
            start = pl.multiple_of(index * size, size)
            put(outs[0], axis, start, size, value[...].astype(kind))

    return body, [own, arrived], [(tuple(shape), kind)]


def add_tail_op(keep, arrived, tail):
    rows, width = keep.shape

    def body(at, ins, outs):
        outs[0][:rows, :] = (ins[0][...].astype(wide) + ins[1][...].astype(wide)).astype(low)
        outs[0][rows:, :] = ins[2][...]

    return body, [keep, arrived, tail], [((rows + tail.shape[0], width), low)]


def join_tail_op(own, arrived, bit, tail):
    rows, width = own.shape
    size = rows - tail

    def body(at, ins, outs):
        for value, index in zip(ins, (at[bit], 1 - at[bit])):
            outs[0][span(index, size), :] = value[:size, :]
        outs[0][2 * size :, :] = (
            ins[0][size:, :].astype(wide) + ins[1][size:, :].astype(wide)
        ).astype(low)

    return body, [own, arrived], [((2 * size + tail, width), low)]


def run_ops(order, ops, needs=()):
    ins = [value for _, values, _ in ops for value in values]
    outs = [out for _, _, shapes in ops for out in shapes]

    def body(in_refs, out_refs, _):
        at = places()
        first = last = 0
        for step, values, shapes in ops:
            step(
                at,
                in_refs[first : first + len(values)],
                out_refs[last : last + len(shapes)],
            )
            first += len(values)
            last += len(shapes)

    flat = list(order(body, ins, outs, needs))
    result = []
    for _, _, shapes in ops:
        result.append(flat[: len(shapes)])
        flat = flat[len(shapes) :]
    return result


FFN_ORDERS = (("y1", "y3", "x"), ("y3", "x", "y1"), ("x", "y1", "y3"))


def ffn_terms(ins, k):
    terms = []
    first = 0
    for operand, start, stop in FFN_PIECES[k]:
        last = first + stop - start
        terms.append((first, last, ins[operand][:, start:stop], ins[4 if operand == 2 else 3]))
        first = last
    return terms


def ffn_send_kernel(arrays):
    def ffn_send(ins, outs, _):
        out = outs[0]
        half = out.shape[1]
        other = 1 - places()["core"]
        base = 0
        for k in arrays:
            for first, last, left, right in ffn_terms(ins, k):
                out[base + first : base + last, :] = dot_cols(
                    left, right[:, span(other, half)]
                ).astype(low)
            base += FFN_ROWS[k]

    return ffn_send


def ffn_keep_kernel(arrays):
    def ffn_keep(ins, outs, _):
        at = places()
        arrived = ins[5]
        base = 0
        for k, keep, send in zip(arrays, outs[0::2], outs[1::2]):
            size = keep.shape[1]
            bit = at[FFN_ORDERS[k][0]]
            for out, index in ((keep, bit), (send, 1 - bit)):
                start = pl.multiple_of((2 * at["core"] + index) * size, size)
                for first, last, left, right in ffn_terms(ins, k):
                    own = dot_cols(left, right[:, pl.ds(start, size)])
                    got = arrived[base + first : base + last, span(index, size)]
                    out[first:last, :] = (own + got.astype(wide)).astype(low)
            base += FFN_ROWS[k]

    return ffn_keep


def attn_terms(ins):
    normed, grad_hidden, grad_query, grad_key, grad_value, heads_out = ins
    half = heads_out.shape[1] // 2
    return [
        [(normed, grad_query[...]), (grad_hidden, heads_out[:, :half])],
        [(normed, grad_key[...]), (grad_hidden, heads_out[:, half:])],
        [(normed, grad_value[...])],
    ]


def attn_half_kernel(own):
    def attn_half(ins, outs, _):
        out = outs[0]
        half = out.shape[0]
        index = places()["core"] if own else 1 - places()["core"]
        first = 0
        for terms in attn_terms(ins):
            for left, right in terms:
                last = first + right.shape[1]
                out[:, first:last] = dot_cols(left[:, span(index, half)], right).astype(out.dtype)
                first = last

    return attn_half


def packed_rows(rows, lanes, width):
    across = width // 128
    full, rest = divmod(lanes // 128, across)
    if rest == 1 and rows % across == 0:
        return rows * full + rows // across
    return rows * (full + (rest > 0))


def place_cells(rows, lanes, width):
    across = width // 128
    cells = lanes // 128
    runs = []
    full = cells // across
    for k in range(full * across):
        runs.append((0, k * 128, (k // across) * rows, (k % across) * 128, rows))
    rest = cells - full * across
    if rest and rows % across == 0 and rest == 1:
        size = rows // across
        for k in range(across):
            runs.append((k * size, full * across * 128, full * rows, k * 128, size))
    elif rest:
        for k in range(rest):
            runs.append((0, (full * across + k) * 128, full * rows, k * 128, rows))
    return runs


def pack(message, base, value):
    rows, lanes = value.shape
    for row, lane, to_row, to_lane, size in place_cells(rows, lanes, message.shape[1]):
        message[base + to_row : base + to_row + size, to_lane : to_lane + 128] = value[
            row : row + size, lane : lane + 128
        ]


def add_packed(keep, message, base, lanes):
    rows = keep.shape[0]
    columns = [[] for _ in range(lanes // 128)]
    for row, lane, from_row, from_lane, size in place_cells(rows, lanes, message.shape[1]):
        here = keep[row : row + size, lane : lane + 128].astype(wide)
        there = message[base + from_row : base + from_row + size, from_lane : from_lane + 128]
        columns[lane // 128].append(here + there.astype(wide))
    return [jnp.concatenate(parts, axis=0) if len(parts) > 1 else parts[0] for parts in columns]


ATTN_ORDERS = (("y1", "y3", "x"), ("y3", "x", "y1"), ("x", "y1", "y3"))
WAYS = ("y1", "y3", "x")


def tops(step):
    return {orders[step]: rows for orders, rows in zip(FFN_ORDERS, FFN_ROWS)}


def round_one_kernel(ins, outs, _):
    at = places()
    own, arrived = ins[6:]
    messages = dict(zip(WAYS, outs[:3]))
    for k in range(3):
        way = FFN_ORDERS[k][2]
        size = outs[6 + k].shape[1]
        for out, index in ((outs[6 + k], at[way]), (messages[way], 1 - at[way])):
            start = pl.multiple_of(index * size, size)
            out[: FFN_ROWS[k], :] = (
                ins[k][:, pl.ds(start, size)].astype(wide)
                + ins[3 + k][:, pl.ds(start, size)].astype(wide)
            ).astype(low)
    base = 0
    for k in range(3):
        keep = outs[3 + k]
        size, lanes = keep.shape
        way = ATTN_ORDERS[k][0]
        for kept, index in ((True, at[way]), (False, 1 - at[way])):
            here = span(index, size)
            for lane in range(0, lanes, 128):
                there = slice(base + lane, base + lane + 128)
                value = (own[here, there] + arrived[here, there].astype(wide)).astype(low)
                if kept:
                    keep[:, lane : lane + 128] = value
                else:
                    row = tops(2)[way] + lane // 128 * size
                    messages[way][row : row + size, :] = value
        base += lanes


def attn_step(at, keeps, arrived, top, step, outs, messages, message_top):
    for k, (keep, out) in enumerate(zip(keeps, outs)):
        came, way = ATTN_ORDERS[k][step - 1], ATTN_ORDERS[k][step]
        columns = add_packed(keep, arrived[came], top[came], keep.shape[1])
        size = keep.shape[0] // 2
        first = at[way] == 0
        go = []
        for lane, column in enumerate(columns):
            one, two = column[:size, :], column[size:, :]
            out[:, lane * 128 : (lane + 1) * 128] = jnp.where(first, one, two).astype(low)
            go.append(jnp.where(first, two, one).astype(low))
        pack(messages[way], message_top[way], jnp.concatenate(go, axis=1))


def ffn_joined(at, sent, arrived, step, messages):
    for k, rows in enumerate(FFN_ROWS):
        back = FFN_ORDERS[k][step]
        message = messages[FFN_ORDERS[k][step - 1]]
        width = sent[back].shape[1]
        for value, index in ((sent[back], at[back]), (arrived[back], 1 - at[back])):
            start = pl.multiple_of(index * width, width)
            message[:rows, pl.ds(start, width)] = value[:rows, :]


def round_two_kernel(ins, outs, _):
    at = places()
    arrived, messages = dict(zip(WAYS, ins[:3])), dict(zip(WAYS, outs[:3]))
    for k, rows in enumerate(FFN_ROWS):
        way = FFN_ORDERS[k][2]
        messages[way][:rows, :] = (
            ins[3 + k][...].astype(wide) + arrived[way][:rows, :].astype(wide)
        ).astype(low)
    attn_step(at, ins[6:9], arrived, tops(2), 1, outs[3:], messages, tops(2))


def round_three_kernel(ins, outs, _):
    at = places()
    sent, arrived = dict(zip(WAYS, ins[:3])), dict(zip(WAYS, ins[3:6]))
    messages = dict(zip(WAYS, outs[:3]))
    ffn_joined(at, sent, arrived, 2, messages)
    attn_step(at, ins[6:9], arrived, tops(2), 2, outs[3:], messages, tops(1))


def round_four_kernel(ins, outs, _):
    at = places()
    sent, arrived = dict(zip(WAYS, ins[:3])), dict(zip(WAYS, ins[3:6]))
    messages = dict(zip(WAYS, outs))
    ffn_joined(at, sent, arrived, 1, messages)
    for k in range(3):
        way = ATTN_ORDERS[k][2]
        keep = ins[6 + k]
        rows, lanes = keep.shape
        first = tops(0)[way]
        for lane, column in enumerate(add_packed(keep, arrived[way], tops(1)[way], lanes)):
            messages[way][first : first + rows, lane * 128 : (lane + 1) * 128] = column.astype(low)
        if k == 2:
            gains = ins[9]
            messages[way][first + rows : first + rows + gains.shape[0], :lanes] = gains[...]


def round_five_kernel(ins, outs, _):
    at = places()
    sent, arrived = dict(zip(WAYS, ins[:3])), dict(zip(WAYS, ins[3:]))
    for k, out in enumerate(outs):
        way = ATTN_ORDERS[k][2]
        first = tops(0)[way]
        lanes = out.shape[1]
        rows = 128
        for value, index in ((sent[way], at[way]), (arrived[way], 1 - at[way])):
            out[span(index, rows), :] = value[first : first + rows, :lanes]
        if k == 2:
            tail = slice(first + rows, first + rows + out.shape[0] - 2 * rows)
            out[2 * rows :, :] = (
                sent[way][tail, :lanes].astype(wide) + arrived[way][tail, :lanes].astype(wide)
            ).astype(low)


def ffn_halves_kernel(ins, outs, _):
    at = places()
    sent, arrived = dict(zip(WAYS, ins[:3])), dict(zip(WAYS, ins[3:]))
    base = 0
    for k, rows in enumerate(FFN_ROWS):
        way = FFN_ORDERS[k][0]
        width = sent[way].shape[1]
        for value, index in ((sent[way], at[way]), (arrived[way], 1 - at[way])):
            start = pl.multiple_of(index * width, width)
            outs[0][base : base + rows, pl.ds(start, width)] = value[:rows, :]
        base += rows


def write_out(order, body, ins, outs, buffers, small=(), into=None, cost=0.3):
    ins, old = list(ins), list(into or [])
    needs = [order.last]
    count, many = len(ins), len(outs)
    skip = count + len(old) + len(needs)
    small = list(small) + [((8, 128), wide)]

    def run(*refs):
        targets = refs[skip : skip + many]
        others = refs[skip + many : skip + many + len(small)]
        scratch = refs[skip + many + len(small) :]
        held, arrived = scratch[: len(buffers)], scratch[len(buffers)]
        others[-1][...] = jnp.zeros_like(others[-1])
        copies = []
        for k, (value, target) in enumerate(body(places(), refs[:count], targets, others[:-1])):
            held[k][...] = value
            copies.append(pltpu.make_async_copy(held[k], target, arrived.at[k]))
            copies[-1].start()
        for copy in copies:
            copy.wait()

    size = sum(shape[0] * shape[1] * 4 for shape in buffers) + sum(
        value.size * value.dtype.itemsize for value in ins
    )
    result = pl.pallas_call(
        run,
        out_shape=[jax.ShapeDtypeStruct(shape, wide) for shape in outs]
        + [jax.ShapeDtypeStruct(shape, kind) for shape, kind in small],
        in_specs=[pl.BlockSpec(memory_space=pltpu.VMEM)] * count
        + [pl.BlockSpec(memory_space=pltpu.HBM)] * len(old)
        + [pl.BlockSpec(memory_space=pl.ANY)] * len(needs),
        out_specs=[pl.BlockSpec(memory_space=pltpu.HBM)] * many
        + [pl.BlockSpec(memory_space=pltpu.VMEM)] * len(small),
        scratch_shapes=[pltpu.VMEM(shape, wide) for shape in buffers]
        + [pltpu.SemaphoreType.DMA((len(buffers),))],
        input_output_aliases={count + k: k for k in range(len(old))},
        compiler_params=pltpu.CompilerParams(vmem_limit_bytes=size + (6 << 20)),
        cost_estimate=pl.CostEstimate(
            flops=int(cost * 1e9), bytes_accessed=0, transcendentals=0
        ),
        name=body.__name__,
    )(*ins, *old, *needs)
    order.last = result[-1]
    return list(result[:-1])


def write_ffn(own):
    def write_ffn_half(at, ins, targets, _):
        half = ins[0].shape[1]
        index = at["core"] if own else 1 - at["core"]
        rows = targets[0].shape[0]
        for k, target in enumerate(targets):
            yield ins[0][k * rows : (k + 1) * rows, :].astype(wide), target.at[:, span(index, half)]

    return write_ffn_half


def write_attn(own):
    def write_attn_half(at, ins, targets, small):
        one, two, three = ins[:3]
        features = three.shape[1]
        half = one.shape[0]
        here = span(at["core"] if own else 1 - at["core"], half)
        yield one[:, :features].astype(wide), targets[0].at[here, :]
        yield two[:, :features].astype(wide), targets[1].at[here, :]
        yield three[:half, :].astype(wide), targets[2].at[here, :]
        halves = (one[:, features:], two[:, features:])
        out = jnp.concatenate([value.astype(wide).T for value in halves], axis=0)
        yield out, targets[3].at[:, here]
        if not own:
            sums = ins[3][half:, :].astype(wide) + three[half:, :].astype(wide)
            for k, gain in enumerate(small):
                gain[:, :HD] = sums[2 * k : 2 * k + 1, :HD]
                gain[:, HD:] = sums[2 * k + 1 : 2 * k + 2, :HD]

    return write_attn_half


def on_device(
    tokens, gain_attn, w_query, w_key, w_value, w_out, gain_ffn, w_gate, w_up, w_down, cotangent
):
    rows, width = tokens.shape
    features = w_query.shape[1]
    units = w_gate.shape[1]
    share = rows // TP
    quarter = rows // 4
    order = Order()
    gain_attn = gain_attn.reshape(1, width)
    gain_ffn = gain_ffn.reshape(1, width)
    w_gate, w_up = w_gate.T, w_up.T
    blocks_out = [((share, width), low)] * 8
    whole = ((rows, width), low)
    small = ((rows, features), low)
    keep_and_send = [((share, width), wide), ((share, width), low)]

    normed_attn, own = order(
        normed_kernel,
        [tokens, gain_attn, w_key, w_value],
        [whole, ((rows, 2 * features), low)],
        temporary=6 << 20, cost=1.0)
    two, four = shifted(own, 2), shifted(own, 4)
    partner_own = by_seq(own, "core")
    (query,) = order(project_kernel, [normed_attn, w_query], [small])
    query_two, query_four = shifted(query, -2), shifted(query, -4)
    query_partner_own = by_seq(query, "core")
    across = by_seq(two, "core")
    partner_four = by_seq(four, "core")
    keys = [own, two, across, four, partner_own, partner_four]
    heads_out, logs, *blocks = order(
        attend_kernel,
        [query] + keys + [w_out],
        [small, ((rows, HD), wide)] + blocks_out,
        scratch=[whole],
        temporary=6 << 20, cost=2.5,
    )
    theirs = z_exchange(blocks[5:])
    mine = z_exchange(blocks[2:5])
    (send,) = order(
        sum_kernel, [blocks[1], theirs[1], theirs[2], theirs[0]], [((share, width), low)], needs=[query_two, query_four]
    )
    arrived = by_tp(send, 1)
    query_two, query_four = hold(order, [query_two, query_four])
    query_across = by_seq(query_two, "core")
    query_partner_four = by_seq(query_four, "core")
    hidden, normed_rows = order(
        norm_rows_kernel,
        [blocks[0]] + mine + [arrived, tokens, gain_ffn],
        keep_and_send,
        needs=[query_across, query_partner_own, query_partner_four],
    )
    gathered = gather_tp(normed_rows)

    normed_ffn, activated, grad_gate, grad_up, *blocks = order(
        ffn_kernel,
        gathered + [w_gate, w_up, w_down, cotangent],
        [whole] + [((rows, units), low)] * 3 + blocks_out,
        scratch=[whole],
        temporary=12 << 20, cost=5.0)
    theirs = z_exchange(blocks[5:])
    ffn_operands = [grad_gate, grad_up, activated, normed_ffn, cotangent]
    half = width // 2
    (sent,) = order(
        ffn_send_kernel([0, 1, 2]),
        ffn_operands,
        [((3 * units, half), low)],
        temporary=6 << 20, cost=2.5)
    core_arrived = by_seq(sent, "core")
    mine = z_exchange(hold(order, blocks[2:5]))
    parts = order(
        ffn_keep_kernel([0, 1, 2]),
        ffn_operands + [core_arrived],
        [((rows_k, half // 2), low) for rows_k in FFN_ROWS for _ in range(2)],
        temporary=6 << 20, cost=2.5)
    ffn_keeps = list(parts[0::2])
    last_part = parts[5]
    ffn_flights = [by_seq(part, names[0]) for part, names in zip(parts[1:4:2], FFN_ORDERS)]

    def ffn_split(steps, needs=()):
        parts = run_ops(
            order,
            [
                split_op(ffn_keeps[k], ffn_flights[k], FFN_ORDERS[k][step], 1)
                for k, step in steps
            ],
            needs,
        )
        for (k, step), (keep, send) in zip(steps, parts):
            ffn_keeps[k] = keep
            ffn_flights[k] = by_seq(send, FFN_ORDERS[k][step])

    (send,) = order(sum_kernel, [blocks[1]] + theirs, [((share, width), low)], cost=3.0)
    arrived = by_tp(send, 1)
    grad_hidden, grad_low, gain_ffn_part = order(
        grad_rows_kernel,
        [blocks[0]] + mine + [arrived, hidden, cotangent, gain_ffn],
        keep_and_send + [((1, width), wide)], cost=1.5)
    (pair,) = order(
        pair_kernel, [grad_low, by_tp(grad_low, 1)], [((quarter, width), low)], cost=1.5
    )
    gathered = [pair] + z_spread(pair)
    ffn_flights += [by_seq(value, FFN_ORDERS[2][0]) for value in hold(order, [last_part])]
    ffn_split([(0, 1), (1, 1)])
    grad_hidden_low, grad_heads = order(
        heads_kernel,
        gathered + [w_out, logs, heads_out],
        [whole, ((rows, features + HD), low)], cost=2.0)
    grad_two, grad_four = shifted(grad_heads, -2), shifted(grad_heads, -4)
    (grad_query,) = order(
        grad_query_kernel,
        [query, heads_out, logs, grad_heads] + keys,
        [small],
        temporary=6 << 20, cost=2.0)
    (ffn_partial,) = order(project_kernel, [activated, w_down], [whole], temporary=6 << 20, cost=1.0)
    grad_two, grad_four, grad_late = hold(order, [grad_two, grad_four, grad_heads])
    grad_partner_own = by_seq(grad_late, "core")
    grad_across = by_seq(grad_two, "core")
    grad_partner_four = by_seq(grad_four, "core")
    cut = width
    grad_key, grad_value = order(
        grad_key_kernel,
        [own, query, query_two, query_across, query_four, query_partner_own, query_partner_four]
        + [grad_late, grad_two, grad_across, grad_four, grad_partner_own, grad_partner_four],
        [small, small],
        needs=ffn_flights[2:],
        temporary=8 << 20, cost=0.3)
    ffn_split([(2, 1)])

    operands = [normed_attn, grad_hidden_low, grad_query, grad_key, grad_value, heads_out]
    (sent,) = order(
        attn_half_kernel(False), operands, [((width // 2, 4 * features), low)], ffn_flights[:2], temporary=4 << 20, cost=2.5)
    core_arrived = by_seq(sent, "core")
    keep_one, keep_two, send_one, send_two = order(
        back_kernel,
        [grad_query, grad_key, grad_value, w_query, w_key, w_value, tokens, gain_ffn_part, ffn_partial],
        [((2 * quarter, cut), low), ((2 * quarter, cut + HD), low)] * 2,
        scratch=[((rows, width + HD), low)],
        temporary=12 << 20, cost=0.3)
    one_arrived, two_arrived = by_tp(send_one, 2), by_tp(send_two, 6)
    (own_half,) = order(
        attn_half_kernel(True), operands, [((width // 2, 4 * features), wide)], temporary=4 << 20)
    widths = (features + features // 2, features + features // 2, features)

    def messages_of(width_out, size, ffn_step, attn_step_out):
        by_way = {orders[attn_step_out]: part for orders, part in zip(ATTN_ORDERS, widths)}
        top = tops(ffn_step)
        return [
            ((top[way] + packed_rows(size, by_way[way], width_out), width_out), low)
            for way in WAYS
        ]

    def kept(size):
        return [((size, part), low) for part in widths]

    def fly(messages):
        return [by_seq(message, way) for message, way in zip(messages, WAYS)]

    *parts, keep_x, keep_y, keep_z, ffn_x, ffn_y, ffn_z = order(
        round_one_kernel,
        ffn_keeps + ffn_flights + [own_half, core_arrived],
        messages_of(128, 512, 2, 0) + kept(512) + [((rows_k, 128), low) for rows_k in FFN_ROWS],
        temporary=4 << 20, cost=4.0,
    )
    flights = fly(parts)

    stay_one, go_one, stay_two, go_two = order(
        sum_middle_kernel,
        [keep_one, one_arrived, keep_two, two_arrived],
        [
            ((quarter, cut), wide),
            ((quarter, cut), low),
            ((quarter, cut + HD), wide),
            ((quarter, cut + HD), low),
        ], cost=3.0)
    one_arrived, two_arrived = by_tp(go_one, 6), by_tp(go_two, 2)

    *parts, keep_x, keep_y, keep_z = order(
        round_two_kernel,
        flights + [ffn_x, ffn_y, ffn_z, keep_x, keep_y, keep_z],
        messages_of(128, 256, 2, 1) + kept(256),
    )
    flights = fly(parts)
    keep, send = order(
        sum_last_kernel,
        [stay_one, one_arrived, stay_two, two_arrived],
        [((share, 2 * width + HD), wide), ((share, 2 * width + HD), low)],
    )
    arrived = by_tp(send, 1)
    *parts, keep_x, keep_y, keep_z = order(
        round_three_kernel,
        parts + flights + [keep_x, keep_y, keep_z],
        messages_of(256, 128, 1, 2) + kept(128),
    )
    flights = fly(parts)
    last_rows, gains = order(
        last_rows_kernel,
        [keep, arrived, grad_hidden, hidden, tokens, gain_attn],
        [((share, 2 * width), low), ((16, features), low)], cost=6.0)
    arrived = by_tp(last_rows, 1)
    below = {ATTN_ORDERS[0][2]: 128, ATTN_ORDERS[1][2]: 128, ATTN_ORDERS[2][2]: 128 + 16}
    parts = order(
        round_four_kernel,
        parts + flights + [keep_x, keep_y, keep_z, gains],
        [((tops(0)[way] + below[way], 512), low) for way in WAYS], cost=8.0)
    flights = fly(parts)
    first, second = order(last_pair_kernel, [last_rows, arrived], [((quarter, width), low)] * 2, cost=0.3)
    first_arrived, second_arrived = by_tp(first, 2), by_tp(second, 6)
    firsts, seconds = order(
        stack_kernel,
        [first, first_arrived, second, second_arrived],
        [((2 * quarter, width), low)] * 2, cost=2.0)
    first_arrived, second_arrived = by_tp(firsts, 6), by_tp(seconds, 2)
    one, two, three = order(
        round_five_kernel,
        list(parts) + flights,
        [((256, widths[0]), low), ((256, widths[1]), low), ((256 + 16, widths[2]), low)],
    )
    ffn_last = list(parts) + flights
    flights = [by_seq(value, orders[1]) for value, orders in zip((one, two, three), ATTN_ORDERS)]
    (ffn_half,) = order(ffn_halves_kernel, ffn_last, [((3 * units, width // 2), low)])

    def attn_join(step, needs=()):
        nonlocal one, two, three, flights
        names = [orders[step] for orders in ATTN_ORDERS]
        (one,), (two,), (three,) = run_ops(
            order,
            [
                join_op(one, flights[0], names[0], 0),
                join_op(two, flights[1], names[1], 0),
                join_tail_op(three, flights[2], names[2], gains.shape[0]),
            ],
            needs,
        )
        names = [orders[step - 1] if step > 0 else "core" for orders in ATTN_ORDERS]
        flights = [by_seq(value, name) for value, name in zip((one, two, three), names)]

    ffn_shapes = [(units, width)] * 3
    ffn_buffers = [(units, width // 2)] * 3
    grads_ffn = write_out(order, write_ffn(True), [ffn_half], ffn_shapes, ffn_buffers)
    attn_join(1, [first_arrived, second_arrived])
    (ffn_half,) = hold(order, [ffn_half], True)
    ffn_arrived = by_seq(ffn_half, "core")
    grads_ffn = write_out(
        order, write_ffn(False), [ffn_arrived], ffn_shapes, ffn_buffers, into=grads_ffn, cost=8.0
    )
    attn_join(0)
    attn_shapes = [(width, features)] * 3 + [(features, width)]
    attn_buffers = [(width // 2, features)] * 3 + [(features, width // 2)]
    grads_attn = write_out(
        order, write_attn(True), [one, two, three], attn_shapes, attn_buffers
    )
    grad_tokens, block_out = order(
        token_outputs_kernel,
        [firsts, first_arrived, seconds, second_arrived],
        [((rows, width), wide), whole],
    )
    grad_w_query, grad_w_key, grad_w_value, grad_w_out, grad_gain_attn, grad_gain_ffn = write_out(
        order,
        write_attn(False),
        flights + [three],
        attn_shapes,
        attn_buffers,
        small=[((1, features), wide)] * 2,
        into=grads_attn,
    )
    return (
        block_out,
        grad_tokens,
        grad_gain_attn.reshape(-1),
        grad_w_query,
        grad_w_key,
        grad_w_value,
        grad_w_out,
        grad_gain_ffn.reshape(-1),
        grads_ffn[0].T,
        grads_ffn[1].T,
        grads_ffn[2],
    )


def solution(mesh):
    fine = Mesh(mesh.devices.reshape(2, 4, 2, TP), SEQ_AXES + ("tp",))
    return jax.shard_map(
        on_device,
        mesh=fine,
        in_specs=(
            P(SEQ_AXES, None),
            P(),
            P(None, "tp"),
            P(None, "tp"),
            P(None, "tp"),
            P("tp", None),
            P(),
            P(None, "tp"),
            P(None, "tp"),
            P("tp", None),
            P(SEQ_AXES, None),
        ),
        out_specs=(
            P(SEQ_AXES, None),
            P(SEQ_AXES, None),
            P("tp"),
            P(None, "tp"),
            P(None, "tp"),
            P(None, "tp"),
            P("tp", None),
            P("tp"),
            P(None, "tp"),
            P(None, "tp"),
            P("tp", None),
        ),
        check_vma=False,
    )
```

```python
import jax
import jax.numpy as jnp
from jax import lax
from jax.experimental import pallas as pl
from jax.experimental.pallas import tpu as pltpu
from jax.sharding import Mesh
from jax.sharding import PartitionSpec as P

HD = 128
W = 1024
SEQ = 16
TP = 8
Z_FLIPS = (2, 1, 3)
FFN_PIECES = (
    ((0, 0, 688), (1, 0, 128)),
    ((1, 128, 688), (2, 0, 256)),
    ((2, 256, 688),),
)
FFN_ROWS = (816, 816, 432)

epsilon = 1e-06
masked_value = -1e30
low = jnp.bfloat16
wide = jnp.float32


def seq_pairs(step):
    pairs = []
    for x_hi in range(2):
        for y in range(4):
            for core in range(2):
                to = step(x_hi, y, core)
                if to is not None:
                    pairs.append((x_hi * 8 + y * 2 + core, to[0] * 8 + to[1] * 2 + to[2]))
    return pairs


EXCHANGE = {
    "core": seq_pairs(lambda x, y, c: (x, y, 1 - c)),
    "y1": seq_pairs(lambda x, y, c: (x, y ^ 1, c)),
    "y3": seq_pairs(lambda x, y, c: (x, y ^ 3, c)),
    "x": seq_pairs(lambda x, y, c: (1 - x, y, c)),
}

SEQ_AXES = ("x_hi", "y", "core")


def by_seq(value, name):
    return lax.ppermute(value, SEQ_AXES, EXCHANGE[name])


def by_tp(value, flip):
    return lax.ppermute(value, "tp", [(k, k ^ flip) for k in range(TP)])


def shifted(value, steps):
    pairs = [(k, k + steps) for k in range(SEQ) if 0 <= k + steps < SEQ]
    return lax.ppermute(value, SEQ_AXES, pairs)


def z_exchange(blocks):
    return [by_tp(block, 2 * flip) for flip, block in zip(Z_FLIPS, blocks)]


def z_spread(block):
    return [by_tp(block, 2 * flip) for flip in Z_FLIPS]


def gather_tp(rows):
    mine = [by_tp(rows, 2 * flip) for flip in Z_FLIPS]
    other = by_tp(rows, 1)
    theirs = [by_tp(other, 2 * flip) for flip in Z_FLIPS]
    return [rows, other] + mine + theirs


def places():
    x_hi = lax.axis_index("x_hi")
    y = lax.axis_index("y")
    core = lax.axis_index("core")
    tp = lax.axis_index("tp")
    return {
        "seq": x_hi * 8 + y * 2 + core,
        "tp": tp,
        "z": tp >> 1,
        "x_low": tp & 1,
        "core": core,
        "y1": (y & 1) ^ (y >> 1),
        "y3": y >> 1,
        "x": x_hi,
    }


class Order:
    def __init__(self):
        self.last = None

    def __call__(self, body, ins, outs, needs=(), scratch=(), temporary=2 << 20, cost=0.3):
        ins = list(ins)
        needs = list(needs)
        if self.last is not None:
            needs.append(self.last)
        skip = len(ins) + len(needs)
        outs = list(outs) + [((8, 128), wide)]
        out_shape = [jax.ShapeDtypeStruct(shape, kind) for shape, kind in outs]
        count = len(ins)

        def run(*refs):
            given = refs[skip : skip + len(outs)]
            given[-1][...] = jnp.zeros_like(given[-1])
            body(refs[:count], given[:-1], refs[skip + len(outs) :])

        def size(shape, kind):
            lanes = -(-shape[-1] // 128) * 128
            total = lanes * jnp.dtype(kind).itemsize
            for extent in shape[:-1]:
                total *= max(extent, 1)
            return total

        held = (
            sum(size(value.shape, value.dtype) for value in ins)
            + sum(size(shape, kind) for shape, kind in outs)
            + sum(size(shape, kind) for shape, kind in scratch)
        )
        result = pl.pallas_call(
            run,
            out_shape=out_shape,
            in_specs=[pl.BlockSpec(memory_space=pltpu.VMEM)] * count
            + [pl.BlockSpec(memory_space=pl.ANY)] * len(needs),
            out_specs=[pl.BlockSpec(memory_space=pltpu.VMEM)] * len(outs),
            scratch_shapes=[pltpu.VMEM(shape, kind) for shape, kind in scratch],
            compiler_params=pltpu.CompilerParams(vmem_limit_bytes=held + temporary),
            cost_estimate=pl.CostEstimate(
                flops=int(cost * 1e9), bytes_accessed=0, transcendentals=0
            ),
            name=body.__name__,
        )(*ins, *needs)
        self.last = result[-1]
        return result[:-1]


def hold(order, values, strict=False):
    values = list(values)
    needs = [order.last]
    if strict:
        values, needs = values + needs, []

    def run(*refs):
        pass

    result = pl.pallas_call(
        run,
        out_shape=[jax.ShapeDtypeStruct(value.shape, value.dtype) for value in values],
        in_specs=[pl.BlockSpec(memory_space=pl.ANY)] * (len(values) + len(needs)),
        out_specs=[pl.BlockSpec(memory_space=pl.ANY)] * len(values),
        input_output_aliases={k: k for k in range(len(values))},
        compiler_params=pltpu.CompilerParams(vmem_limit_bytes=1 << 20),
        cost_estimate=pl.CostEstimate(flops=0, bytes_accessed=0, transcendentals=0),
    )(*values, *needs)
    if strict:
        order.last = result[-1]
        result = result[:-1]
    return result


def dot(left, right):
    return jnp.dot(left, right, preferred_element_type=wide)


def dot_rows(left, right):
    return lax.dot_general(left, right, (((1,), (1,)), ((), ())), preferred_element_type=wide)


def dot_cols(left, right):
    return lax.dot_general(left, right, (((0,), (0,)), ((), ())), preferred_element_type=wide)


def rms_factor(rows):
    return lax.rsqrt(jnp.mean(rows * rows, axis=-1, keepdims=True) + epsilon)


def norm_back(grad_normed, unit_rows, factor, gain_vec):
    scaled = grad_normed * gain_vec
    return factor * (scaled - unit_rows * jnp.mean(scaled * unit_rows, axis=-1, keepdims=True))


def span(index, size):
    return pl.ds(pl.multiple_of(index * size, size), size)


def eight_blocks(at, size):
    here = [span(2 * at["z"] + x, size) for x in (at["x_low"], 1 - at["x_low"])]
    mine = [span(2 * (at["z"] ^ flip) + at["x_low"], size) for flip in Z_FLIPS]
    theirs = [span(2 * (at["z"] ^ flip) + 1 - at["x_low"], size) for flip in Z_FLIPS]
    return here + mine + theirs


def write_eight(partial, at, outs):
    for place, out in zip(eight_blocks(at, outs[0].shape[0]), outs):
        out[...] = partial[place, :]


def read_eight(whole, at, blocks):
    for place, block in zip(eight_blocks(at, blocks[0].shape[0]), blocks):
        whole[place, :] = block[...]


def read_pairs(whole, z, blocks):
    size = blocks[0].shape[0]
    for flip, block in zip((0,) + Z_FLIPS, blocks):
        whole[span(z ^ flip, size), :] = block[...]


def normed_kernel(ins, outs, _):
    tokens, gain, w_key, w_value = ins
    normed, key_value = outs
    inputs = tokens[...].astype(wide)
    rows = (inputs * rms_factor(inputs) * gain[...]).astype(low)
    normed[...] = rows
    features = w_key.shape[1]
    key_value[:, :features] = dot(rows, w_key[...]).astype(low)
    key_value[:, features:] = dot(rows, w_value[...]).astype(low)


def project_kernel(ins, outs, _):
    outs[0][...] = dot(ins[0][...], ins[1][...]).astype(low)


def last_block(at, own_of_partner, four_of_partner, way):
    near = at["core"] == (0 if way == 1 else 1)
    return jnp.where(near, four_of_partner, own_of_partner)


def seen_scores(scores, order, distance, gap, inside):
    if order == 0:
        return jnp.where(gap >= 0, scores, masked_value)
    if order == 3:
        return jnp.where((gap < 0) & inside, scores, masked_value)
    return jnp.where(inside, scores, masked_value)


def distances(at, way):
    near = at["core"] == (0 if way == 1 else 1)
    return [0, 2, jnp.where(near, 1, 3), 4, jnp.where(near, 3, 1)]


def gap_of(rows, flipped=False):
    first = lax.broadcasted_iota(jnp.int32, (rows, rows), 0)
    second = lax.broadcasted_iota(jnp.int32, (rows, rows), 1)
    return second - first if flipped else first - second


def attend_kernel(ins, outs, scratch):
    query, own, two, across, four, partner_own, partner_four, w_out = ins
    heads_out, log_out = outs[:2]
    rows, features = query.shape
    at = places()
    scale = HD ** (-0.5)
    gap = gap_of(rows)
    away = distances(at, 1)
    blocks = [own[...], two[...], across[...], four[...]]
    blocks.append(last_block(at, partner_own[...], partner_four[...], 1))
    logs = []
    mixed = []
    for head in range(features // HD):
        here = slice(head * HD, (head + 1) * HD)
        there = slice(features + head * HD, features + (head + 1) * HD)
        scores = [
            seen_scores(
                dot_rows(query[:, here], block[:, here]) * scale,
                order,
                distance,
                gap,
                at["seq"] >= distance,
            )
            for order, (block, distance) in enumerate(zip(blocks, away))
        ]
        peak = scores[0].max(axis=-1, keepdims=True)
        for part in scores[1:]:
            peak = jnp.maximum(peak, part.max(axis=-1, keepdims=True))
        raised = [jnp.exp(part - peak) for part in scores]
        total = raised[0].sum(axis=-1, keepdims=True)
        for part in raised[1:]:
            total = total + part.sum(axis=-1, keepdims=True)
        inverse = 1.0 / total
        out = dot((raised[0] * inverse).astype(low), blocks[0][:, there])
        for part, block in zip(raised[1:], blocks[1:]):
            out = out + dot((part * inverse).astype(low), block[:, there])
        mixed.append(out.astype(low))
        logs.append(peak + jnp.log(total))
    for head, out in enumerate(mixed):
        heads_out[:, head * HD : (head + 1) * HD] = out
    lane = lax.broadcasted_iota(jnp.int32, (rows, HD), 1)
    log_out[...] = jnp.where(lane < 64, logs[0], logs[1])
    partial = scratch[0]
    partial[...] = dot(heads_out[...], w_out[...]).astype(low)
    write_eight(partial, at, outs[2:])


def sum_kernel(ins, outs, _):
    total = ins[0][...].astype(wide)
    for block in ins[1:]:
        total = total + block[...].astype(wide)
    outs[0][...] = total.astype(outs[0].dtype)


def sum_refs(refs):
    total = refs[0][...].astype(wide)
    for ref in refs[1:]:
        total = total + ref[...].astype(wide)
    return total


def norm_rows_kernel(ins, outs, _):
    tokens, gain = ins[5:]
    hidden, normed = outs
    at = places()
    rows = tokens[span(at["tp"], hidden.shape[0]), :].astype(wide) + sum_refs(ins[:5])
    hidden[...] = rows
    normed[...] = (rows * rms_factor(rows) * gain[...]).astype(low)


def pair_kernel(ins, outs, _):
    at = places()
    size = ins[0].shape[0]
    outs[0][span(at["x_low"], size), :] = ins[0][...]
    outs[0][span(1 - at["x_low"], size), :] = ins[1][...]


def ffn_kernel(ins, outs, scratch):
    w_gate, w_up, w_down, cotangent = ins[8:]
    normed, activated, grad_gate, grad_up = outs[:4]
    at = places()
    read_eight(normed, at, ins[:8])
    rows = normed[...]
    gate_pre = dot_rows(rows, w_gate[...])
    up_pre = dot_rows(rows, w_up[...])
    grad_act = dot_rows(cotangent[...], w_down[...])
    sigmoid = jax.nn.sigmoid(gate_pre)
    silu = gate_pre * sigmoid
    activated[...] = (silu * up_pre).astype(low)
    grad_gate[...] = (grad_act * up_pre * sigmoid * (1.0 + gate_pre * (1.0 - sigmoid))).astype(low)
    grad_up[...] = (grad_act * silu).astype(low)
    partial = scratch[0]
    partial[...] = (dot(grad_gate[...], w_gate[...]) + dot(grad_up[...], w_up[...])).astype(low)
    write_eight(partial, at, outs[4:])


def grad_rows_kernel(ins, outs, _):
    hidden, cotangent, gain = ins[5:]
    grad_hidden, grad_low, gain_part = outs
    at = places()
    grad_normed = sum_refs(ins[:5])
    rows = hidden[...]
    factor = rms_factor(rows)
    unit = rows * factor
    gain_part[...] = jnp.sum(grad_normed * unit, axis=0, keepdims=True)
    grad = cotangent[span(at["tp"], rows.shape[0]), :].astype(wide) + norm_back(
        grad_normed, unit, factor, gain[...]
    )
    grad_hidden[...] = grad
    grad_low[...] = grad.astype(low)


def heads_kernel(ins, outs, _):
    w_out, logs, heads_out = ins[4:]
    grad_hidden, grad_heads = outs
    read_pairs(grad_hidden, places()["z"], ins[:4])
    grad = dot_rows(grad_hidden[...], w_out[...]).astype(low)
    rows, features = grad.shape
    grad_heads[:, :features] = grad
    product = grad.astype(wide) * heads_out[...].astype(wide)
    values = [logs[:, :1], logs[:, 64:65]]
    for head in range(2):
        values.append(jnp.sum(product[:, head * HD : (head + 1) * HD], axis=-1, keepdims=True))
    group = lax.broadcasted_iota(jnp.int32, (rows, HD), 1) >> 3
    both = jnp.zeros((rows, HD), wide)
    for k, value in enumerate(values):
        both = jnp.where((group & 3) == k, value, both)
    first = both.astype(low).astype(wide)
    second = (both - first).astype(low).astype(wide)
    rest = jnp.where(group < 8, second, both - first - second)
    grad_heads[:, features:] = jnp.where(group < 4, first, rest).astype(low)


def grad_query_kernel(ins, outs, _):
    query_all, heads_out, logs, grad_heads, own, two, across, four, partner_own, partner_four = ins
    rows, features = query_all.shape
    at = places()
    scale = HD ** (-0.5)
    gap = gap_of(rows)
    away = distances(at, 1)
    blocks = [own[...], two[...], across[...], four[...]]
    blocks.append(last_block(at, partner_own[...], partner_four[...], 1))
    for head in range(features // HD):
        here = slice(head * HD, (head + 1) * HD)
        there = slice(features + head * HD, features + (head + 1) * HD)
        query = query_all[:, here]
        grad = grad_heads[:, here]
        log_total = logs[:, head * 64 : head * 64 + 1]
        inner = jnp.sum(
            grad.astype(wide) * heads_out[:, here].astype(wide), axis=-1, keepdims=True
        )
        total = jnp.zeros((rows, HD), wide)
        for order, (block, distance) in enumerate(zip(blocks, away)):
            scores = seen_scores(
                dot_rows(query, block[:, here]) * scale,
                order,
                distance,
                gap,
                at["seq"] >= distance,
            )
            weights = jnp.exp(scores - log_total)
            grad_scores = weights * (dot_rows(grad, block[:, there]) - inner)
            total = total + dot(grad_scores.astype(low), block[:, here])
        outs[0][:, here] = (total * scale).astype(low)


def grad_key_kernel(ins, outs, scratch):
    key_value = ins[0]
    sides = ins[1:7]
    grads = ins[7:13]
    grad_key, grad_value = outs
    rows, features = grad_key.shape
    at = places()
    scale = HD ** (-0.5)
    gap = gap_of(rows, flipped=True)
    away = distances(at, -1)
    side_blocks = [side[...] for side in sides[:4]]
    side_blocks.append(last_block(at, sides[4][...], sides[5][...], -1))
    grad_blocks = [grad[...] for grad in grads[:4]]
    grad_blocks.append(last_block(at, grads[4][...], grads[5][...], -1))
    sums = [grad[:, features:].astype(wide).T for grad in grad_blocks]
    for head in range(features // HD):
        here = slice(head * HD, (head + 1) * HD)
        there = slice(features + head * HD, features + (head + 1) * HD)
        key = key_value[:, here]
        value = key_value[:, there]
        total_key = jnp.zeros((rows, HD), wide)
        total_value = jnp.zeros((rows, HD), wide)
        for order, (side, grad_all, logs, distance) in enumerate(
            zip(side_blocks, grad_blocks, sums, away)
        ):
            query = side[:, here]
            grad = grad_all[:, here]
            log_total, inner = [
                logs[8 * k : 8 * k + 1]
                + logs[32 + 8 * k : 33 + 8 * k]
                + logs[64 + 8 * k : 65 + 8 * k]
                for k in (head, 2 + head)
            ]
            scores = seen_scores(
                dot_rows(key, query) * scale, order, distance, gap, at["seq"] + distance < SEQ
            )
            weights = jnp.exp(scores - log_total)
            total_value = total_value + dot(weights.astype(low), grad)
            grad_scores = weights * (dot_rows(value, grad) - inner)
            total_key = total_key + dot(grad_scores.astype(low), query)
        grad_key[:, here] = (total_key * scale).astype(low)
        grad_value[:, here] = total_value.astype(low)


def back_kernel(ins, outs, scratch):
    grad_query, grad_key, grad_value, w_query, w_key, w_value, tokens, gain_ffn_part, ffn_partial = ins
    keep_one, keep_two, send_one, send_two = outs
    at = places()
    rows = tokens.shape[0]
    back = (
        dot_rows(grad_query[...], w_query[...])
        + dot_rows(grad_key[...], w_key[...])
        + dot_rows(grad_value[...], w_value[...])
    )
    inputs = tokens[...].astype(wide)
    gain_attn_part = jnp.sum(back * (inputs * rms_factor(inputs)), axis=0, keepdims=True)
    partial = scratch[0]
    width = tokens.shape[1]
    partial[:, :width] = back.astype(low)
    share = rows // TP
    cells = width // TP // HD
    for k in range(TP):
        parts = [
            gain[:, (k * cells + cell) * HD : (k * cells + cell + 1) * HD]
            for gain in (gain_attn_part, gain_ffn_part[...])
            for cell in range(cells)
        ]
        parts.append(jnp.zeros((share - len(parts), HD), wide))
        partial[k * share : (k + 1) * share, width:] = jnp.concatenate(parts, axis=0).astype(low)
    size = rows // 4
    z = at["z"]
    cut = width // 2
    for out, first, flips in (
        (keep_one, 0, (0, 3)),
        (send_one, 0, (1, 2)),
        (keep_two, cut, (0, 1)),
        (send_two, cut, (3, 2)),
    ):
        for k, flip in enumerate(flips):
            here = slice(k * size, (k + 1) * size)
            there = span(z ^ flip, size)
            out[here, :cut] = partial[there, first : first + cut]
            out[here, cut:width] = ffn_partial[there, first : first + cut]
            if first > 0:
                out[here, width:] = partial[there, width:]


def sum_middle_kernel(ins, outs, _):
    for keep, arrived, stay, send in ((ins[0], ins[1], outs[0], outs[1]), (ins[2], ins[3], outs[2], outs[3])):
        size = stay.shape[0]
        stay[...] = keep[:size, :].astype(wide) + arrived[:size, :].astype(wide)
        send[...] = (keep[size:, :].astype(wide) + arrived[size:, :].astype(wide)).astype(low)


def sum_last_kernel(ins, outs, _):
    keep, send = outs
    at = places()
    size = keep.shape[0]
    width = ins[0].shape[1]
    cut = width // 2
    for out, index in ((keep, at["x_low"]), (send, 1 - at["x_low"])):
        here = span(index, size)
        first = (ins[0][here, :] + ins[1][here, :].astype(wide)).astype(out.dtype)
        second = (ins[2][here, :] + ins[3][here, :].astype(wide)).astype(out.dtype)
        out[:, :cut] = first[:, :cut]
        out[:, cut:width] = second[:, :cut]
        out[:, width : width + cut] = first[:, cut:]
        out[:, width + cut : 2 * width] = second[:, cut:width]
        out[:, 2 * width :] = second[:, width:]


def last_rows_kernel(ins, outs, _):
    keep, arrived, grad_hidden, hidden, tokens, gain = ins
    rows_out, gains = outs
    width = hidden.shape[1]
    at = places()
    inputs = tokens[span(at["tp"], keep.shape[0]), :].astype(wide)
    factor = rms_factor(inputs)
    grad_normed = keep[:, :width] + arrived[:, :width].astype(wide)
    grad = grad_hidden[...] + norm_back(grad_normed, inputs * factor, factor, gain[...])
    rows_out[:, :width] = grad.astype(low)
    rows_out[:, width:] = (
        hidden[...] + keep[:, width : 2 * width] + arrived[:, width : 2 * width].astype(wide)
    ).astype(low)
    sums = keep[:, 2 * width :] + arrived[:, 2 * width :].astype(wide)
    gains[...] = jnp.zeros_like(gains)
    gains[:, : sums.shape[1]] = sums[: gains.shape[0], :].astype(low)


def last_pair_kernel(ins, outs, _):
    at = places()
    size = ins[0].shape[0]
    width = outs[0].shape[1]
    for value, index in zip(ins, (at["x_low"], 1 - at["x_low"])):
        outs[0][span(index, size), :] = value[:, :width]
        outs[1][span(index, size), :] = value[:, width:]


def stack_kernel(ins, outs, _):
    for k, out in enumerate(outs):
        size = ins[2 * k].shape[0]
        out[:size, :] = ins[2 * k][...]
        out[size:, :] = ins[2 * k + 1][...]


def token_outputs_kernel(ins, outs, _):
    z = places()["z"]
    size = ins[0].shape[0] // 2
    for out, own, arrived, flips in (
        (outs[0], ins[0], ins[1], (0, 1, 3, 2)),
        (outs[1], ins[2], ins[3], (0, 3, 1, 2)),
    ):
        blocks = (own[:size, :], own[size:, :], arrived[:size, :], arrived[size:, :])
        for flip, block in zip(flips, blocks):
            out[span(z ^ flip, size), :] = block.astype(out.dtype)


def part(ref, axis, start, size):
    return ref[:, pl.ds(start, size)] if axis == 1 else ref[pl.ds(start, size), :]


def put(ref, axis, start, size, value):
    if axis == 1:
        ref[:, pl.ds(start, size)] = value
    else:
        ref[pl.ds(start, size), :] = value


def split_op(keep, arrived, bit, axis):
    shape = list(keep.shape)
    shape[axis] //= 2
    size = shape[axis]

    def body(at, ins, outs):
        for out, index in zip(outs, (at[bit], 1 - at[bit])):
            start = pl.multiple_of(index * size, size)
            out[...] = (
                part(ins[0], axis, start, size).astype(wide)
                + part(ins[1], axis, start, size).astype(wide)
            ).astype(low)

    return body, [keep, arrived], [(tuple(shape), low)] * 2


def add_op(keep, arrived):
    def body(at, ins, outs):
        outs[0][...] = (ins[0][...].astype(wide) + ins[1][...].astype(wide)).astype(
            outs[0].dtype
        )

    return body, [keep, arrived], [(keep.shape, keep.dtype)]


def join_op(own, arrived, bit, axis, kind=low):
    shape = list(own.shape)
    size = shape[axis]
    shape[axis] *= 2

    def body(at, ins, outs):
        for value, index in zip(ins, (at[bit], 1 - at[bit])):
            start = pl.multiple_of(index * size, size)
            put(outs[0], axis, start, size, value[...].astype(kind))

    return body, [own, arrived], [(tuple(shape), kind)]


def add_tail_op(keep, arrived, tail):
    rows, width = keep.shape

    def body(at, ins, outs):
        outs[0][:rows, :] = (ins[0][...].astype(wide) + ins[1][...].astype(wide)).astype(low)
        outs[0][rows:, :] = ins[2][...]

    return body, [keep, arrived, tail], [((rows + tail.shape[0], width), low)]


def join_tail_op(own, arrived, bit, tail):
    rows, width = own.shape
    size = rows - tail

    def body(at, ins, outs):
        for value, index in zip(ins, (at[bit], 1 - at[bit])):
            outs[0][span(index, size), :] = value[:size, :]
        outs[0][2 * size :, :] = (
            ins[0][size:, :].astype(wide) + ins[1][size:, :].astype(wide)
        ).astype(low)

    return body, [own, arrived], [((2 * size + tail, width), low)]


def run_ops(order, ops, needs=()):
    ins = [value for _, values, _ in ops for value in values]
    outs = [out for _, _, shapes in ops for out in shapes]

    def body(in_refs, out_refs, _):
        at = places()
        first = last = 0
        for step, values, shapes in ops:
            step(
                at,
                in_refs[first : first + len(values)],
                out_refs[last : last + len(shapes)],
            )
            first += len(values)
            last += len(shapes)

    flat = list(order(body, ins, outs, needs))
    result = []
    for _, _, shapes in ops:
        result.append(flat[: len(shapes)])
        flat = flat[len(shapes) :]
    return result


FFN_ORDERS = (("y1", "y3", "x"), ("y3", "x", "y1"), ("x", "y1", "y3"))


def ffn_terms(ins, k):
    terms = []
    first = 0
    for operand, start, stop in FFN_PIECES[k]:
        last = first + stop - start
        terms.append((first, last, ins[operand][:, start:stop], ins[4 if operand == 2 else 3]))
        first = last
    return terms


def ffn_send_kernel(arrays):
    def ffn_send(ins, outs, _):
        out = outs[0]
        half = out.shape[1]
        other = 1 - places()["core"]
        base = 0
        for k in arrays:
            for first, last, left, right in ffn_terms(ins, k):
                out[base + first : base + last, :] = dot_cols(
                    left, right[:, span(other, half)]
                ).astype(low)
            base += FFN_ROWS[k]

    return ffn_send


def ffn_keep_kernel(arrays):
    def ffn_keep(ins, outs, _):
        at = places()
        arrived = ins[5]
        base = 0
        for k, keep, send in zip(arrays, outs[0::2], outs[1::2]):
            size = keep.shape[1]
            bit = at[FFN_ORDERS[k][0]]
            for out, index in ((keep, bit), (send, 1 - bit)):
                start = pl.multiple_of((2 * at["core"] + index) * size, size)
                for first, last, left, right in ffn_terms(ins, k):
                    own = dot_cols(left, right[:, pl.ds(start, size)])
                    got = arrived[base + first : base + last, span(index, size)]
                    out[first:last, :] = (own + got.astype(wide)).astype(low)
            base += FFN_ROWS[k]

    return ffn_keep


def attn_terms(ins):
    normed, grad_hidden, grad_query, grad_key, grad_value, heads_out = ins
    half = heads_out.shape[1] // 2
    return [
        [(normed, grad_query[...]), (grad_hidden, heads_out[:, :half])],
        [(normed, grad_key[...]), (grad_hidden, heads_out[:, half:])],
        [(normed, grad_value[...])],
    ]


def attn_half_kernel(own):
    def attn_half(ins, outs, _):
        out = outs[0]
        half = out.shape[0]
        index = places()["core"] if own else 1 - places()["core"]
        first = 0
        for terms in attn_terms(ins):
            for left, right in terms:
                last = first + right.shape[1]
                out[:, first:last] = dot_cols(left[:, span(index, half)], right).astype(out.dtype)
                first = last

    return attn_half


def packed_rows(rows, lanes, width):
    across = width // 128
    full, rest = divmod(lanes // 128, across)
    if rest == 1 and rows % across == 0:
        return rows * full + rows // across
    return rows * (full + (rest > 0))


def place_cells(rows, lanes, width):
    across = width // 128
    cells = lanes // 128
    runs = []
    full = cells // across
    for k in range(full * across):
        runs.append((0, k * 128, (k // across) * rows, (k % across) * 128, rows))
    rest = cells - full * across
    if rest and rows % across == 0 and rest == 1:
        size = rows // across
        for k in range(across):
            runs.append((k * size, full * across * 128, full * rows, k * 128, size))
    elif rest:
        for k in range(rest):
            runs.append((0, (full * across + k) * 128, full * rows, k * 128, rows))
    return runs


def pack(message, base, value):
    rows, lanes = value.shape
    for row, lane, to_row, to_lane, size in place_cells(rows, lanes, message.shape[1]):
        message[base + to_row : base + to_row + size, to_lane : to_lane + 128] = value[
            row : row + size, lane : lane + 128
        ]


def add_packed(keep, message, base, lanes):
    rows = keep.shape[0]
    columns = [[] for _ in range(lanes // 128)]
    for row, lane, from_row, from_lane, size in place_cells(rows, lanes, message.shape[1]):
        here = keep[row : row + size, lane : lane + 128].astype(wide)
        there = message[base + from_row : base + from_row + size, from_lane : from_lane + 128]
        columns[lane // 128].append(here + there.astype(wide))
    return [jnp.concatenate(parts, axis=0) if len(parts) > 1 else parts[0] for parts in columns]


ATTN_ORDERS = (("y1", "y3", "x"), ("y3", "x", "y1"), ("x", "y1", "y3"))
WAYS = ("y1", "y3", "x")


def tops(step):
    return {orders[step]: rows for orders, rows in zip(FFN_ORDERS, FFN_ROWS)}


def round_one_kernel(ins, outs, _):
    at = places()
    own, arrived = ins[6:]
    messages = dict(zip(WAYS, outs[:3]))
    for k in range(3):
        way = FFN_ORDERS[k][2]
        size = outs[6 + k].shape[1]
        for out, index in ((outs[6 + k], at[way]), (messages[way], 1 - at[way])):
            start = pl.multiple_of(index * size, size)
            out[: FFN_ROWS[k], :] = (
                ins[k][:, pl.ds(start, size)].astype(wide)
                + ins[3 + k][:, pl.ds(start, size)].astype(wide)
            ).astype(low)
    base = 0
    for k in range(3):
        keep = outs[3 + k]
        size, lanes = keep.shape
        way = ATTN_ORDERS[k][0]
        for kept, index in ((True, at[way]), (False, 1 - at[way])):
            here = span(index, size)
            for lane in range(0, lanes, 128):
                there = slice(base + lane, base + lane + 128)
                value = (own[here, there] + arrived[here, there].astype(wide)).astype(low)
                if kept:
                    keep[:, lane : lane + 128] = value
                else:
                    row = tops(2)[way] + lane // 128 * size
                    messages[way][row : row + size, :] = value
        base += lanes


def attn_step(at, keeps, arrived, top, step, outs, messages, message_top):
    for k, (keep, out) in enumerate(zip(keeps, outs)):
        came, way = ATTN_ORDERS[k][step - 1], ATTN_ORDERS[k][step]
        columns = add_packed(keep, arrived[came], top[came], keep.shape[1])
        size = keep.shape[0] // 2
        first = at[way] == 0
        go = []
        for lane, column in enumerate(columns):
            one, two = column[:size, :], column[size:, :]
            out[:, lane * 128 : (lane + 1) * 128] = jnp.where(first, one, two).astype(low)
            go.append(jnp.where(first, two, one).astype(low))
        pack(messages[way], message_top[way], jnp.concatenate(go, axis=1))


def ffn_joined(at, sent, arrived, step, messages):
    for k, rows in enumerate(FFN_ROWS):
        back = FFN_ORDERS[k][step]
        message = messages[FFN_ORDERS[k][step - 1]]
        width = sent[back].shape[1]
        for value, index in ((sent[back], at[back]), (arrived[back], 1 - at[back])):
            start = pl.multiple_of(index * width, width)
            message[:rows, pl.ds(start, width)] = value[:rows, :]


def round_two_kernel(ins, outs, _):
    at = places()
    arrived, messages = dict(zip(WAYS, ins[:3])), dict(zip(WAYS, outs[:3]))
    for k, rows in enumerate(FFN_ROWS):
        way = FFN_ORDERS[k][2]
        messages[way][:rows, :] = (
            ins[3 + k][...].astype(wide) + arrived[way][:rows, :].astype(wide)
        ).astype(low)
    attn_step(at, ins[6:9], arrived, tops(2), 1, outs[3:], messages, tops(2))


def round_three_kernel(ins, outs, _):
    at = places()
    sent, arrived = dict(zip(WAYS, ins[:3])), dict(zip(WAYS, ins[3:6]))
    messages = dict(zip(WAYS, outs[:3]))
    ffn_joined(at, sent, arrived, 2, messages)
    attn_step(at, ins[6:9], arrived, tops(2), 2, outs[3:], messages, tops(1))


def round_four_kernel(ins, outs, _):
    at = places()
    sent, arrived = dict(zip(WAYS, ins[:3])), dict(zip(WAYS, ins[3:6]))
    messages = dict(zip(WAYS, outs))
    ffn_joined(at, sent, arrived, 1, messages)
    for k in range(3):
        way = ATTN_ORDERS[k][2]
        keep = ins[6 + k]
        rows, lanes = keep.shape
        first = tops(0)[way]
        for lane, column in enumerate(add_packed(keep, arrived[way], tops(1)[way], lanes)):
            messages[way][first : first + rows, lane * 128 : (lane + 1) * 128] = column.astype(low)
        if k == 2:
            gains = ins[9]
            messages[way][first + rows : first + rows + gains.shape[0], :lanes] = gains[...]


def round_five_kernel(ins, outs, _):
    at = places()
    sent, arrived = dict(zip(WAYS, ins[:3])), dict(zip(WAYS, ins[3:]))
    for k, out in enumerate(outs):
        way = ATTN_ORDERS[k][2]
        first = tops(0)[way]
        lanes = out.shape[1]
        rows = 128
        for value, index in ((sent[way], at[way]), (arrived[way], 1 - at[way])):
            out[span(index, rows), :] = value[first : first + rows, :lanes]
        if k == 2:
            tail = slice(first + rows, first + rows + out.shape[0] - 2 * rows)
            out[2 * rows :, :] = (
                sent[way][tail, :lanes].astype(wide) + arrived[way][tail, :lanes].astype(wide)
            ).astype(low)


def ffn_halves_kernel(ins, outs, _):
    at = places()
    sent, arrived = dict(zip(WAYS, ins[:3])), dict(zip(WAYS, ins[3:]))
    base = 0
    for k, rows in enumerate(FFN_ROWS):
        way = FFN_ORDERS[k][0]
        width = sent[way].shape[1]
        for value, index in ((sent[way], at[way]), (arrived[way], 1 - at[way])):
            start = pl.multiple_of(index * width, width)
            outs[0][base : base + rows, pl.ds(start, width)] = value[:rows, :]
        base += rows


def write_out(order, body, ins, outs, buffers, small=(), into=None, cost=0.3):
    ins, old = list(ins), list(into or [])
    needs = [order.last]
    count, many = len(ins), len(outs)
    skip = count + len(old) + len(needs)
    small = list(small) + [((8, 128), wide)]

    def run(*refs):
        targets = refs[skip : skip + many]
        others = refs[skip + many : skip + many + len(small)]
        scratch = refs[skip + many + len(small) :]
        held, arrived = scratch[: len(buffers)], scratch[len(buffers)]
        others[-1][...] = jnp.zeros_like(others[-1])
        copies = []
        for k, (value, target) in enumerate(body(places(), refs[:count], targets, others[:-1])):
            held[k][...] = value
            copies.append(pltpu.make_async_copy(held[k], target, arrived.at[k]))
            copies[-1].start()
        for copy in copies:
            copy.wait()

    size = sum(shape[0] * shape[1] * 4 for shape in buffers) + sum(
        value.size * value.dtype.itemsize for value in ins
    )
    result = pl.pallas_call(
        run,
        out_shape=[jax.ShapeDtypeStruct(shape, wide) for shape in outs]
        + [jax.ShapeDtypeStruct(shape, kind) for shape, kind in small],
        in_specs=[pl.BlockSpec(memory_space=pltpu.VMEM)] * count
        + [pl.BlockSpec(memory_space=pltpu.HBM)] * len(old)
        + [pl.BlockSpec(memory_space=pl.ANY)] * len(needs),
        out_specs=[pl.BlockSpec(memory_space=pltpu.HBM)] * many
        + [pl.BlockSpec(memory_space=pltpu.VMEM)] * len(small),
        scratch_shapes=[pltpu.VMEM(shape, wide) for shape in buffers]
        + [pltpu.SemaphoreType.DMA((len(buffers),))],
        input_output_aliases={count + k: k for k in range(len(old))},
        compiler_params=pltpu.CompilerParams(vmem_limit_bytes=size + (6 << 20)),
        cost_estimate=pl.CostEstimate(
            flops=int(cost * 1e9), bytes_accessed=0, transcendentals=0
        ),
        name=body.__name__,
    )(*ins, *old, *needs)
    order.last = result[-1]
    return list(result[:-1])


def write_ffn(own):
    def write_ffn_half(at, ins, targets, _):
        half = ins[0].shape[1]
        index = at["core"] if own else 1 - at["core"]
        rows = targets[0].shape[0]
        for k, target in enumerate(targets):
            yield ins[0][k * rows : (k + 1) * rows, :].astype(wide), target.at[:, span(index, half)]

    return write_ffn_half


def write_attn(own):
    def write_attn_half(at, ins, targets, small):
        one, two, three = ins[:3]
        features = three.shape[1]
        half = one.shape[0]
        here = span(at["core"] if own else 1 - at["core"], half)
        yield one[:, :features].astype(wide), targets[0].at[here, :]
        yield two[:, :features].astype(wide), targets[1].at[here, :]
        yield three[:half, :].astype(wide), targets[2].at[here, :]
        halves = (one[:, features:], two[:, features:])
        out = jnp.concatenate([value.astype(wide).T for value in halves], axis=0)
        yield out, targets[3].at[:, here]
        if not own:
            sums = ins[3][half:, :].astype(wide) + three[half:, :].astype(wide)
            for k, gain in enumerate(small):
                gain[:, :HD] = sums[2 * k : 2 * k + 1, :HD]
                gain[:, HD:] = sums[2 * k + 1 : 2 * k + 2, :HD]

    return write_attn_half


def on_device(
    tokens, gain_attn, w_query, w_key, w_value, w_out, gain_ffn, w_gate, w_up, w_down, cotangent
):
    rows, width = tokens.shape
    features = w_query.shape[1]
    units = w_gate.shape[1]
    share = rows // TP
    quarter = rows // 4
    order = Order()
    gain_attn = gain_attn.reshape(1, width)
    gain_ffn = gain_ffn.reshape(1, width)
    w_gate, w_up = w_gate.T, w_up.T
    blocks_out = [((share, width), low)] * 8
    whole = ((rows, width), low)
    small = ((rows, features), low)
    keep_and_send = [((share, width), wide), ((share, width), low)]

    normed_attn, own = order(
        normed_kernel,
        [tokens, gain_attn, w_key, w_value],
        [whole, ((rows, 2 * features), low)],
        temporary=6 << 20, cost=1.0)
    two, four = shifted(own, 2), shifted(own, 4)
    partner_own = by_seq(own, "core")
    (query,) = order(project_kernel, [normed_attn, w_query], [small])
    query_two, query_four = shifted(query, -2), shifted(query, -4)
    query_partner_own = by_seq(query, "core")
    across = by_seq(two, "core")
    partner_four = by_seq(four, "core")
    keys = [own, two, across, four, partner_own, partner_four]
    heads_out, logs, *blocks = order(
        attend_kernel,
        [query] + keys + [w_out],
        [small, ((rows, HD), wide)] + blocks_out,
        scratch=[whole],
        temporary=6 << 20, cost=2.5,
    )
    theirs = z_exchange(blocks[5:])
    mine = z_exchange(blocks[2:5])
    (send,) = order(
        sum_kernel, [blocks[1], theirs[1], theirs[2], theirs[0]], [((share, width), low)], needs=[query_two, query_four]
    )
    arrived = by_tp(send, 1)
    query_two, query_four = hold(order, [query_two, query_four])
    query_across = by_seq(query_two, "core")
    query_partner_four = by_seq(query_four, "core")
    hidden, normed_rows = order(
        norm_rows_kernel,
        [blocks[0]] + mine + [arrived, tokens, gain_ffn],
        keep_and_send,
        needs=[query_across, query_partner_own, query_partner_four],
    )
    gathered = gather_tp(normed_rows)

    normed_ffn, activated, grad_gate, grad_up, *blocks = order(
        ffn_kernel,
        gathered + [w_gate, w_up, w_down, cotangent],
        [whole] + [((rows, units), low)] * 3 + blocks_out,
        scratch=[whole],
        temporary=12 << 20, cost=5.0)
    theirs = z_exchange(blocks[5:])
    ffn_operands = [grad_gate, grad_up, activated, normed_ffn, cotangent]
    half = width // 2
    (sent,) = order(
        ffn_send_kernel([0, 1, 2]),
        ffn_operands,
        [((3 * units, half), low)],
        temporary=6 << 20, cost=2.5)
    core_arrived = by_seq(sent, "core")
    mine = z_exchange(hold(order, blocks[2:5]))
    parts = order(
        ffn_keep_kernel([0, 1, 2]),
        ffn_operands + [core_arrived],
        [((rows_k, half // 2), low) for rows_k in FFN_ROWS for _ in range(2)],
        temporary=6 << 20, cost=2.5)
    ffn_keeps = list(parts[0::2])
    last_part = parts[5]
    ffn_flights = [by_seq(part, names[0]) for part, names in zip(parts[1:4:2], FFN_ORDERS)]

    def ffn_split(steps, needs=()):
        parts = run_ops(
            order,
            [
                split_op(ffn_keeps[k], ffn_flights[k], FFN_ORDERS[k][step], 1)
                for k, step in steps
            ],
            needs,
        )
        for (k, step), (keep, send) in zip(steps, parts):
            ffn_keeps[k] = keep
            ffn_flights[k] = by_seq(send, FFN_ORDERS[k][step])

    (send,) = order(sum_kernel, [blocks[1]] + theirs, [((share, width), low)], cost=3.0)
    arrived = by_tp(send, 1)
    grad_hidden, grad_low, gain_ffn_part = order(
        grad_rows_kernel,
        [blocks[0]] + mine + [arrived, hidden, cotangent, gain_ffn],
        keep_and_send + [((1, width), wide)], cost=1.5)
    (pair,) = order(
        pair_kernel, [grad_low, by_tp(grad_low, 1)], [((quarter, width), low)], cost=1.5
    )
    gathered = [pair] + z_spread(pair)
    ffn_flights += [by_seq(value, FFN_ORDERS[2][0]) for value in hold(order, [last_part])]
    ffn_split([(0, 1), (1, 1)])
    (ffn_partial,) = order(project_kernel, [activated, w_down], [whole], temporary=6 << 20, cost=1.0)
    grad_hidden_low, grad_heads = order(
        heads_kernel,
        gathered + [w_out, logs, heads_out],
        [whole, ((rows, features + HD), low)], cost=2.0)
    grad_two, grad_four = shifted(grad_heads, -2), shifted(grad_heads, -4)
    (grad_query,) = order(
        grad_query_kernel,
        [query, heads_out, logs, grad_heads] + keys,
        [small],
        temporary=6 << 20, cost=2.0)
    grad_two, grad_four, grad_late = hold(order, [grad_two, grad_four, grad_heads])
    grad_partner_own = by_seq(grad_late, "core")
    grad_across = by_seq(grad_two, "core")
    grad_partner_four = by_seq(grad_four, "core")
    cut = width
    grad_key, grad_value = order(
        grad_key_kernel,
        [own, query, query_two, query_across, query_four, query_partner_own, query_partner_four]
        + [grad_late, grad_two, grad_across, grad_four, grad_partner_own, grad_partner_four],
        [small, small],
        needs=ffn_flights[2:],
        temporary=8 << 20, cost=0.3)
    ffn_split([(2, 1)])

    operands = [normed_attn, grad_hidden_low, grad_query, grad_key, grad_value, heads_out]
    (sent,) = order(
        attn_half_kernel(False), operands, [((width // 2, 4 * features), low)], ffn_flights[:2], temporary=4 << 20, cost=2.5)
    core_arrived = by_seq(sent, "core")
    keep_one, keep_two, send_one, send_two = order(
        back_kernel,
        [grad_query, grad_key, grad_value, w_query, w_key, w_value, tokens, gain_ffn_part, ffn_partial],
        [((2 * quarter, cut), low), ((2 * quarter, cut + HD), low)] * 2,
        scratch=[((rows, width + HD), low)],
        temporary=12 << 20, cost=0.3)
    one_arrived, two_arrived = by_tp(send_one, 2), by_tp(send_two, 6)
    (own_half,) = order(
        attn_half_kernel(True), operands, [((width // 2, 4 * features), wide)], temporary=4 << 20)
    widths = (features + features // 2, features + features // 2, features)

    def messages_of(width_out, size, ffn_step, attn_step_out):
        by_way = {orders[attn_step_out]: part for orders, part in zip(ATTN_ORDERS, widths)}
        top = tops(ffn_step)
        return [
            ((top[way] + packed_rows(size, by_way[way], width_out), width_out), low)
            for way in WAYS
        ]

    def kept(size):
        return [((size, part), low) for part in widths]

    def fly(messages):
        return [by_seq(message, way) for message, way in zip(messages, WAYS)]

    *parts, keep_x, keep_y, keep_z, ffn_x, ffn_y, ffn_z = order(
        round_one_kernel,
        ffn_keeps + ffn_flights + [own_half, core_arrived],
        messages_of(128, 512, 2, 0) + kept(512) + [((rows_k, 128), low) for rows_k in FFN_ROWS],
        temporary=4 << 20, cost=4.0,
    )
    flights = fly(parts)

    stay_one, go_one, stay_two, go_two = order(
        sum_middle_kernel,
        [keep_one, one_arrived, keep_two, two_arrived],
        [
            ((quarter, cut), wide),
            ((quarter, cut), low),
            ((quarter, cut + HD), wide),
            ((quarter, cut + HD), low),
        ], cost=3.0)
    one_arrived, two_arrived = by_tp(go_one, 6), by_tp(go_two, 2)

    *parts, keep_x, keep_y, keep_z = order(
        round_two_kernel,
        flights + [ffn_x, ffn_y, ffn_z, keep_x, keep_y, keep_z],
        messages_of(128, 256, 2, 1) + kept(256),
    )
    flights = fly(parts)
    keep, send = order(
        sum_last_kernel,
        [stay_one, one_arrived, stay_two, two_arrived],
        [((share, 2 * width + HD), wide), ((share, 2 * width + HD), low)],
    )
    arrived = by_tp(send, 1)
    *parts, keep_x, keep_y, keep_z = order(
        round_three_kernel,
        parts + flights + [keep_x, keep_y, keep_z],
        messages_of(256, 128, 1, 2) + kept(128),
    )
    flights = fly(parts)
    last_rows, gains = order(
        last_rows_kernel,
        [keep, arrived, grad_hidden, hidden, tokens, gain_attn],
        [((share, 2 * width), low), ((16, features), low)], cost=6.0)
    arrived = by_tp(last_rows, 1)
    below = {ATTN_ORDERS[0][2]: 128, ATTN_ORDERS[1][2]: 128, ATTN_ORDERS[2][2]: 128 + 16}
    parts = order(
        round_four_kernel,
        parts + flights + [keep_x, keep_y, keep_z, gains],
        [((tops(0)[way] + below[way], 512), low) for way in WAYS], cost=8.0)
    flights = fly(parts)
    first, second = order(last_pair_kernel, [last_rows, arrived], [((quarter, width), low)] * 2, cost=0.3)
    first_arrived, second_arrived = by_tp(first, 2), by_tp(second, 6)
    firsts, seconds = order(
        stack_kernel,
        [first, first_arrived, second, second_arrived],
        [((2 * quarter, width), low)] * 2, cost=2.0)
    first_arrived, second_arrived = by_tp(firsts, 6), by_tp(seconds, 2)
    one, two, three = order(
        round_five_kernel,
        list(parts) + flights,
        [((256, widths[0]), low), ((256, widths[1]), low), ((256 + 16, widths[2]), low)],
    )
    ffn_last = list(parts) + flights
    flights = [by_seq(value, orders[1]) for value, orders in zip((one, two, three), ATTN_ORDERS)]
    (ffn_half,) = order(ffn_halves_kernel, ffn_last, [((3 * units, width // 2), low)])

    def attn_join(step, needs=()):
        nonlocal one, two, three, flights
        names = [orders[step] for orders in ATTN_ORDERS]
        (one,), (two,), (three,) = run_ops(
            order,
            [
                join_op(one, flights[0], names[0], 0),
                join_op(two, flights[1], names[1], 0),
                join_tail_op(three, flights[2], names[2], gains.shape[0]),
            ],
            needs,
        )
        names = [orders[step - 1] if step > 0 else "core" for orders in ATTN_ORDERS]
        flights = [by_seq(value, name) for value, name in zip((one, two, three), names)]

    ffn_shapes = [(units, width)] * 3
    ffn_buffers = [(units, width // 2)] * 3
    grads_ffn = write_out(order, write_ffn(True), [ffn_half], ffn_shapes, ffn_buffers)
    attn_join(1, [first_arrived, second_arrived])
    (ffn_half,) = hold(order, [ffn_half], True)
    ffn_arrived = by_seq(ffn_half, "core")
    grads_ffn = write_out(
        order, write_ffn(False), [ffn_arrived], ffn_shapes, ffn_buffers, into=grads_ffn, cost=8.0
    )
    attn_join(0)
    attn_shapes = [(width, features)] * 3 + [(features, width)]
    attn_buffers = [(width // 2, features)] * 3 + [(features, width // 2)]
    grads_attn = write_out(
        order, write_attn(True), [one, two, three], attn_shapes, attn_buffers
    )
    grad_tokens, block_out = order(
        token_outputs_kernel,
        [firsts, first_arrived, seconds, second_arrived],
        [((rows, width), wide), whole],
    )
    grad_w_query, grad_w_key, grad_w_value, grad_w_out, grad_gain_attn, grad_gain_ffn = write_out(
        order,
        write_attn(False),
        flights + [three],
        attn_shapes,
        attn_buffers,
        small=[((1, features), wide)] * 2,
        into=grads_attn,
    )
    return (
        block_out,
        grad_tokens,
        grad_gain_attn.reshape(-1),
        grad_w_query,
        grad_w_key,
        grad_w_value,
        grad_w_out,
        grad_gain_ffn.reshape(-1),
        grads_ffn[0].T,
        grads_ffn[1].T,
        grads_ffn[2],
    )


def solution(mesh):
    fine = Mesh(mesh.devices.reshape(2, 4, 2, TP), SEQ_AXES + ("tp",))
    return jax.shard_map(
        on_device,
        mesh=fine,
        in_specs=(
            P(SEQ_AXES, None),
            P(),
            P(None, "tp"),
            P(None, "tp"),
            P(None, "tp"),
            P("tp", None),
            P(),
            P(None, "tp"),
            P(None, "tp"),
            P("tp", None),
            P(SEQ_AXES, None),
        ),
        out_specs=(
            P(SEQ_AXES, None),
            P(SEQ_AXES, None),
            P("tp"),
            P(None, "tp"),
            P(None, "tp"),
            P(None, "tp"),
            P("tp", None),
            P("tp"),
            P(None, "tp"),
            P(None, "tp"),
            P("tp", None),
        ),
        check_vma=False,
    )
```

```python
import jax
import jax.numpy as jnp
from jax import lax
from jax.experimental import pallas as pl
from jax.experimental.pallas import tpu as pltpu
from jax.sharding import Mesh
from jax.sharding import PartitionSpec as P

HD = 128
W = 1024
SEQ = 16
TP = 8
Z_FLIPS = (2, 1, 3)
FFN_PIECES = (
    ((0, 0, 688), (1, 0, 128)),
    ((1, 128, 688), (2, 0, 256)),
    ((2, 256, 688),),
)
FFN_ROWS = (816, 816, 432)

epsilon = 1e-06
masked_value = -1e30
low = jnp.bfloat16
wide = jnp.float32


def seq_pairs(step):
    pairs = []
    for x_hi in range(2):
        for y in range(4):
            for core in range(2):
                to = step(x_hi, y, core)
                if to is not None:
                    pairs.append((x_hi * 8 + y * 2 + core, to[0] * 8 + to[1] * 2 + to[2]))
    return pairs


EXCHANGE = {
    "core": seq_pairs(lambda x, y, c: (x, y, 1 - c)),
    "y1": seq_pairs(lambda x, y, c: (x, y ^ 1, c)),
    "y3": seq_pairs(lambda x, y, c: (x, y ^ 3, c)),
    "x": seq_pairs(lambda x, y, c: (1 - x, y, c)),
}

SEQ_AXES = ("x_hi", "y", "core")


def by_seq(value, name):
    return lax.ppermute(value, SEQ_AXES, EXCHANGE[name])


def by_tp(value, flip):
    return lax.ppermute(value, "tp", [(k, k ^ flip) for k in range(TP)])


def shifted(value, steps):
    pairs = [(k, k + steps) for k in range(SEQ) if 0 <= k + steps < SEQ]
    return lax.ppermute(value, SEQ_AXES, pairs)


def z_exchange(blocks):
    return [by_tp(block, 2 * flip) for flip, block in zip(Z_FLIPS, blocks)]


def z_spread(block):
    return [by_tp(block, 2 * flip) for flip in Z_FLIPS]


def gather_tp(rows):
    mine = [by_tp(rows, 2 * flip) for flip in Z_FLIPS]
    other = by_tp(rows, 1)
    theirs = [by_tp(other, 2 * flip) for flip in Z_FLIPS]
    return [rows, other] + mine + theirs


def places():
    x_hi = lax.axis_index("x_hi")
    y = lax.axis_index("y")
    core = lax.axis_index("core")
    tp = lax.axis_index("tp")
    return {
        "seq": x_hi * 8 + y * 2 + core,
        "tp": tp,
        "z": tp >> 1,
        "x_low": tp & 1,
        "core": core,
        "y1": (y & 1) ^ (y >> 1),
        "y3": y >> 1,
        "x": x_hi,
    }


class Order:
    def __init__(self):
        self.last = None

    def __call__(self, body, ins, outs, needs=(), scratch=(), temporary=2 << 20, cost=0.3):
        ins = list(ins)
        needs = list(needs)
        if self.last is not None:
            needs.append(self.last)
        skip = len(ins) + len(needs)
        outs = list(outs) + [((8, 128), wide)]
        out_shape = [jax.ShapeDtypeStruct(shape, kind) for shape, kind in outs]
        count = len(ins)

        def run(*refs):
            given = refs[skip : skip + len(outs)]
            given[-1][...] = jnp.zeros_like(given[-1])
            body(refs[:count], given[:-1], refs[skip + len(outs) :])

        def size(shape, kind):
            lanes = -(-shape[-1] // 128) * 128
            total = lanes * jnp.dtype(kind).itemsize
            for extent in shape[:-1]:
                total *= max(extent, 1)
            return total

        held = (
            sum(size(value.shape, value.dtype) for value in ins)
            + sum(size(shape, kind) for shape, kind in outs)
            + sum(size(shape, kind) for shape, kind in scratch)
        )
        result = pl.pallas_call(
            run,
            out_shape=out_shape,
            in_specs=[pl.BlockSpec(memory_space=pltpu.VMEM)] * count
            + [pl.BlockSpec(memory_space=pl.ANY)] * len(needs),
            out_specs=[pl.BlockSpec(memory_space=pltpu.VMEM)] * len(outs),
            scratch_shapes=[pltpu.VMEM(shape, kind) for shape, kind in scratch],
            compiler_params=pltpu.CompilerParams(vmem_limit_bytes=held + temporary),
            cost_estimate=pl.CostEstimate(
                flops=int(cost * 1e9), bytes_accessed=0, transcendentals=0
            ),
            name=body.__name__,
        )(*ins, *needs)
        self.last = result[-1]
        return result[:-1]


def hold(order, values, strict=False):
    values = list(values)
    needs = [order.last]
    if strict:
        values, needs = values + needs, []

    def run(*refs):
        pass

    result = pl.pallas_call(
        run,
        out_shape=[jax.ShapeDtypeStruct(value.shape, value.dtype) for value in values],
        in_specs=[pl.BlockSpec(memory_space=pl.ANY)] * (len(values) + len(needs)),
        out_specs=[pl.BlockSpec(memory_space=pl.ANY)] * len(values),
        input_output_aliases={k: k for k in range(len(values))},
        compiler_params=pltpu.CompilerParams(vmem_limit_bytes=1 << 20),
        cost_estimate=pl.CostEstimate(flops=0, bytes_accessed=0, transcendentals=0),
    )(*values, *needs)
    if strict:
        order.last = result[-1]
        result = result[:-1]
    return result


def dot(left, right):
    return jnp.dot(left, right, preferred_element_type=wide)


def dot_rows(left, right):
    return lax.dot_general(left, right, (((1,), (1,)), ((), ())), preferred_element_type=wide)


def dot_cols(left, right):
    return lax.dot_general(left, right, (((0,), (0,)), ((), ())), preferred_element_type=wide)


def rms_factor(rows):
    return lax.rsqrt(jnp.mean(rows * rows, axis=-1, keepdims=True) + epsilon)


def norm_back(grad_normed, unit_rows, factor, gain_vec):
    scaled = grad_normed * gain_vec
    return factor * (scaled - unit_rows * jnp.mean(scaled * unit_rows, axis=-1, keepdims=True))


def span(index, size):
    return pl.ds(pl.multiple_of(index * size, size), size)


def eight_blocks(at, size):
    here = [span(2 * at["z"] + x, size) for x in (at["x_low"], 1 - at["x_low"])]
    mine = [span(2 * (at["z"] ^ flip) + at["x_low"], size) for flip in Z_FLIPS]
    theirs = [span(2 * (at["z"] ^ flip) + 1 - at["x_low"], size) for flip in Z_FLIPS]
    return here + mine + theirs


def write_eight(partial, at, outs):
    for place, out in zip(eight_blocks(at, outs[0].shape[0]), outs):
        out[...] = partial[place, :]


def read_eight(whole, at, blocks):
    for place, block in zip(eight_blocks(at, blocks[0].shape[0]), blocks):
        whole[place, :] = block[...]


def read_pairs(whole, z, blocks):
    size = blocks[0].shape[0]
    for flip, block in zip((0,) + Z_FLIPS, blocks):
        whole[span(z ^ flip, size), :] = block[...]


def normed_kernel(ins, outs, _):
    tokens, gain, w_key, w_value = ins
    normed, key_value = outs
    inputs = tokens[...].astype(wide)
    rows = (inputs * rms_factor(inputs) * gain[...]).astype(low)
    normed[...] = rows
    features = w_key.shape[1]
    key_value[:, :features] = dot(rows, w_key[...]).astype(low)
    key_value[:, features:] = dot(rows, w_value[...]).astype(low)


def project_kernel(ins, outs, _):
    outs[0][...] = dot(ins[0][...], ins[1][...]).astype(low)


def last_block(at, own_of_partner, four_of_partner, way):
    near = at["core"] == (0 if way == 1 else 1)
    return jnp.where(near, four_of_partner, own_of_partner)


def seen_scores(scores, order, distance, gap, inside):
    if order == 0:
        return jnp.where(gap >= 0, scores, masked_value)
    if order == 3:
        return jnp.where((gap < 0) & inside, scores, masked_value)
    return jnp.where(inside, scores, masked_value)


def distances(at, way):
    near = at["core"] == (0 if way == 1 else 1)
    return [0, 2, jnp.where(near, 1, 3), 4, jnp.where(near, 3, 1)]


def gap_of(rows, flipped=False):
    first = lax.broadcasted_iota(jnp.int32, (rows, rows), 0)
    second = lax.broadcasted_iota(jnp.int32, (rows, rows), 1)
    return second - first if flipped else first - second


def attend_kernel(ins, outs, scratch):
    query, own, two, across, four, partner_own, partner_four, w_out = ins
    heads_out, log_out = outs[:2]
    rows, features = query.shape
    at = places()
    scale = HD ** (-0.5)
    gap = gap_of(rows)
    away = distances(at, 1)
    blocks = [own[...], two[...], across[...], four[...]]
    blocks.append(last_block(at, partner_own[...], partner_four[...], 1))
    logs = []
    mixed = []
    for head in range(features // HD):
        here = slice(head * HD, (head + 1) * HD)
        there = slice(features + head * HD, features + (head + 1) * HD)
        scores = [
            seen_scores(
                dot_rows(query[:, here], block[:, here]) * scale,
                order,
                distance,
                gap,
                at["seq"] >= distance,
            )
            for order, (block, distance) in enumerate(zip(blocks, away))
        ]
        peak = scores[0].max(axis=-1, keepdims=True)
        for part in scores[1:]:
            peak = jnp.maximum(peak, part.max(axis=-1, keepdims=True))
        raised = [jnp.exp(part - peak) for part in scores]
        total = raised[0].sum(axis=-1, keepdims=True)
        for part in raised[1:]:
            total = total + part.sum(axis=-1, keepdims=True)
        inverse = 1.0 / total
        out = dot((raised[0] * inverse).astype(low), blocks[0][:, there])
        for part, block in zip(raised[1:], blocks[1:]):
            out = out + dot((part * inverse).astype(low), block[:, there])
        mixed.append(out.astype(low))
        logs.append(peak + jnp.log(total))
    for head, out in enumerate(mixed):
        heads_out[:, head * HD : (head + 1) * HD] = out
    lane = lax.broadcasted_iota(jnp.int32, (rows, HD), 1)
    log_out[...] = jnp.where(lane < 64, logs[0], logs[1])
    partial = scratch[0]
    partial[...] = dot(heads_out[...], w_out[...]).astype(low)
    write_eight(partial, at, outs[2:])


def sum_kernel(ins, outs, _):
    total = ins[0][...].astype(wide)
    for block in ins[1:]:
        total = total + block[...].astype(wide)
    outs[0][...] = total.astype(outs[0].dtype)


def sum_refs(refs):
    total = refs[0][...].astype(wide)
    for ref in refs[1:]:
        total = total + ref[...].astype(wide)
    return total


def norm_rows_kernel(ins, outs, _):
    tokens, gain = ins[5:]
    hidden, normed = outs
    at = places()
    rows = tokens[span(at["tp"], hidden.shape[0]), :].astype(wide) + sum_refs(ins[:5])
    hidden[...] = rows
    normed[...] = (rows * rms_factor(rows) * gain[...]).astype(low)


def pair_kernel(ins, outs, _):
    at = places()
    size = ins[0].shape[0]
    outs[0][span(at["x_low"], size), :] = ins[0][...]
    outs[0][span(1 - at["x_low"], size), :] = ins[1][...]


def ffn_kernel(ins, outs, scratch):
    w_gate, w_up, w_down, cotangent = ins[8:]
    normed, activated, grad_gate, grad_up = outs[:4]
    at = places()
    read_eight(normed, at, ins[:8])
    rows = normed[...]
    gate_pre = dot_rows(rows, w_gate[...])
    up_pre = dot_rows(rows, w_up[...])
    grad_act = dot_rows(cotangent[...], w_down[...])
    sigmoid = jax.nn.sigmoid(gate_pre)
    silu = gate_pre * sigmoid
    activated[...] = (silu * up_pre).astype(low)
    grad_gate[...] = (grad_act * up_pre * sigmoid * (1.0 + gate_pre * (1.0 - sigmoid))).astype(low)
    grad_up[...] = (grad_act * silu).astype(low)
    partial = scratch[0]
    partial[...] = (dot(grad_gate[...], w_gate[...]) + dot(grad_up[...], w_up[...])).astype(low)
    write_eight(partial, at, outs[4:])


def grad_rows_kernel(ins, outs, _):
    hidden, cotangent, gain = ins[5:]
    grad_hidden, grad_low, gain_part = outs
    at = places()
    grad_normed = sum_refs(ins[:5])
    rows = hidden[...]
    factor = rms_factor(rows)
    unit = rows * factor
    gain_part[...] = jnp.sum(grad_normed * unit, axis=0, keepdims=True)
    grad = cotangent[span(at["tp"], rows.shape[0]), :].astype(wide) + norm_back(
        grad_normed, unit, factor, gain[...]
    )
    grad_hidden[...] = grad
    grad_low[...] = grad.astype(low)


def heads_kernel(ins, outs, _):
    w_out, logs, heads_out = ins[4:]
    grad_hidden, grad_heads = outs
    read_pairs(grad_hidden, places()["z"], ins[:4])
    grad = dot_rows(grad_hidden[...], w_out[...]).astype(low)
    rows, features = grad.shape
    grad_heads[:, :features] = grad
    product = grad.astype(wide) * heads_out[...].astype(wide)
    values = [logs[:, :1], logs[:, 64:65]]
    for head in range(2):
        values.append(jnp.sum(product[:, head * HD : (head + 1) * HD], axis=-1, keepdims=True))
    group = lax.broadcasted_iota(jnp.int32, (rows, HD), 1) >> 3
    both = jnp.zeros((rows, HD), wide)
    for k, value in enumerate(values):
        both = jnp.where((group & 3) == k, value, both)
    first = both.astype(low).astype(wide)
    second = (both - first).astype(low).astype(wide)
    rest = jnp.where(group < 8, second, both - first - second)
    grad_heads[:, features:] = jnp.where(group < 4, first, rest).astype(low)


def grad_query_kernel(ins, outs, _):
    query_all, heads_out, logs, grad_heads, own, two, across, four, partner_own, partner_four = ins
    rows, features = query_all.shape
    at = places()
    scale = HD ** (-0.5)
    gap = gap_of(rows)
    away = distances(at, 1)
    blocks = [own[...], two[...], across[...], four[...]]
    blocks.append(last_block(at, partner_own[...], partner_four[...], 1))
    for head in range(features // HD):
        here = slice(head * HD, (head + 1) * HD)
        there = slice(features + head * HD, features + (head + 1) * HD)
        query = query_all[:, here]
        grad = grad_heads[:, here]
        log_total = logs[:, head * 64 : head * 64 + 1]
        inner = jnp.sum(
            grad.astype(wide) * heads_out[:, here].astype(wide), axis=-1, keepdims=True
        )
        total = jnp.zeros((rows, HD), wide)
        for order, (block, distance) in enumerate(zip(blocks, away)):
            scores = seen_scores(
                dot_rows(query, block[:, here]) * scale,
                order,
                distance,
                gap,
                at["seq"] >= distance,
            )
            weights = jnp.exp(scores - log_total)
            grad_scores = weights * (dot_rows(grad, block[:, there]) - inner)
            total = total + dot(grad_scores.astype(low), block[:, here])
        outs[0][:, here] = (total * scale).astype(low)


def grad_key_kernel(ins, outs, scratch):
    key_value = ins[0]
    sides = ins[1:7]
    grads = ins[7:13]
    grad_key, grad_value = outs
    rows, features = grad_key.shape
    at = places()
    scale = HD ** (-0.5)
    gap = gap_of(rows, flipped=True)
    away = distances(at, -1)
    side_blocks = [side[...] for side in sides[:4]]
    side_blocks.append(last_block(at, sides[4][...], sides[5][...], -1))
    grad_blocks = [grad[...] for grad in grads[:4]]
    grad_blocks.append(last_block(at, grads[4][...], grads[5][...], -1))
    sums = [grad[:, features:].astype(wide).T for grad in grad_blocks]
    for head in range(features // HD):
        here = slice(head * HD, (head + 1) * HD)
        there = slice(features + head * HD, features + (head + 1) * HD)
        key = key_value[:, here]
        value = key_value[:, there]
        total_key = jnp.zeros((rows, HD), wide)
        total_value = jnp.zeros((rows, HD), wide)
        for order, (side, grad_all, logs, distance) in enumerate(
            zip(side_blocks, grad_blocks, sums, away)
        ):
            query = side[:, here]
            grad = grad_all[:, here]
            log_total, inner = [
                logs[8 * k : 8 * k + 1]
                + logs[32 + 8 * k : 33 + 8 * k]
                + logs[64 + 8 * k : 65 + 8 * k]
                for k in (head, 2 + head)
            ]
            scores = seen_scores(
                dot_rows(key, query) * scale, order, distance, gap, at["seq"] + distance < SEQ
            )
            weights = jnp.exp(scores - log_total)
            total_value = total_value + dot(weights.astype(low), grad)
            grad_scores = weights * (dot_rows(value, grad) - inner)
            total_key = total_key + dot(grad_scores.astype(low), query)
        grad_key[:, here] = (total_key * scale).astype(low)
        grad_value[:, here] = total_value.astype(low)


def back_kernel(ins, outs, scratch):
    grad_query, grad_key, grad_value, w_query, w_key, w_value, tokens, gain_ffn_part, ffn_partial = ins
    keep_one, keep_two, send_one, send_two = outs
    at = places()
    rows = tokens.shape[0]
    back = (
        dot_rows(grad_query[...], w_query[...])
        + dot_rows(grad_key[...], w_key[...])
        + dot_rows(grad_value[...], w_value[...])
    )
    inputs = tokens[...].astype(wide)
    gain_attn_part = jnp.sum(back * (inputs * rms_factor(inputs)), axis=0, keepdims=True)
    partial = scratch[0]
    width = tokens.shape[1]
    partial[:, :width] = back.astype(low)
    share = rows // TP
    cells = width // TP // HD
    for k in range(TP):
        parts = [
            gain[:, (k * cells + cell) * HD : (k * cells + cell + 1) * HD]
            for gain in (gain_attn_part, gain_ffn_part[...])
            for cell in range(cells)
        ]
        parts.append(jnp.zeros((share - len(parts), HD), wide))
        partial[k * share : (k + 1) * share, width:] = jnp.concatenate(parts, axis=0).astype(low)
    size = rows // 4
    z = at["z"]
    cut = width // 2
    for out, first, flips in (
        (keep_one, 0, (0, 3)),
        (send_one, 0, (1, 2)),
        (keep_two, cut, (0, 1)),
        (send_two, cut, (3, 2)),
    ):
        for k, flip in enumerate(flips):
            here = slice(k * size, (k + 1) * size)
            there = span(z ^ flip, size)
            out[here, :cut] = partial[there, first : first + cut]
            out[here, cut:width] = ffn_partial[there, first : first + cut]
            if first > 0:
                out[here, width:] = partial[there, width:]


def sum_middle_kernel(ins, outs, _):
    for keep, arrived, stay, send in ((ins[0], ins[1], outs[0], outs[1]), (ins[2], ins[3], outs[2], outs[3])):
        size = stay.shape[0]
        stay[...] = keep[:size, :].astype(wide) + arrived[:size, :].astype(wide)
        send[...] = (keep[size:, :].astype(wide) + arrived[size:, :].astype(wide)).astype(low)


def sum_last_kernel(ins, outs, _):
    keep, send = outs
    at = places()
    size = keep.shape[0]
    width = ins[0].shape[1]
    cut = width // 2
    for out, index in ((keep, at["x_low"]), (send, 1 - at["x_low"])):
        here = span(index, size)
        first = (ins[0][here, :] + ins[1][here, :].astype(wide)).astype(out.dtype)
        second = (ins[2][here, :] + ins[3][here, :].astype(wide)).astype(out.dtype)
        out[:, :cut] = first[:, :cut]
        out[:, cut:width] = second[:, :cut]
        out[:, width : width + cut] = first[:, cut:]
        out[:, width + cut : 2 * width] = second[:, cut:width]
        out[:, 2 * width :] = second[:, width:]


def last_rows_kernel(ins, outs, _):
    keep, arrived, grad_hidden, hidden, tokens, gain = ins
    rows_out, gains = outs
    width = hidden.shape[1]
    at = places()
    inputs = tokens[span(at["tp"], keep.shape[0]), :].astype(wide)
    factor = rms_factor(inputs)
    grad_normed = keep[:, :width] + arrived[:, :width].astype(wide)
    grad = grad_hidden[...] + norm_back(grad_normed, inputs * factor, factor, gain[...])
    rows_out[:, :width] = grad.astype(low)
    rows_out[:, width:] = (
        hidden[...] + keep[:, width : 2 * width] + arrived[:, width : 2 * width].astype(wide)
    ).astype(low)
    sums = keep[:, 2 * width :] + arrived[:, 2 * width :].astype(wide)
    gains[...] = jnp.zeros_like(gains)
    gains[:, : sums.shape[1]] = sums[: gains.shape[0], :].astype(low)


def last_pair_kernel(ins, outs, _):
    at = places()
    size = ins[0].shape[0]
    width = outs[0].shape[1]
    for value, index in zip(ins, (at["x_low"], 1 - at["x_low"])):
        outs[0][span(index, size), :] = value[:, :width]
        outs[1][span(index, size), :] = value[:, width:]


def stack_kernel(ins, outs, _):
    for k, out in enumerate(outs):
        size = ins[2 * k].shape[0]
        out[:size, :] = ins[2 * k][...]
        out[size:, :] = ins[2 * k + 1][...]


def token_outputs_kernel(ins, outs, _):
    z = places()["z"]
    size = ins[0].shape[0] // 2
    for out, own, arrived, flips in (
        (outs[0], ins[0], ins[1], (0, 1, 3, 2)),
        (outs[1], ins[2], ins[3], (0, 3, 1, 2)),
    ):
        blocks = (own[:size, :], own[size:, :], arrived[:size, :], arrived[size:, :])
        for flip, block in zip(flips, blocks):
            out[span(z ^ flip, size), :] = block.astype(out.dtype)


def part(ref, axis, start, size):
    return ref[:, pl.ds(start, size)] if axis == 1 else ref[pl.ds(start, size), :]


def put(ref, axis, start, size, value):
    if axis == 1:
        ref[:, pl.ds(start, size)] = value
    else:
        ref[pl.ds(start, size), :] = value


def split_op(keep, arrived, bit, axis):
    shape = list(keep.shape)
    shape[axis] //= 2
    size = shape[axis]

    def body(at, ins, outs):
        for out, index in zip(outs, (at[bit], 1 - at[bit])):
            start = pl.multiple_of(index * size, size)
            out[...] = (
                part(ins[0], axis, start, size).astype(wide)
                + part(ins[1], axis, start, size).astype(wide)
            ).astype(low)

    return body, [keep, arrived], [(tuple(shape), low)] * 2


def add_op(keep, arrived):
    def body(at, ins, outs):
        outs[0][...] = (ins[0][...].astype(wide) + ins[1][...].astype(wide)).astype(
            outs[0].dtype
        )

    return body, [keep, arrived], [(keep.shape, keep.dtype)]


def join_op(own, arrived, bit, axis, kind=low):
    shape = list(own.shape)
    size = shape[axis]
    shape[axis] *= 2

    def body(at, ins, outs):
        for value, index in zip(ins, (at[bit], 1 - at[bit])):
            start = pl.multiple_of(index * size, size)
            put(outs[0], axis, start, size, value[...].astype(kind))

    return body, [own, arrived], [(tuple(shape), kind)]


def add_tail_op(keep, arrived, tail):
    rows, width = keep.shape

    def body(at, ins, outs):
        outs[0][:rows, :] = (ins[0][...].astype(wide) + ins[1][...].astype(wide)).astype(low)
        outs[0][rows:, :] = ins[2][...]

    return body, [keep, arrived, tail], [((rows + tail.shape[0], width), low)]


def join_tail_op(own, arrived, bit, tail):
    rows, width = own.shape
    size = rows - tail

    def body(at, ins, outs):
        for value, index in zip(ins, (at[bit], 1 - at[bit])):
            outs[0][span(index, size), :] = value[:size, :]
        outs[0][2 * size :, :] = (
            ins[0][size:, :].astype(wide) + ins[1][size:, :].astype(wide)
        ).astype(low)

    return body, [own, arrived], [((2 * size + tail, width), low)]


def run_ops(order, ops, needs=()):
    ins = [value for _, values, _ in ops for value in values]
    outs = [out for _, _, shapes in ops for out in shapes]

    def body(in_refs, out_refs, _):
        at = places()
        first = last = 0
        for step, values, shapes in ops:
            step(
                at,
                in_refs[first : first + len(values)],
                out_refs[last : last + len(shapes)],
            )
            first += len(values)
            last += len(shapes)

    flat = list(order(body, ins, outs, needs))
    result = []
    for _, _, shapes in ops:
        result.append(flat[: len(shapes)])
        flat = flat[len(shapes) :]
    return result


FFN_ORDERS = (("y1", "y3", "x"), ("y3", "x", "y1"), ("x", "y1", "y3"))


def ffn_terms(ins, k):
    terms = []
    first = 0
    for operand, start, stop in FFN_PIECES[k]:
        last = first + stop - start
        terms.append((first, last, ins[operand][:, start:stop], ins[4 if operand == 2 else 3]))
        first = last
    return terms


def ffn_send_kernel(arrays):
    def ffn_send(ins, outs, _):
        out = outs[0]
        half = out.shape[1]
        other = 1 - places()["core"]
        base = 0
        for k in arrays:
            for first, last, left, right in ffn_terms(ins, k):
                out[base + first : base + last, :] = dot_cols(
                    left, right[:, span(other, half)]
                ).astype(low)
            base += FFN_ROWS[k]

    return ffn_send


def ffn_keep_kernel(arrays):
    def ffn_keep(ins, outs, _):
        at = places()
        arrived = ins[5]
        base = 0
        for k, keep, send in zip(arrays, outs[0::2], outs[1::2]):
            size = keep.shape[1]
            bit = at[FFN_ORDERS[k][0]]
            for out, index in ((keep, bit), (send, 1 - bit)):
                start = pl.multiple_of((2 * at["core"] + index) * size, size)
                for first, last, left, right in ffn_terms(ins, k):
                    own = dot_cols(left, right[:, pl.ds(start, size)])
                    got = arrived[base + first : base + last, span(index, size)]
                    out[first:last, :] = (own + got.astype(wide)).astype(low)
            base += FFN_ROWS[k]

    return ffn_keep


def attn_terms(ins):
    normed, grad_hidden, grad_query, grad_key, grad_value, heads_out = ins
    half = heads_out.shape[1] // 2
    return [
        [(normed, grad_query[...]), (grad_hidden, heads_out[:, :half])],
        [(normed, grad_key[...]), (grad_hidden, heads_out[:, half:])],
        [(normed, grad_value[...])],
    ]


def attn_half_kernel(own):
    def attn_half(ins, outs, _):
        out = outs[0]
        half = out.shape[0]
        index = places()["core"] if own else 1 - places()["core"]
        first = 0
        for terms in attn_terms(ins):
            for left, right in terms:
                last = first + right.shape[1]
                out[:, first:last] = dot_cols(left[:, span(index, half)], right).astype(out.dtype)
                first = last

    return attn_half


def packed_rows(rows, lanes, width):
    across = width // 128
    full, rest = divmod(lanes // 128, across)
    if rest == 1 and rows % across == 0:
        return rows * full + rows // across
    return rows * (full + (rest > 0))


def place_cells(rows, lanes, width):
    across = width // 128
    cells = lanes // 128
    runs = []
    full = cells // across
    for k in range(full * across):
        runs.append((0, k * 128, (k // across) * rows, (k % across) * 128, rows))
    rest = cells - full * across
    if rest and rows % across == 0 and rest == 1:
        size = rows // across
        for k in range(across):
            runs.append((k * size, full * across * 128, full * rows, k * 128, size))
    elif rest:
        for k in range(rest):
            runs.append((0, (full * across + k) * 128, full * rows, k * 128, rows))
    return runs


def pack(message, base, value):
    rows, lanes = value.shape
    for row, lane, to_row, to_lane, size in place_cells(rows, lanes, message.shape[1]):
        message[base + to_row : base + to_row + size, to_lane : to_lane + 128] = value[
            row : row + size, lane : lane + 128
        ]


def add_packed(keep, message, base, lanes):
    rows = keep.shape[0]
    columns = [[] for _ in range(lanes // 128)]
    for row, lane, from_row, from_lane, size in place_cells(rows, lanes, message.shape[1]):
        here = keep[row : row + size, lane : lane + 128].astype(wide)
        there = message[base + from_row : base + from_row + size, from_lane : from_lane + 128]
        columns[lane // 128].append(here + there.astype(wide))
    return [jnp.concatenate(parts, axis=0) if len(parts) > 1 else parts[0] for parts in columns]


ATTN_ORDERS = (("y1", "y3", "x"), ("y3", "x", "y1"), ("x", "y1", "y3"))
WAYS = ("y1", "y3", "x")


def tops(step):
    return {orders[step]: rows for orders, rows in zip(FFN_ORDERS, FFN_ROWS)}


def round_one_kernel(ins, outs, _):
    at = places()
    own, arrived = ins[6:]
    messages = dict(zip(WAYS, outs[:3]))
    for k in range(3):
        way = FFN_ORDERS[k][2]
        size = outs[6 + k].shape[1]
        for out, index in ((outs[6 + k], at[way]), (messages[way], 1 - at[way])):
            start = pl.multiple_of(index * size, size)
            out[: FFN_ROWS[k], :] = (
                ins[k][:, pl.ds(start, size)].astype(wide)
                + ins[3 + k][:, pl.ds(start, size)].astype(wide)
            ).astype(low)
    base = 0
    for k in range(3):
        keep = outs[3 + k]
        size, lanes = keep.shape
        way = ATTN_ORDERS[k][0]
        for kept, index in ((True, at[way]), (False, 1 - at[way])):
            here = span(index, size)
            for lane in range(0, lanes, 128):
                there = slice(base + lane, base + lane + 128)
                value = (own[here, there] + arrived[here, there].astype(wide)).astype(low)
                if kept:
                    keep[:, lane : lane + 128] = value
                else:
                    row = tops(2)[way] + lane // 128 * size
                    messages[way][row : row + size, :] = value
        base += lanes


def attn_step(at, keeps, arrived, top, step, outs, messages, message_top):
    for k, (keep, out) in enumerate(zip(keeps, outs)):
        came, way = ATTN_ORDERS[k][step - 1], ATTN_ORDERS[k][step]
        columns = add_packed(keep, arrived[came], top[came], keep.shape[1])
        size = keep.shape[0] // 2
        first = at[way] == 0
        go = []
        for lane, column in enumerate(columns):
            one, two = column[:size, :], column[size:, :]
            out[:, lane * 128 : (lane + 1) * 128] = jnp.where(first, one, two).astype(low)
            go.append(jnp.where(first, two, one).astype(low))
        pack(messages[way], message_top[way], jnp.concatenate(go, axis=1))


def ffn_joined(at, sent, arrived, step, messages):
    for k, rows in enumerate(FFN_ROWS):
        back = FFN_ORDERS[k][step]
        message = messages[FFN_ORDERS[k][step - 1]]
        width = sent[back].shape[1]
        for value, index in ((sent[back], at[back]), (arrived[back], 1 - at[back])):
            start = pl.multiple_of(index * width, width)
            message[:rows, pl.ds(start, width)] = value[:rows, :]


def round_two_kernel(ins, outs, _):
    at = places()
    arrived, messages = dict(zip(WAYS, ins[:3])), dict(zip(WAYS, outs[:3]))
    for k, rows in enumerate(FFN_ROWS):
        way = FFN_ORDERS[k][2]
        messages[way][:rows, :] = (
            ins[3 + k][...].astype(wide) + arrived[way][:rows, :].astype(wide)
        ).astype(low)
    attn_step(at, ins[6:9], arrived, tops(2), 1, outs[3:], messages, tops(2))


def round_three_kernel(ins, outs, _):
    at = places()
    sent, arrived = dict(zip(WAYS, ins[:3])), dict(zip(WAYS, ins[3:6]))
    messages = dict(zip(WAYS, outs[:3]))
    ffn_joined(at, sent, arrived, 2, messages)
    attn_step(at, ins[6:9], arrived, tops(2), 2, outs[3:], messages, tops(1))


def round_four_kernel(ins, outs, _):
    at = places()
    sent, arrived = dict(zip(WAYS, ins[:3])), dict(zip(WAYS, ins[3:6]))
    messages = dict(zip(WAYS, outs))
    ffn_joined(at, sent, arrived, 1, messages)
    for k in range(3):
        way = ATTN_ORDERS[k][2]
        keep = ins[6 + k]
        rows, lanes = keep.shape
        first = tops(0)[way]
        for lane, column in enumerate(add_packed(keep, arrived[way], tops(1)[way], lanes)):
            messages[way][first : first + rows, lane * 128 : (lane + 1) * 128] = column.astype(low)
        if k == 2:
            gains = ins[9]
            messages[way][first + rows : first + rows + gains.shape[0], :lanes] = gains[...]


def round_five_kernel(ins, outs, _):
    at = places()
    sent, arrived = dict(zip(WAYS, ins[:3])), dict(zip(WAYS, ins[3:]))
    for k, out in enumerate(outs):
        way = ATTN_ORDERS[k][2]
        first = tops(0)[way]
        lanes = out.shape[1]
        rows = 128
        for value, index in ((sent[way], at[way]), (arrived[way], 1 - at[way])):
            out[span(index, rows), :] = value[first : first + rows, :lanes]
        if k == 2:
            tail = slice(first + rows, first + rows + out.shape[0] - 2 * rows)
            out[2 * rows :, :] = (
                sent[way][tail, :lanes].astype(wide) + arrived[way][tail, :lanes].astype(wide)
            ).astype(low)


def ffn_halves_kernel(ins, outs, _):
    at = places()
    sent, arrived = dict(zip(WAYS, ins[:3])), dict(zip(WAYS, ins[3:]))
    base = 0
    for k, rows in enumerate(FFN_ROWS):
        way = FFN_ORDERS[k][0]
        width = sent[way].shape[1]
        for value, index in ((sent[way], at[way]), (arrived[way], 1 - at[way])):
            start = pl.multiple_of(index * width, width)
            outs[0][base : base + rows, pl.ds(start, width)] = value[:rows, :]
        base += rows


def write_out(order, body, ins, outs, buffers, small=(), into=None, cost=0.3):
    ins, old = list(ins), list(into or [])
    needs = [order.last]
    count, many = len(ins), len(outs)
    skip = count + len(old) + len(needs)
    small = list(small) + [((8, 128), wide)]

    def run(*refs):
        targets = refs[skip : skip + many]
        others = refs[skip + many : skip + many + len(small)]
        scratch = refs[skip + many + len(small) :]
        held, arrived = scratch[: len(buffers)], scratch[len(buffers)]
        others[-1][...] = jnp.zeros_like(others[-1])
        copies = []
        for k, (value, target) in enumerate(body(places(), refs[:count], targets, others[:-1])):
            held[k][...] = value
            copies.append(pltpu.make_async_copy(held[k], target, arrived.at[k]))
            copies[-1].start()
        for copy in copies:
            copy.wait()

    size = sum(shape[0] * shape[1] * 4 for shape in buffers) + sum(
        value.size * value.dtype.itemsize for value in ins
    )
    result = pl.pallas_call(
        run,
        out_shape=[jax.ShapeDtypeStruct(shape, wide) for shape in outs]
        + [jax.ShapeDtypeStruct(shape, kind) for shape, kind in small],
        in_specs=[pl.BlockSpec(memory_space=pltpu.VMEM)] * count
        + [pl.BlockSpec(memory_space=pltpu.HBM)] * len(old)
        + [pl.BlockSpec(memory_space=pl.ANY)] * len(needs),
        out_specs=[pl.BlockSpec(memory_space=pltpu.HBM)] * many
        + [pl.BlockSpec(memory_space=pltpu.VMEM)] * len(small),
        scratch_shapes=[pltpu.VMEM(shape, wide) for shape in buffers]
        + [pltpu.SemaphoreType.DMA((len(buffers),))],
        input_output_aliases={count + k: k for k in range(len(old))},
        compiler_params=pltpu.CompilerParams(vmem_limit_bytes=size + (6 << 20)),
        cost_estimate=pl.CostEstimate(
            flops=int(cost * 1e9), bytes_accessed=0, transcendentals=0
        ),
        name=body.__name__,
    )(*ins, *old, *needs)
    order.last = result[-1]
    return list(result[:-1])


def write_ffn(own):
    def write_ffn_half(at, ins, targets, _):
        half = ins[0].shape[1]
        index = at["core"] if own else 1 - at["core"]
        rows = targets[0].shape[0]
        for k, target in enumerate(targets):
            yield ins[0][k * rows : (k + 1) * rows, :].astype(wide), target.at[:, span(index, half)]

    return write_ffn_half


def write_attn(own):
    def write_attn_half(at, ins, targets, small):
        one, two, three = ins[:3]
        features = three.shape[1]
        half = one.shape[0]
        here = span(at["core"] if own else 1 - at["core"], half)
        yield one[:, :features].astype(wide), targets[0].at[here, :]
        yield two[:, :features].astype(wide), targets[1].at[here, :]
        yield three[:half, :].astype(wide), targets[2].at[here, :]
        halves = (one[:, features:], two[:, features:])
        out = jnp.concatenate([value.astype(wide).T for value in halves], axis=0)
        yield out, targets[3].at[:, here]
        if not own:
            sums = ins[3][half:, :].astype(wide) + three[half:, :].astype(wide)
            for k, gain in enumerate(small):
                gain[:, :HD] = sums[2 * k : 2 * k + 1, :HD]
                gain[:, HD:] = sums[2 * k + 1 : 2 * k + 2, :HD]

    return write_attn_half


def on_device(
    tokens, gain_attn, w_query, w_key, w_value, w_out, gain_ffn, w_gate, w_up, w_down, cotangent
):
    rows, width = tokens.shape
    features = w_query.shape[1]
    units = w_gate.shape[1]
    share = rows // TP
    quarter = rows // 4
    order = Order()
    gain_attn = gain_attn.reshape(1, width)
    gain_ffn = gain_ffn.reshape(1, width)
    w_gate, w_up = w_gate.T, w_up.T
    blocks_out = [((share, width), low)] * 8
    whole = ((rows, width), low)
    small = ((rows, features), low)
    keep_and_send = [((share, width), wide), ((share, width), low)]

    normed_attn, own = order(
        normed_kernel,
        [tokens, gain_attn, w_key, w_value],
        [whole, ((rows, 2 * features), low)],
        temporary=6 << 20, cost=1.0)
    two, four = shifted(own, 2), shifted(own, 4)
    partner_own = by_seq(own, "core")
    (query,) = order(project_kernel, [normed_attn, w_query], [small])
    query_two, query_four = shifted(query, -2), shifted(query, -4)
    query_partner_own = by_seq(query, "core")
    across = by_seq(two, "core")
    partner_four = by_seq(four, "core")
    keys = [own, two, across, four, partner_own, partner_four]
    heads_out, logs, *blocks = order(
        attend_kernel,
        [query] + keys + [w_out],
        [small, ((rows, HD), wide)] + blocks_out,
        scratch=[whole],
        temporary=6 << 20, cost=2.5,
    )
    theirs = z_exchange(blocks[5:])
    mine = z_exchange(blocks[2:5])
    (send,) = order(
        sum_kernel, [blocks[1], theirs[1], theirs[2], theirs[0]], [((share, width), low)], needs=[query_two, query_four]
    )
    arrived = by_tp(send, 1)
    query_two, query_four = hold(order, [query_two, query_four])
    query_across = by_seq(query_two, "core")
    query_partner_four = by_seq(query_four, "core")
    hidden, normed_rows = order(
        norm_rows_kernel,
        [blocks[0]] + mine + [arrived, tokens, gain_ffn],
        keep_and_send,
        needs=[query_across, query_partner_own, query_partner_four],
    )
    gathered = gather_tp(normed_rows)

    normed_ffn, activated, grad_gate, grad_up, *blocks = order(
        ffn_kernel,
        gathered + [w_gate, w_up, w_down, cotangent],
        [whole] + [((rows, units), low)] * 3 + blocks_out,
        scratch=[whole],
        temporary=12 << 20, cost=5.0)
    theirs = z_exchange(blocks[5:])
    ffn_operands = [grad_gate, grad_up, activated, normed_ffn, cotangent]
    half = width // 2
    (sent,) = order(
        ffn_send_kernel([0, 1, 2]),
        ffn_operands,
        [((3 * units, half), low)],
        temporary=6 << 20, cost=2.5)
    core_arrived = by_seq(sent, "core")
    mine = z_exchange(hold(order, blocks[2:5]))
    parts = order(
        ffn_keep_kernel([0, 1, 2]),
        ffn_operands + [core_arrived],
        [((rows_k, half // 2), low) for rows_k in FFN_ROWS for _ in range(2)],
        temporary=6 << 20, cost=2.5)
    ffn_keeps = list(parts[0::2])
    last_part = parts[5]
    ffn_flights = [by_seq(part, names[0]) for part, names in zip(parts[1:4:2], FFN_ORDERS)]

    def ffn_split(steps, needs=()):
        parts = run_ops(
            order,
            [
                split_op(ffn_keeps[k], ffn_flights[k], FFN_ORDERS[k][step], 1)
                for k, step in steps
            ],
            needs,
        )
        for (k, step), (keep, send) in zip(steps, parts):
            ffn_keeps[k] = keep
            ffn_flights[k] = by_seq(send, FFN_ORDERS[k][step])

    (send,) = order(sum_kernel, [blocks[1]] + theirs, [((share, width), low)], cost=3.0)
    arrived = by_tp(send, 1)
    grad_hidden, grad_low, gain_ffn_part = order(
        grad_rows_kernel,
        [blocks[0]] + mine + [arrived, hidden, cotangent, gain_ffn],
        keep_and_send + [((1, width), wide)], cost=1.5)
    (pair,) = order(
        pair_kernel, [grad_low, by_tp(grad_low, 1)], [((quarter, width), low)], cost=1.5
    )
    gathered = [pair] + z_spread(pair)
    ffn_flights += [by_seq(value, FFN_ORDERS[2][0]) for value in hold(order, [last_part])]
    ffn_split([(0, 1), (1, 1)])
    grad_hidden_low, grad_heads = order(
        heads_kernel,
        gathered + [w_out, logs, heads_out],
        [whole, ((rows, features + HD), low)], cost=2.0)
    grad_two, grad_four = shifted(grad_heads, -2), shifted(grad_heads, -4)
    (grad_query,) = order(
        grad_query_kernel,
        [query, heads_out, logs, grad_heads] + keys,
        [small],
        temporary=6 << 20, cost=2.0)
    (ffn_partial,) = order(project_kernel, [activated, w_down], [whole], temporary=6 << 20, cost=1.0)
    grad_two, grad_four, grad_late = hold(order, [grad_two, grad_four, grad_heads])
    grad_partner_own = by_seq(grad_late, "core")
    grad_across = by_seq(grad_two, "core")
    grad_partner_four = by_seq(grad_four, "core")
    cut = width
    grad_key, grad_value = order(
        grad_key_kernel,
        [own, query, query_two, query_across, query_four, query_partner_own, query_partner_four]
        + [grad_late, grad_two, grad_across, grad_four, grad_partner_own, grad_partner_four],
        [small, small],
        needs=ffn_flights[2:],
        temporary=8 << 20, cost=0.3)
    ffn_split([(2, 1)])
    keep_one, keep_two, send_one, send_two = order(
        back_kernel,
        [grad_query, grad_key, grad_value, w_query, w_key, w_value, tokens, gain_ffn_part, ffn_partial],
        [((2 * quarter, cut), low), ((2 * quarter, cut + HD), low)] * 2,
        scratch=[((rows, width + HD), low)],
        temporary=12 << 20, cost=0.3)
    one_arrived, two_arrived = by_tp(send_one, 2), by_tp(send_two, 6)

    operands = [normed_attn, grad_hidden_low, grad_query, grad_key, grad_value, heads_out]
    (sent,) = order(
        attn_half_kernel(False), operands, [((width // 2, 4 * features), low)], ffn_flights[:2], temporary=4 << 20, cost=2.5)
    core_arrived = by_seq(sent, "core")
    (own_half,) = order(
        attn_half_kernel(True), operands, [((width // 2, 4 * features), wide)], temporary=4 << 20)
    widths = (features + features // 2, features + features // 2, features)

    def messages_of(width_out, size, ffn_step, attn_step_out):
        by_way = {orders[attn_step_out]: part for orders, part in zip(ATTN_ORDERS, widths)}
        top = tops(ffn_step)
        return [
            ((top[way] + packed_rows(size, by_way[way], width_out), width_out), low)
            for way in WAYS
        ]

    def kept(size):
        return [((size, part), low) for part in widths]

    def fly(messages):
        return [by_seq(message, way) for message, way in zip(messages, WAYS)]

    *parts, keep_x, keep_y, keep_z, ffn_x, ffn_y, ffn_z = order(
        round_one_kernel,
        ffn_keeps + ffn_flights + [own_half, core_arrived],
        messages_of(128, 512, 2, 0) + kept(512) + [((rows_k, 128), low) for rows_k in FFN_ROWS],
        temporary=4 << 20, cost=4.0,
    )
    flights = fly(parts)

    stay_one, go_one, stay_two, go_two = order(
        sum_middle_kernel,
        [keep_one, one_arrived, keep_two, two_arrived],
        [
            ((quarter, cut), wide),
            ((quarter, cut), low),
            ((quarter, cut + HD), wide),
            ((quarter, cut + HD), low),
        ], cost=3.0)
    one_arrived, two_arrived = by_tp(go_one, 6), by_tp(go_two, 2)

    *parts, keep_x, keep_y, keep_z = order(
        round_two_kernel,
        flights + [ffn_x, ffn_y, ffn_z, keep_x, keep_y, keep_z],
        messages_of(128, 256, 2, 1) + kept(256),
    )
    flights = fly(parts)
    keep, send = order(
        sum_last_kernel,
        [stay_one, one_arrived, stay_two, two_arrived],
        [((share, 2 * width + HD), wide), ((share, 2 * width + HD), low)],
    )
    arrived = by_tp(send, 1)
    *parts, keep_x, keep_y, keep_z = order(
        round_three_kernel,
        parts + flights + [keep_x, keep_y, keep_z],
        messages_of(256, 128, 1, 2) + kept(128),
    )
    flights = fly(parts)
    last_rows, gains = order(
        last_rows_kernel,
        [keep, arrived, grad_hidden, hidden, tokens, gain_attn],
        [((share, 2 * width), low), ((16, features), low)], cost=6.0)
    arrived = by_tp(last_rows, 1)
    below = {ATTN_ORDERS[0][2]: 128, ATTN_ORDERS[1][2]: 128, ATTN_ORDERS[2][2]: 128 + 16}
    parts = order(
        round_four_kernel,
        parts + flights + [keep_x, keep_y, keep_z, gains],
        [((tops(0)[way] + below[way], 512), low) for way in WAYS], cost=8.0)
    flights = fly(parts)
    first, second = order(last_pair_kernel, [last_rows, arrived], [((quarter, width), low)] * 2, cost=0.3)
    first_arrived, second_arrived = by_tp(first, 2), by_tp(second, 6)
    firsts, seconds = order(
        stack_kernel,
        [first, first_arrived, second, second_arrived],
        [((2 * quarter, width), low)] * 2, cost=2.0)
    first_arrived, second_arrived = by_tp(firsts, 6), by_tp(seconds, 2)
    one, two, three = order(
        round_five_kernel,
        list(parts) + flights,
        [((256, widths[0]), low), ((256, widths[1]), low), ((256 + 16, widths[2]), low)],
    )
    ffn_last = list(parts) + flights
    flights = [by_seq(value, orders[1]) for value, orders in zip((one, two, three), ATTN_ORDERS)]
    (ffn_half,) = order(ffn_halves_kernel, ffn_last, [((3 * units, width // 2), low)])

    def attn_join(step, needs=()):
        nonlocal one, two, three, flights
        names = [orders[step] for orders in ATTN_ORDERS]
        (one,), (two,), (three,) = run_ops(
            order,
            [
                join_op(one, flights[0], names[0], 0),
                join_op(two, flights[1], names[1], 0),
                join_tail_op(three, flights[2], names[2], gains.shape[0]),
            ],
            needs,
        )
        names = [orders[step - 1] if step > 0 else "core" for orders in ATTN_ORDERS]
        flights = [by_seq(value, name) for value, name in zip((one, two, three), names)]

    ffn_shapes = [(units, width)] * 3
    ffn_buffers = [(units, width // 2)] * 3
    grads_ffn = write_out(order, write_ffn(True), [ffn_half], ffn_shapes, ffn_buffers)
    attn_join(1, [first_arrived, second_arrived])
    (ffn_half,) = hold(order, [ffn_half], True)
    ffn_arrived = by_seq(ffn_half, "core")
    grads_ffn = write_out(
        order, write_ffn(False), [ffn_arrived], ffn_shapes, ffn_buffers, into=grads_ffn, cost=8.0
    )
    grad_tokens, block_out = order(
        token_outputs_kernel,
        [firsts, first_arrived, seconds, second_arrived],
        [((rows, width), wide), whole],
    )
    attn_join(0)
    attn_shapes = [(width, features)] * 3 + [(features, width)]
    attn_buffers = [(width // 2, features)] * 3 + [(features, width // 2)]
    grads_attn = write_out(
        order, write_attn(True), [one, two, three], attn_shapes, attn_buffers
    )
    grad_w_query, grad_w_key, grad_w_value, grad_w_out, grad_gain_attn, grad_gain_ffn = write_out(
        order,
        write_attn(False),
        flights + [three],
        attn_shapes,
        attn_buffers,
        small=[((1, features), wide)] * 2,
        into=grads_attn,
    )
    return (
        block_out,
        grad_tokens,
        grad_gain_attn.reshape(-1),
        grad_w_query,
        grad_w_key,
        grad_w_value,
        grad_w_out,
        grad_gain_ffn.reshape(-1),
        grads_ffn[0].T,
        grads_ffn[1].T,
        grads_ffn[2],
    )


def solution(mesh):
    fine = Mesh(mesh.devices.reshape(2, 4, 2, TP), SEQ_AXES + ("tp",))
    return jax.shard_map(
        on_device,
        mesh=fine,
        in_specs=(
            P(SEQ_AXES, None),
            P(),
            P(None, "tp"),
            P(None, "tp"),
            P(None, "tp"),
            P("tp", None),
            P(),
            P(None, "tp"),
            P(None, "tp"),
            P("tp", None),
            P(SEQ_AXES, None),
        ),
        out_specs=(
            P(SEQ_AXES, None),
            P(SEQ_AXES, None),
            P("tp"),
            P(None, "tp"),
            P(None, "tp"),
            P(None, "tp"),
            P("tp", None),
            P("tp"),
            P(None, "tp"),
            P(None, "tp"),
            P("tp", None),
        ),
        check_vma=False,
    )
```
